32 devices in a mesh: dp: 8 (over z, x), head: 4 (over y, core).
Axes of the slice: x: 2, y: 2, z: 4, core: 2. Of those that a mesh axis runs over, the one named last changes fastest.
Arguments:
- layer_input: bfloat16 [32768, 768], P(('dp', 'head')), may hold values from -6 to 6
- out_grad: bfloat16 [32768, 768], P(('dp', 'head'))
- matrices: float32 [3, 768, 3072], P(None, None, ('dp', 'head'))
- mat_first: float32 [3, 768, 3072], P(None, None, ('dp', 'head'))
- mat_second: float32 [3, 768, 3072], P(None, None, ('dp', 'head')), as said below
- mat_ema: float32 [3, 768, 3072], P(None, None, ('dp', 'head'))
- gains: float32 [2, 768], replicated, may hold values from 0.5 to 1.5
- gain_first: float32 [2, 768], replicated
- gain_second: float32 [2, 768], replicated, as said below
- rel_bias: float32 [32, 12], replicated, may hold values from -3 to 3
- bias_first: float32 [32, 12], replicated
- bias_second: float32 [32, 12], replicated, as said below
- bucket_len: int32 [64], P('dp'), may hold values from 128 to 512, as said below
- item_count: int32 [64], P('dp'), may hold values from 1 to 4, as said below
- bucket_table: int32 [1023], replicated, may hold values from 0 to 31, as said below
Outputs:
- layer_output: bfloat16 [32768, 768], P(('dp', 'head'))
- input_grad: float32 [32768, 768], P(('dp', 'head'))
- mat_grad: float32 [3, 768, 3072], P(None, None, ('dp', 'head'))
- mat_new: float32 [3, 768, 3072], P(None, None, ('dp', 'head'))
- mat_first_new: float32 [3, 768, 3072], P(None, None, ('dp', 'head'))
- mat_second_new: float32 [3, 768, 3072], P(None, None, ('dp', 'head'))
- mat_ema_new: float32 [3, 768, 3072], P(None, None, ('dp', 'head'))
- gain_grad: float32 [2, 768], replicated
- gain_new: float32 [2, 768], replicated
- gain_first_new: float32 [2, 768], replicated
- gain_second_new: float32 [2, 768], replicated
- bias_grad: float32 [32, 12], replicated
- bias_new: float32 [32, 12], replicated
- bias_first_new: float32 [32, 12], replicated
- bias_second_new: float32 [32, 12], replicated
The draws below stay inside these ranges and needn't reach their ends.
Inputs may be any that keep to these rules, and one draw needn't show every extreme that they name: `bucket_len`: every packed row holds items of one length, 128, 256 or 512; some row has length 128 and some row 512. `item_count`: items fill a packed row from its start, at most 512 divided by the row's length of them; the other slots are padding; some row holds 4. `bucket_table`: entry r + 511 is the bucket of relative position r, query position minus key position. `mat_second`: positive. `gain_second`: positive. `bias_second`: positive.
All inputs are finite; a program needn't handle non-finite values.
Results may differ from the reference program's by a relative error of at most 0.014.
The reference program's roundings to bfloat16 on the way count: a program that leaves them out, or rounds other values in their place, can miss the bound.
Values may be sent and summed in bfloat16 or wider, within the bound.
No kernel may reach another device: no remote copies, remote signals or barrier semaphores. Data moves between devices by JAX's collectives and lax.ppermute only.
A program may use at most 256 MiB of HBM per device.

```python
import math
import jax
import jax.numpy as jnp
from jax import lax

D = 768
FF = 3072
HEADS = 12
HD = 64
BUCKETS = 32
ROW = 512
STEP = 10
TOKENS = 32768
ROWS_ALL = 64


def column_scales():
    columns = jnp.arange(FF, dtype=jnp.int32)
    quarter = columns // D
    query_scale = 2.0 / math.sqrt(HD)
    first = jnp.where(quarter == 0, query_scale, jnp.where(quarter == 3, 1.5, 1.0)).astype(jnp.float32) / math.sqrt(D)
    second = jnp.full((FF,), 1.0 / math.sqrt(D), jnp.float32)
    third = jnp.full((FF,), math.sqrt(2.0 / FF), jnp.float32)
    return jnp.stack([first, second, third])[:, None, :]


def matrix_grad_size():
    columns = jnp.arange(FF, dtype=jnp.int32)
    quarter = columns // D
    first = jnp.where(quarter == 0, 8.0, jnp.where(quarter == 1, 3.0, jnp.where(quarter == 2, 1.6, 1.0))).astype(jnp.float32)
    second = jnp.full((FF,), 0.5, jnp.float32)
    third = jnp.full((FF,), 0.75, jnp.float32)
    return jnp.stack([first, second, third])[:, None, :] * math.sqrt(TOKENS)


def gain_grad_size():
    return jnp.array([4.5, 1.0], jnp.float32)[:, None] * math.sqrt(TOKENS)


def bias_grad_size():
    return math.sqrt(TOKENS)


def first_moment(key, shape, size):
    return 0.11 * size * jax.random.normal(key, shape, jnp.float32)


def second_moment(key, shape, size):
    factor = jnp.exp(jax.random.uniform(key, shape, jnp.float32, 0.0, math.log(4.0)))
    return 0.001 * size * size * factor


def draw_matrices(key, part):
    inner = jax.random.fold_in(key, 21)
    noise = jax.random.normal(inner, (3, D, FF), jnp.float32)
    return noise * column_scales()


def draw_mat_ema(key, part):
    inner = jax.random.fold_in(key, 22)
    noise = jax.random.normal(inner, (3, D, FF), jnp.float32)
    return noise * column_scales()


def draw_mat_first(key, part):
    return first_moment(jax.random.fold_in(key, 61), (3, D, FF), matrix_grad_size())


def draw_mat_second(key, part):
    return second_moment(jax.random.fold_in(key, 62), (3, D, FF), matrix_grad_size())


def draw_gain_first(key, part):
    return first_moment(jax.random.fold_in(key, 63), (2, D), gain_grad_size())


def draw_gain_second(key, part):
    return second_moment(jax.random.fold_in(key, 64), (2, D), gain_grad_size())


def draw_bias_first(key, part):
    return first_moment(jax.random.fold_in(key, 65), (BUCKETS, HEADS), bias_grad_size())


def draw_bias_second(key, part):
    return second_moment(jax.random.fold_in(key, 66), (BUCKETS, HEADS), bias_grad_size())


def draw_out_grad(key, part):
    inner = jax.random.fold_in(key, 31)
    ramp = 0.5 + jnp.arange(TOKENS, dtype=jnp.float32)[:, None] / TOKENS
    return (jax.random.normal(inner, (TOKENS, D), jnp.float32) * ramp).astype(jnp.bfloat16)


def row_plan(key):
    inner = jax.random.fold_in(key, 41)
    first_key, second_key, third_key, fourth_key = jax.random.split(inner, 4)
    level = jax.random.randint(first_key, (ROWS_ALL,), 0, 3)
    length = jnp.where(level == 0, ROW // 4, jnp.where(level == 1, ROW // 2, ROW)).astype(jnp.int32)
    items = jax.random.randint(second_key, (ROWS_ALL,), 1, ROW // length + 1)
    index = jnp.arange(ROWS_ALL, dtype=jnp.int32)
    short_row = jax.random.randint(third_key, (), 0, ROWS_ALL // 2)
    long_row = jax.random.randint(fourth_key, (), ROWS_ALL // 2, ROWS_ALL)
    length = jnp.where(index == short_row, ROW // 4, length)
    items = jnp.where(index == short_row, 4, items)
    length = jnp.where(index == long_row, ROW, length)
    items = jnp.where(index == long_row, 1, items)
    return (length.astype(jnp.int32), items.astype(jnp.int32))


def draw_bucket_len(key, part):
    return row_plan(key)[0]


def draw_item_count(key, part):
    return row_plan(key)[1]


def draw_bucket_table(key, part):
    inner = jax.random.fold_in(key, 51)
    near = BUCKETS // 4
    half = BUCKETS // 2
    upper = max((ROW - near) // near, 2)
    gaps = jax.random.randint(inner, (near,), 1, upper)
    edges = near + jnp.cumsum(gaps)[:near - 1]
    offset = jnp.arange(2 * ROW - 1, dtype=jnp.int32) - (ROW - 1)

    def bucket_of(distance):
        far = near + jnp.sum((distance[:, None] >= edges[None, :]).astype(jnp.int32), axis=1)
        return jnp.where(distance < near, distance, far)
    negative = bucket_of(jnp.maximum(-offset, 0))
    positive = half + bucket_of(jnp.maximum(offset - 1, 0))
    return jnp.where(offset > 0, positive, negative).astype(jnp.int32)


def levels(own_key, shape, shards, smallest, high):
    def one(axis_at, shards_of):
        draws = jax.random.uniform(jax.random.fold_in(jax.random.fold_in(own_key, 6), axis_at), (shards_of,), jnp.float32, smallest / len(shards), high / len(shards))
        return jnp.repeat(jnp.exp(draws), shape[axis_at] // shards_of).reshape((-1,) + (1,) * (len(shape) - axis_at - 1))

    level = one(*shards[0])
    for cut in shards[1:]:
        level = level * one(*cut)
    return level


def scatter_about(rng, dims, width, limit, cuts=(), kind=jnp.bfloat16):
    level = levels(rng, dims, cuts, -0.22, 0.18) if cuts else 1.0
    values = jax.random.normal(rng, dims, jnp.float32) * width * level
    return jnp.minimum(jnp.maximum(values, -limit), limit).astype(kind)


def setup_inputs(seed: int = 0) -> dict:
    keys = jax.random.split(jax.random.key(seed), 16)
    layer_input = scatter_about(keys[0], (TOKENS, D), 1.0, 6.0, ((0, 32),))
    out_grad = draw_out_grad(jax.random.fold_in(keys[15], 71), 0)
    matrices = draw_matrices(jax.random.fold_in(keys[15], 71), 0)
    mat_first = draw_mat_first(jax.random.fold_in(keys[15], 71), 0)
    mat_second = draw_mat_second(jax.random.fold_in(keys[15], 71), 0)
    mat_ema = draw_mat_ema(jax.random.fold_in(keys[15], 71), 0)
    gains = jnp.clip(1.0 + 0.1 * jax.random.normal(keys[6], (2, D), jnp.float32), 0.5, 1.5)
    gain_first = draw_gain_first(jax.random.fold_in(keys[15], 71), 0)
    gain_second = draw_gain_second(jax.random.fold_in(keys[15], 71), 0)
    rel_bias = scatter_about(keys[9], (BUCKETS, HEADS), 0.5, 3.0, (), jnp.float32)
    bias_first = draw_bias_first(jax.random.fold_in(keys[15], 71), 0)
    bias_second = draw_bias_second(jax.random.fold_in(keys[15], 71), 0)
    bucket_len = draw_bucket_len(jax.random.fold_in(keys[15], 71), 0)
    item_count = draw_item_count(jax.random.fold_in(keys[15], 71), 0)
    bucket_table = draw_bucket_table(jax.random.fold_in(keys[15], 71), 0)
    return dict(layer_input=layer_input, out_grad=out_grad, matrices=matrices, mat_first=mat_first, mat_second=mat_second, mat_ema=mat_ema, gains=gains, gain_first=gain_first, gain_second=gain_second, rel_bias=rel_bias, bias_first=bias_first, bias_second=bias_second, bucket_len=bucket_len, item_count=item_count, bucket_table=bucket_table)


EPS = 1e-06
NEG = -1e+30
RATE = 0.05
RATE_SMALL = 0.5
BETA_ONE = 0.9
BETA_TWO = 0.999
ADAM_EPS = 1e-08
DECAY = 0.1
EMA_KEEP = 0.75
HIGH = lax.Precision.HIGHEST

@jax.custom_vjp
def low(v):
    return lax.optimization_barrier(v.astype(jnp.bfloat16)).astype(jnp.float32)

@jax.custom_vjp
def low_back(v):
    return v

def low_keep(v):
    return (low(v), None)

def low_pass(kept, grad):
    return (grad,)

def back_keep(v):
    return (v, None)

def back_low(kept, grad):
    return (low(grad),)
low.defvjp(low_keep, low_pass)
low_back.defvjp(back_keep, back_low)

def rms_scale(value, gain):
    return value * lax.rsqrt(lax.optimization_barrier(jnp.mean(value * value, axis=-1, keepdims=True)) + EPS) * gain

def smooth_gate(value):
    return 0.5 * value * (1.0 + jnp.tanh(0.7978845608 * (value + 0.044715 * value * value * value)))

def bucket_onehot(bucket_table):
    places = jnp.arange(ROW, dtype=jnp.int32)
    offsets = (places[:, None] - places[None, :] + (ROW - 1)).reshape(-1).astype(jnp.int32)
    chosen = jnp.take(bucket_table, offsets)
    return (chosen[None, :] == jnp.arange(BUCKETS, dtype=jnp.int32)[:, None]).astype(jnp.float32)

def row_masks(lengths, counts):
    places = jnp.arange(ROW, dtype=jnp.int32)
    live_rows = places[None, :] < (lengths * counts)[:, None]
    items = places[None, :] // lengths[:, None]
    allowed = (items[:, :, None] == items[:, None, :]) & live_rows[:, None, :]
    return (allowed, live_rows.astype(jnp.float32))

def forward(weights, gain_pair, table_bias, inputs, onehot, allowed, live_rows):
    normed = low(rms_scale(inputs, gain_pair[0]))
    attn_weight = weights[0]
    packed = low(low_back(jnp.dot(normed, attn_weight[:, :3 * D], precision=HIGH)))
    packed = packed.reshape(-1, ROW, 3, HEADS, HD)
    queries = packed[:, :, 0]
    key_rows = packed[:, :, 1]
    values = packed[:, :, 2]
    bias_full = jnp.dot(table_bias.T, onehot, precision=HIGH).reshape(HEADS, ROW, ROW)
    scores = jnp.einsum('gihd,gjhd->ghij', queries, key_rows, precision=HIGH) + bias_full[None]
    scores = low_back(scores)
    scores = jnp.where(allowed[:, None], scores, NEG)
    attention = jax.nn.softmax(scores, axis=-1) * live_rows[:, None, :, None]
    mixed_heads = jnp.einsum('ghij,gjhd->gihd', low(attention), values, precision=HIGH).reshape(-1, D)
    mixed_heads = low(low_back(mixed_heads))
    branch = low_back(jnp.dot(mixed_heads, attn_weight[:, 3 * D:], precision=HIGH))
    middle = inputs + branch
    second = low(rms_scale(middle, gain_pair[1]))
    pre_act = low_back(jnp.dot(second, weights[1], precision=HIGH))
    hidden = low(low_back(smooth_gate(pre_act)))
    return middle + low_back(jnp.dot(hidden, weights[2].T, precision=HIGH))

def adam_update(param, grad, first, second, rate):
    first_new = BETA_ONE * first + (1.0 - BETA_ONE) * grad
    second_new = BETA_TWO * second + (1.0 - BETA_TWO) * grad * grad
    first_hat = first_new / (1.0 - BETA_ONE ** STEP)
    second_hat = second_new / (1.0 - BETA_TWO ** STEP)
    param_new = param - rate * (first_hat / (jnp.sqrt(second_hat) + ADAM_EPS) + DECAY * param)
    return (param_new, first_new, second_new)

def reference(layer_input, out_grad, matrices, mat_first, mat_second, mat_ema, gains, gain_first, gain_second, rel_bias, bias_first, bias_second, bucket_len, item_count, bucket_table):
    weights = matrices.astype(jnp.bfloat16).astype(jnp.float32)
    onehot = bucket_onehot(bucket_table)
    group = math.gcd(ROWS_ALL, 8)
    blocks = ROWS_ALL // group
    inputs = layer_input.astype(jnp.float32).reshape(blocks, group * ROW, D)
    cotangent = out_grad.astype(jnp.float32).reshape(blocks, group * ROW, D)
    lengths = bucket_len.reshape(blocks, group)
    counts = item_count.reshape(blocks, group)

    def block_step(totals, pieces):
        block_in, block_grad, block_len, block_count = pieces
        allowed, live_rows = row_masks(block_len, block_count)

        def local(weight_in, gain_in, bias_in, value_in):
            return forward(weight_in, gain_in, bias_in, value_in, onehot, allowed, live_rows)
        result, pullback = jax.vjp(local, weights, gains, rel_bias, block_in)
        grad_weight, grad_gain, grad_bias, grad_input = pullback(block_grad)
        totals = (totals[0] + grad_weight, totals[1] + grad_gain, totals[2] + grad_bias)
        return (totals, (result.astype(jnp.bfloat16), grad_input))
    start = (jnp.zeros_like(weights), jnp.zeros_like(gains), jnp.zeros_like(rel_bias))
    totals, (outputs, input_grads) = lax.scan(block_step, start, (inputs, cotangent, lengths, counts))
    mat_grad, gain_grad, bias_grad = totals
    mat_new, mat_first_new, mat_second_new = adam_update(matrices, mat_grad, mat_first, mat_second, RATE)
    mat_ema_new = EMA_KEEP * mat_ema + (1.0 - EMA_KEEP) * mat_new
    gain_new, gain_first_new, gain_second_new = adam_update(gains, gain_grad, gain_first, gain_second, RATE_SMALL)
    bias_new, bias_first_new, bias_second_new = adam_update(rel_bias, bias_grad, bias_first, bias_second, RATE_SMALL)
    return (outputs.reshape(TOKENS, D), input_grads.reshape(TOKENS, D), mat_grad, mat_new, mat_first_new, mat_second_new, mat_ema_new, gain_grad, gain_new, gain_first_new, gain_second_new, bias_grad, bias_new, bias_first_new, bias_second_new)
```

```python
import functools

import jax
import jax.numpy as jnp
from jax import lax
from jax.experimental import pallas as pl
from jax.experimental.pallas import tpu as pltpu
from jax.sharding import Mesh, PartitionSpec as P

D = 768
FF = 3072
HEADS = 12
HD = 64
BUCKETS = 32
ROW = 512
STEP = 10
PAIRS = HEADS // 2
WIDE = 2 * HD
SUB = 128
SPAN = 1024
TOEP = 896

EPS = 1e-06
RATE = 0.05
RATE_SMALL = 0.5
BETA_ONE = 0.9
BETA_TWO = 0.999
ADAM_EPS = 1e-08
DECAY = 0.1
EMA_KEEP = 0.75

F32 = jnp.float32
BF16 = jnp.bfloat16
VMEM_LIMIT = 56 * 1024 * 1024
TILE = 256

NN = (((1,), (0,)), ((), ()))
NT = (((1,), (1,)), ((), ()))
TN = (((0,), (0,)), ((), ()))


def dot(left, right, dims):
    return lax.dot_general(left, right, dims, preferred_element_type=F32)


def params(**more):
    return pltpu.CompilerParams(vmem_limit_bytes=VMEM_LIMIT, **more)


def cost(flops, moved, special=0):
    return pl.CostEstimate(flops=int(flops), bytes_accessed=int(moved), transcendentals=int(special))


def whole(shape):
    return pl.BlockSpec(shape, lambda *_: (0,) * len(shape))


def tiles(rows, columns):
    return pl.BlockSpec((rows, columns), lambda i: (i, 0))


def qkv_kernel(x_ref, gain_ref, weight_ref, normed_ref, packed_ref):
    x = x_ref[...].astype(F32)
    scale = lax.rsqrt(jnp.mean(x * x, axis=-1, keepdims=True) + EPS)
    normed = (x * scale * gain_ref[...]).astype(BF16)
    normed_ref[...] = normed
    for part in range(3):
        cols = slice(part * D, (part + 1) * D)
        packed_ref[:, cols] = dot(normed, weight_ref[cols, :], NT).astype(BF16)


def qkv_call(x, gain, weight):
    tokens = x.shape[0]
    return pl.pallas_call(
        qkv_kernel,
        grid=(tokens // TILE,),
        in_specs=[tiles(TILE, D), whole((1, D)), whole((3 * D, D))],
        out_specs=[tiles(TILE, D), tiles(TILE, 3 * D)],
        out_shape=[
            jax.ShapeDtypeStruct((tokens, D), BF16),
            jax.ShapeDtypeStruct((tokens, 3 * D), BF16),
        ],
        compiler_params=params(),
        cost_estimate=cost(2 * tokens * D * 3 * D, 16e6),
        name="norm_qkv",
    )(x, gain, weight)


def fill_toeplitz(table_ref, toep):
    for h in range(2):
        line = jnp.broadcast_to(table_ref[0, h : h + 1, :], (SUB, SPAN))
        rolled = pltpu.roll(line, SPAN - (SUB - 1), 1, stride=1, stride_axis=0)
        toep[h] = rolled[:, :TOEP]


def head_masks():
    lane = lax.broadcasted_iota(jnp.int32, (1, WIDE), 1)
    return [(lane < HD).astype(BF16), (lane >= HD).astype(BF16)]


def bias_block(toep, h, first, rows, span):
    parts = []
    for t in range(rows // SUB):
        left = ROW - SUB - first - t * SUB
        parts.append(toep[h, :, left : left + span])
    return parts[0] if len(parts) == 1 else jnp.concatenate(parts, axis=0)


def for_items(length, count, body):
    @pl.when(length == ROW)
    def _():
        for first in range(0, ROW, 2 * SUB):
            body(0, first, 2 * SUB, ROW)

    @pl.when(length == ROW // 2)
    def _():
        @pl.loop(0, count)
        def _(item):
            body(item * (ROW // 2), 0, ROW // 2, ROW // 2)

    @pl.when(length == ROW // 4)
    def _():
        @pl.loop(0, count)
        def _(item):
            body(item * (ROW // 4), 0, ROW // 4, ROW // 4)


def aligned(start):
    return start if isinstance(start, int) else pl.multiple_of(start, SUB)


def attend_kernel(len_ref, count_ref, q_ref, k_ref, v_ref, table_ref, o_ref, lse_ref, toep):
    row = pl.program_id(1)

    @pl.when(row == 0)
    def _():
        fill_toeplitz(table_ref, toep)

    length = len_ref[row]
    count = count_ref[row]
    masks = head_masks()

    @pl.when(length * count < ROW)
    def _():
        o_ref[...] = jnp.zeros_like(o_ref)
        lse_ref[...] = jnp.zeros_like(lse_ref)

    def body(start, first, rows, span):
        keys_at = pl.ds(aligned(start), span)
        rows_at = pl.ds(aligned(start + first), rows)
        q = q_ref[rows_at, :]
        k = k_ref[keys_at, :]
        v = v_ref[keys_at, :]
        mixed = None
        stats = []
        for h in range(2):
            s = dot(q, k * masks[h], NT) + bias_block(toep, h, first, rows, span)
            top = jnp.max(s, axis=-1, keepdims=True)
            e = jnp.exp(s - top)
            total = jnp.sum(e, axis=-1, keepdims=True)
            p = (e * (1.0 / total)).astype(BF16)
            part = dot(p, v * masks[h], NN)
            mixed = part if mixed is None else mixed + part
            stats.append(jnp.broadcast_to(top + jnp.log(total), (rows, HD)))
        o_ref[rows_at, :] = mixed.astype(BF16)
        lse_ref[rows_at, :] = jnp.concatenate(stats, axis=1)

    for_items(length, count, body)


def pair_blocks(offset):
    return pl.BlockSpec((ROW, WIDE), lambda p, r, *_: (r, offset + p))


def attend_call(lengths, counts, packed, table):
    tokens = packed.shape[0]
    rows = tokens // ROW
    return pl.pallas_call(
        attend_kernel,
        grid_spec=pltpu.PrefetchScalarGridSpec(
            num_scalar_prefetch=2,
            grid=(PAIRS, rows),
            in_specs=[
                pair_blocks(0),
                pair_blocks(PAIRS),
                pair_blocks(2 * PAIRS),
                pl.BlockSpec((1, 2, SPAN), lambda p, r, *_: (p, 0, 0)),
            ],
            out_specs=[pair_blocks(0), pair_blocks(0)],
            scratch_shapes=[pltpu.VMEM((2, SUB, TOEP), F32)],
        ),
        out_shape=[
            jax.ShapeDtypeStruct((tokens, D), BF16),
            jax.ShapeDtypeStruct((tokens, D), F32),
        ],
        compiler_params=params(),
        cost_estimate=cost(12e9, 10e6, 7e6),
        name="attend",
    )(lengths, counts, packed, packed, packed, table)


def fold_diagonals(grid):
    height = SUB
    total = jnp.concatenate([grid, jnp.zeros((SUB, SPAN - TOEP), F32)], axis=1)
    while height > 8:
        height //= 2
        total = pltpu.roll(total[:height], height, 1) + total[height:]
    line = total[7:8]
    for r in range(7):
        line = line + pltpu.roll(total, 7 - r, 1)[r : r + 1]
    return line


def attend_back_kernel(
    len_ref, count_ref, q_ref, k_ref, v_ref, do_ref, lse_ref, table_ref,
    dq_ref, dk_ref, dv_ref, dbias_ref, toep, diag, dk_acc, dv_acc,
):
    row = pl.program_id(1)

    @pl.when(row == 0)
    def _():
        fill_toeplitz(table_ref, toep)
        diag[...] = jnp.zeros_like(diag)

    length = len_ref[row]
    count = count_ref[row]
    masks = head_masks()

    @pl.when(length * count < ROW)
    def _():
        dq_ref[...] = jnp.zeros_like(dq_ref)
        dk_ref[...] = jnp.zeros_like(dk_ref)
        dv_ref[...] = jnp.zeros_like(dv_ref)

    def body(start, first, rows, span):
        keys_at = pl.ds(aligned(start), span)
        rows_at = pl.ds(aligned(start + first), rows)
        q = q_ref[rows_at, :]
        do = do_ref[rows_at, :]
        k = k_ref[keys_at, :]
        v = v_ref[keys_at, :]
        dq = dk = dv = None
        for h in range(2):
            kh = k * masks[h]
            lse = lse_ref[rows_at, h * HD : h * HD + 1]
            s = dot(q, kh, NT) + bias_block(toep, h, first, rows, span)
            p = jnp.exp(s - lse)
            dp = dot(do, v * masks[h], NT)
            t = p * dp
            ds = t - p * jnp.sum(t, axis=-1, keepdims=True)
            for sub in range(rows // SUB):
                left = ROW - SUB - first - sub * SUB
                diag[h, :, left : left + span] += ds[sub * SUB : (sub + 1) * SUB]
            low = ds.astype(BF16)
            parts = (
                dot(low, kh, NN),
                dot(low, q * masks[h], TN),
                dot(p.astype(BF16), do * masks[h], TN),
            )
            if dq is None:
                dq, dk, dv = parts
            else:
                dq, dk, dv = dq + parts[0], dk + parts[1], dv + parts[2]
        dq_ref[rows_at, :] = dq.astype(BF16)
        if rows == span:
            dk_ref[keys_at, :] = dk.astype(BF16)
            dv_ref[keys_at, :] = dv.astype(BF16)
        elif first == 0:
            dk_acc[...] = dk
            dv_acc[...] = dv
        else:
            dk_ref[...] = (dk_acc[...] + dk).astype(BF16)
            dv_ref[...] = (dv_acc[...] + dv).astype(BF16)

    for_items(length, count, body)

    @pl.when(row == pl.num_programs(1) - 1)
    def _():
        for h in range(2):
            dbias_ref[0, h : h + 1, :] = fold_diagonals(diag[h])


def attend_back_call(lengths, counts, packed, grad_mixed, lse, table):
    tokens = packed.shape[0]
    rows = tokens // ROW
    low = jax.ShapeDtypeStruct((tokens, D), BF16)
    table_block = pl.BlockSpec((1, 2, SPAN), lambda p, r, *_: (p, 0, 0))
    return pl.pallas_call(
        attend_back_kernel,
        grid_spec=pltpu.PrefetchScalarGridSpec(
            num_scalar_prefetch=2,
            grid=(PAIRS, rows),
            in_specs=[
                pair_blocks(0),
                pair_blocks(PAIRS),
                pair_blocks(2 * PAIRS),
                pair_blocks(0),
                pair_blocks(0),
                table_block,
            ],
            out_specs=[pair_blocks(0), pair_blocks(0), pair_blocks(0), table_block],
            scratch_shapes=[
                pltpu.VMEM((2, SUB, TOEP), F32),
                pltpu.VMEM((2, SUB, TOEP), F32),
                pltpu.VMEM((ROW, WIDE), F32),
                pltpu.VMEM((ROW, WIDE), F32),
            ],
        ),
        out_shape=[low, low, low, jax.ShapeDtypeStruct((PAIRS, 2, SPAN), F32)],
        compiler_params=params(),
        cost_estimate=cost(30e9, 16e6, 7e6),
        name="attend_back",
    )(lengths, counts, packed, packed, packed, grad_mixed, lse, table)


def middle_kernel(x_ref, mixed_ref, gain_ref, weight_ref, middle_ref, second_ref):
    middle = x_ref[...].astype(F32) + dot(mixed_ref[...], weight_ref[...], NT)
    middle_ref[...] = middle
    scale = lax.rsqrt(jnp.mean(middle * middle, axis=-1, keepdims=True) + EPS)
    second_ref[...] = (middle * scale * gain_ref[...]).astype(BF16)


def middle_call(x, mixed, gain, weight):
    tokens = x.shape[0]
    return pl.pallas_call(
        middle_kernel,
        grid=(tokens // TILE,),
        in_specs=[tiles(TILE, D), tiles(TILE, D), whole((1, D)), whole((D, D))],
        out_specs=[tiles(TILE, D), tiles(TILE, D)],
        out_shape=[
            jax.ShapeDtypeStruct((tokens, D), F32),
            jax.ShapeDtypeStruct((tokens, D), BF16),
        ],
        compiler_params=params(),
        cost_estimate=cost(2 * tokens * D * D, 9e6),
        name="middle",
    )(x, mixed, gain, weight)


def feed_kernel(second_ref, grad_ref, up_ref, down_ref, out_ref, back_ref, gup_ref, gdown_ref, hidden, dpre):
    step = pl.program_id(0)
    tokens = second_ref.shape[0]

    @pl.when(step == 0)
    def _():
        out_ref[...] = jnp.zeros_like(out_ref)
        back_ref[...] = jnp.zeros_like(back_ref)

    up = up_ref[...]
    down = down_ref[...]

    @pl.loop(0, tokens // TILE)
    def _(tile):
        at = pl.ds(pl.multiple_of(tile * TILE, TILE), TILE)
        u = dot(second_ref[at, :], up, NT)
        square = u * u
        t = jnp.tanh(0.7978845608 * u * (1.0 + 0.044715 * square))
        plus = 0.5 * (1.0 + t)
        low = (u * plus).astype(BF16)
        slope = plus + (0.5 * 0.7978845608) * u * (1.0 - t * t) * (1.0 + 3 * 0.044715 * square)
        dh = dot(grad_ref[at, :], down, NT).astype(BF16).astype(F32)
        du = (dh * slope).astype(BF16)
        hidden[at, :] = low
        dpre[at, :] = du
        out_ref[at, :] += dot(low, down, NN)
        back_ref[at, :] += dot(du, up, NN)

    gdown_ref[...] = dot(hidden[...], grad_ref[...], TN)
    gup_ref[...] = dot(dpre[...], second_ref[...], TN)


def feed_call(second, out_grad, up, down, chunk=384):
    tokens = second.shape[0]
    units = up.shape[0]
    acc = jax.ShapeDtypeStruct((tokens, D), F32)
    grad = jax.ShapeDtypeStruct((units, D), F32)
    return pl.pallas_call(
        feed_kernel,
        grid=(units // chunk,),
        in_specs=[whole((tokens, D)), whole((tokens, D)), tiles(chunk, D), tiles(chunk, D)],
        out_specs=[whole((tokens, D)), whole((tokens, D)), tiles(chunk, D), tiles(chunk, D)],
        out_shape=[acc, acc, grad, grad],
        scratch_shapes=[pltpu.VMEM((tokens, chunk), BF16), pltpu.VMEM((tokens, chunk), BF16)],
        compiler_params=params(),
        cost_estimate=cost(12 * tokens * units * D, 40e6, tokens * units),
        name="feed",
    )(second, out_grad, up, down)


def middle_back_kernel(
    part_ref, middle_ref, grad_ref, mixed_ref, gain_ref, weight_ref,
    dmiddle_ref, dmixed_ref, dgain_ref, dweight_ref,
):
    step = pl.program_id(0)
    db = part_ref[...]
    middle = middle_ref[...]
    scale = lax.rsqrt(jnp.mean(middle * middle, axis=-1, keepdims=True) + EPS)
    dn = db * gain_ref[...]
    inner = jnp.mean(dn * middle, axis=-1, keepdims=True)
    dmiddle = grad_ref[...].astype(F32) + scale * dn - middle * (scale * scale * scale * inner)
    dmiddle_ref[...] = dmiddle
    low = dmiddle.astype(BF16)
    dmixed_ref[...] = dot(low, weight_ref[...], NN).astype(BF16)
    dgain = jnp.sum(db * middle * scale, axis=0, keepdims=True)
    dweight = dot(low, mixed_ref[...], TN)

    @pl.when(step == 0)
    def _():
        dgain_ref[...] = dgain
        dweight_ref[...] = dweight

    @pl.when(step > 0)
    def _():
        dgain_ref[...] += dgain
        dweight_ref[...] += dweight


def middle_back_call(part, middle, out_grad, mixed, gain, weight):
    tokens = part.shape[0]
    return pl.pallas_call(
        middle_back_kernel,
        grid=(tokens // TILE,),
        in_specs=[tiles(TILE, D)] * 4 + [whole((1, D)), whole((D, D))],
        out_specs=[tiles(TILE, D), tiles(TILE, D), whole((1, D)), whole((D, D))],
        out_shape=[
            jax.ShapeDtypeStruct((tokens, D), F32),
            jax.ShapeDtypeStruct((tokens, D), BF16),
            jax.ShapeDtypeStruct((1, D), F32),
            jax.ShapeDtypeStruct((D, D), F32),
        ],
        compiler_params=params(),
        cost_estimate=cost(4 * tokens * D * D, 18e6),
        name="middle_back",
    )(part, middle, out_grad, mixed, gain, weight)


def qkv_grad_kernel(dq_ref, dk_ref, dv_ref, normed_ref, out_ref):
    step = pl.program_id(0)
    for part, ref in enumerate((dq_ref, dk_ref, dv_ref)):

        @pl.when(step // 2 == part)
        def _(ref=ref):
            out_ref[...] = dot(ref[...], normed_ref[...], TN)


def qkv_grad_call(dq, dk, dv, normed):
    tokens = normed.shape[0]
    half = D // 2

    def columns(part):
        return pl.BlockSpec((tokens, half), lambda i: (0, jnp.clip(i - 2 * part, 0, 1)))

    return pl.pallas_call(
        qkv_grad_kernel,
        grid=(6,),
        in_specs=[columns(0), columns(1), columns(2), whole((tokens, D))],
        out_specs=tiles(half, D),
        out_shape=jax.ShapeDtypeStruct((3 * D, D), F32),
        compiler_params=params(),
        cost_estimate=cost(2 * tokens * D * 3 * D, 16e6),
        name="qkv_grad",
    )(dq, dk, dv, normed)


def input_back_kernel(dq_ref, dk_ref, dv_ref, x_ref, dmiddle_ref, gain_ref, weight_ref, dx_ref, dgain_ref):
    step = pl.program_id(0)
    da = dot(dq_ref[...], weight_ref[:D, :], NN)
    da += dot(dk_ref[...], weight_ref[D : 2 * D, :], NN)
    da += dot(dv_ref[...], weight_ref[2 * D :, :], NN)
    x = x_ref[...].astype(F32)
    scale = lax.rsqrt(jnp.mean(x * x, axis=-1, keepdims=True) + EPS)
    dm = da * gain_ref[...]
    inner = jnp.mean(dm * x, axis=-1, keepdims=True)
    dx_ref[...] = dmiddle_ref[...] + scale * dm - x * (scale * scale * scale * inner)
    dgain = jnp.sum(da * x * scale, axis=0, keepdims=True)

    @pl.when(step == 0)
    def _():
        dgain_ref[...] = dgain

    @pl.when(step > 0)
    def _():
        dgain_ref[...] += dgain


def input_back_call(dq, dk, dv, x, dmiddle, gain, weight):
    tokens = x.shape[0]
    return pl.pallas_call(
        input_back_kernel,
        grid=(tokens // TILE,),
        in_specs=[tiles(TILE, D)] * 5 + [whole((1, D)), whole((3 * D, D))],
        out_specs=[tiles(TILE, D), whole((1, D))],
        out_shape=[jax.ShapeDtypeStruct((tokens, D), F32), jax.ShapeDtypeStruct((1, D), F32)],
        compiler_params=params(),
        cost_estimate=cost(2 * tokens * D * 3 * D, 18e6),
        name="input_back",
    )(dq, dk, dv, x, dmiddle, gain, weight)


def adam_update(param, grad, first, second, rate):
    first_new = BETA_ONE * first + (1.0 - BETA_ONE) * grad
    second_new = BETA_TWO * second + (1.0 - BETA_TWO) * grad * grad
    first_hat = first_new / (1.0 - BETA_ONE**STEP)
    second_hat = second_new / (1.0 - BETA_TWO**STEP)
    param_new = param - rate * (first_hat / (jnp.sqrt(second_hat) + ADAM_EPS) + DECAY * param)
    return (param_new, first_new, second_new)


AXES = ("z1", "z0", "x", "y", "c", "r")


def on_device(
    layer_input, out_grad, matrices, mat_first, mat_second, mat_ema, gains, gain_first, gain_second,
    rel_bias, bias_first, bias_second, bucket_len, item_count, bucket_table,
):
    shards = jnp.swapaxes(matrices, 1, 2).astype(BF16)
    gathered = [lax.all_gather(shards[i], AXES, axis=0, tiled=True) for i in range(3)]
    qkv_weight = gathered[0][: 3 * D]
    out_weight = gathered[0][3 * D :]

    flipped = jnp.concatenate([bucket_table[::-1], jnp.full((1,), -1, jnp.int32)])
    onehot = (flipped[None, :] == jnp.arange(BUCKETS, dtype=jnp.int32)[:, None]).astype(F32)
    table = jnp.dot(rel_bias.T, onehot, precision=lax.Precision.HIGHEST).reshape(PAIRS, 2, SPAN)

    gain_one = gains[0:1]
    gain_two = gains[1:2]
    normed, packed = qkv_call(layer_input, gain_one, qkv_weight)
    mixed, lse = attend_call(bucket_len, item_count, packed, table)
    middle, second = middle_call(layer_input, mixed, gain_two, out_weight)
    ffn, back, grad_up, grad_down = feed_call(second, out_grad, gathered[1], gathered[2])
    dmiddle, dmixed, dgain_two, grad_out = middle_back_call(
        back, middle, out_grad, mixed, gain_two, out_weight
    )
    dq, dk, dv, dlines = attend_back_call(bucket_len, item_count, packed, dmixed, lse, table)
    grad_qkv = qkv_grad_call(dq, dk, dv, normed)
    input_grad, dgain_one = input_back_call(dq, dk, dv, layer_input, dmiddle, gain_one, qkv_weight)
    layer_output = (middle + ffn).astype(BF16)

    def scatter(value):
        return lax.psum_scatter(value, AXES, scatter_dimension=0, tiled=True)

    summed = [scatter(jnp.concatenate([grad_qkv, grad_out])), scatter(grad_up), scatter(grad_down)]
    mat_grad = jnp.swapaxes(jnp.stack(summed), 1, 2)
    bias_local = jnp.dot(onehot, dlines.reshape(HEADS, SPAN).T, precision=lax.Precision.HIGHEST)
    gain_local = jnp.concatenate([dgain_one, dgain_two])
    gain_grad, bias_grad = lax.psum((gain_local, bias_local), AXES)
    mat_new, mat_first_new, mat_second_new = adam_update(
        matrices, mat_grad, mat_first, mat_second, RATE
    )
    mat_ema_new = EMA_KEEP * mat_ema + (1.0 - EMA_KEEP) * mat_new
    gain_new, gain_first_new, gain_second_new = adam_update(
        gains, gain_grad, gain_first, gain_second, RATE_SMALL
    )
    bias_new, bias_first_new, bias_second_new = adam_update(
        rel_bias, bias_grad, bias_first, bias_second, RATE_SMALL
    )
    return (
        layer_output, input_grad, mat_grad, mat_new, mat_first_new, mat_second_new, mat_ema_new,
        gain_grad, gain_new, gain_first_new, gain_second_new,
        bias_grad, bias_new, bias_first_new, bias_second_new,
    )


def solution(mesh):
    devices = mesh.devices.size
    fine = Mesh(mesh.devices.reshape(2, 2, 2, 2, 2, devices // 32), AXES)
    rows = P(AXES, None)
    columns = P(None, None, AXES)
    return jax.shard_map(
        on_device,
        mesh=fine,
        in_specs=(rows, rows) + (columns,) * 4 + (P(),) * 6 + (P(AXES), P(AXES), P()),
        out_specs=(rows, rows) + (columns,) * 5 + (P(),) * 8,
        check_vma=False,
    )
```

```python
import functools

import jax
import jax.numpy as jnp
from jax import lax
from jax.experimental import pallas as pl
from jax.experimental.pallas import tpu as pltpu
from jax.sharding import Mesh, PartitionSpec as P

D = 768
FF = 3072
HEADS = 12
HD = 64
BUCKETS = 32
ROW = 512
STEP = 10
PAIRS = HEADS // 2
WIDE = 2 * HD
SUB = 128
SPAN = 1024
TOEP = 896

EPS = 1e-06
RATE = 0.05
RATE_SMALL = 0.5
BETA_ONE = 0.9
BETA_TWO = 0.999
ADAM_EPS = 1e-08
DECAY = 0.1
EMA_KEEP = 0.75

F32 = jnp.float32
BF16 = jnp.bfloat16
VMEM_LIMIT = 56 * 1024 * 1024
TILE = 256
SHARD = 96
HALF = 48
PIECES = 16
GROUP = 2
GROUPS = PAIRS // GROUP
PART = GROUP * WIDE

NN = (((1,), (0,)), ((), ()))
NT = (((1,), (1,)), ((), ()))
TN = (((0,), (0,)), ((), ()))


def dot(left, right, dims):
    return lax.dot_general(left, right, dims, preferred_element_type=F32)


def params(**more):
    return pltpu.CompilerParams(vmem_limit_bytes=VMEM_LIMIT, **more)


def cost(flops, moved, special=0):
    return pl.CostEstimate(flops=int(flops), bytes_accessed=int(moved), transcendentals=int(special))


def whole(shape):
    return pl.BlockSpec(shape, lambda *_: (0,) * len(shape))


def tiles(rows, columns):
    return pl.BlockSpec((rows, columns), lambda i, *_: (i, 0))


def out_block():
    return pl.BlockSpec((D, D), lambda i: (3, 0))


def qkv_kernel(me_ref, *refs):
    pieces = refs[:PIECES]
    x_ref, gain_ref, normed_ref, packed_ref, weight_ref, sem = refs[PIECES:]

    @pl.when(pl.program_id(0) == 0)
    def _():
        copies = []
        for i, ref in enumerate(pieces):
            core, half, plane = i // 8, i // 4 % 2, i % 4
            for z in range(4):
                owner = me_ref[0] ^ (z * 8 + plane * 2 + core)
                row = pl.multiple_of(owner * SHARD + half * HALF, 16)
                copies.append(
                    pltpu.make_async_copy(
                        ref.at[pl.ds(z * HALF, HALF)], weight_ref.at[pl.ds(row, HALF)], sem
                    )
                )
        for copy in copies:
            copy.start()
        for copy in copies:
            copy.wait()

    x = x_ref[...].astype(F32)
    scale = lax.rsqrt(jnp.mean(x * x, axis=-1, keepdims=True) + EPS)
    normed = (x * scale * gain_ref[...]).astype(BF16)
    normed_ref[...] = normed
    for part in range(3):
        cols = slice(part * D, (part + 1) * D)
        packed_ref[:, cols] = dot(normed, weight_ref[cols, :], NT).astype(BF16)


def qkv_call(me, pieces, x, gain):
    tokens = x.shape[0]
    anywhere = pl.BlockSpec(memory_space=pl.ANY)
    return pl.pallas_call(
        qkv_kernel,
        grid_spec=pltpu.PrefetchScalarGridSpec(
            num_scalar_prefetch=1,
            grid=(tokens // TILE,),
            in_specs=[anywhere] * PIECES + [tiles(TILE, D), whole((1, D))],
            out_specs=[tiles(TILE, D), tiles(TILE, 3 * D), whole((4 * D, D))],
            scratch_shapes=[pltpu.SemaphoreType.DMA],
        ),
        out_shape=[
            jax.ShapeDtypeStruct((tokens, D), BF16),
            jax.ShapeDtypeStruct((tokens, 3 * D), BF16),
            jax.ShapeDtypeStruct((4 * D, D), BF16),
        ],
        compiler_params=params(),
        cost_estimate=cost(2 * tokens * D * 3 * D, 16e6),
        name="norm_qkv",
    )(me, *pieces, x, gain)


def fill_toeplitz(table_ref, toep):
    for h in range(2):
        line = jnp.broadcast_to(table_ref[0, h : h + 1, :], (SUB, SPAN))
        rolled = pltpu.roll(line, SPAN - (SUB - 1), 1, stride=1, stride_axis=0)
        toep[h] = rolled[:, :TOEP]


def head_masks():
    lane = lax.broadcasted_iota(jnp.int32, (1, WIDE), 1)
    return [(lane < HD).astype(BF16), (lane >= HD).astype(BF16)]


def bias_block(toep, h, first, rows, span):
    parts = []
    for t in range(rows // SUB):
        left = ROW - SUB - first - t * SUB
        parts.append(toep[h, :, left : left + span])
    return parts[0] if len(parts) == 1 else jnp.concatenate(parts, axis=0)


def for_items(length, count, body):
    @pl.when(length == ROW)
    def _():
        for first in range(0, ROW, 2 * SUB):
            body(0, first, 2 * SUB, ROW)

    @pl.when(length == ROW // 2)
    def _():
        @pl.loop(0, count)
        def _(item):
            body(item * (ROW // 2), 0, ROW // 2, ROW // 2)

    @pl.when(length == ROW // 4)
    def _():
        @pl.loop(0, count)
        def _(item):
            body(item * (ROW // 4), 0, ROW // 4, ROW // 4)


def aligned(start):
    return start if isinstance(start, int) else pl.multiple_of(start, SUB)


def attend_kernel(len_ref, count_ref, q_ref, k_ref, v_ref, table_ref, o_ref, lse_ref, toep):
    row = pl.program_id(1)

    @pl.when(row == 0)
    def _():
        fill_toeplitz(table_ref, toep)

    length = len_ref[row]
    count = count_ref[row]
    masks = head_masks()

    @pl.when(length * count < ROW)
    def _():
        o_ref[...] = jnp.zeros_like(o_ref)
        lse_ref[...] = jnp.zeros_like(lse_ref)

    def body(start, first, rows, span):
        keys_at = pl.ds(aligned(start), span)
        rows_at = pl.ds(aligned(start + first), rows)
        q = q_ref[rows_at, :]
        k = k_ref[keys_at, :]
        v = v_ref[keys_at, :]
        mixed = None
        stats = []
        for h in range(2):
            s = dot(q, k * masks[h], NT) + bias_block(toep, h, first, rows, span)
            top = jnp.max(s, axis=-1, keepdims=True)
            e = jnp.exp(s - top)
            total = jnp.sum(e, axis=-1, keepdims=True)
            p = (e * (1.0 / total)).astype(BF16)
            part = dot(p, v * masks[h], NN)
            mixed = part if mixed is None else mixed + part
            stats.append(jnp.broadcast_to(top + jnp.log(total), (rows, HD)))
        o_ref[rows_at, :] = mixed.astype(BF16)
        lse_ref[rows_at, :] = jnp.concatenate(stats, axis=1)

    for_items(length, count, body)


def pair_blocks(offset):
    return pl.BlockSpec((ROW, WIDE), lambda p, r, *_: (r, offset + p))


def attend_call(lengths, counts, packed, table, group):
    tokens = packed.shape[0]
    rows = tokens // ROW
    at = group * GROUP
    return pl.pallas_call(
        attend_kernel,
        grid_spec=pltpu.PrefetchScalarGridSpec(
            num_scalar_prefetch=2,
            grid=(GROUP, rows),
            in_specs=[
                pair_blocks(at),
                pair_blocks(PAIRS + at),
                pair_blocks(2 * PAIRS + at),
                pl.BlockSpec((1, 2, SPAN), lambda p, r, *_: (at + p, 0, 0)),
            ],
            out_specs=[pair_blocks(0), pair_blocks(0)],
            scratch_shapes=[pltpu.VMEM((2, SUB, TOEP), F32)],
        ),
        out_shape=[
            jax.ShapeDtypeStruct((tokens, GROUP * WIDE), BF16),
            jax.ShapeDtypeStruct((tokens, GROUP * WIDE), F32),
        ],
        compiler_params=params(),
        cost_estimate=cost(4e9, 4e6, 2e6),
        name="attend",
    )(lengths, counts, packed, packed, packed, table)


def fold_diagonals(grid):
    height = SUB
    total = jnp.concatenate([grid, jnp.zeros((SUB, SPAN - TOEP), F32)], axis=1)
    while height > 8:
        height //= 2
        total = pltpu.roll(total[:height], height, 1) + total[height:]
    line = total[7:8]
    for r in range(7):
        line = line + pltpu.roll(total, 7 - r, 1)[r : r + 1]
    return line


def attend_back_kernel(
    len_ref, count_ref, q_ref, k_ref, v_ref, do_ref, lse_ref, table_ref,
    dq_ref, dk_ref, dv_ref, dbias_ref, toep, diag, dk_acc, dv_acc,
):
    row = pl.program_id(1)

    @pl.when(row == 0)
    def _():
        fill_toeplitz(table_ref, toep)
        diag[...] = jnp.zeros_like(diag)

    length = len_ref[row]
    count = count_ref[row]
    masks = head_masks()

    @pl.when(length * count < ROW)
    def _():
        dq_ref[...] = jnp.zeros_like(dq_ref)
        dk_ref[...] = jnp.zeros_like(dk_ref)
        dv_ref[...] = jnp.zeros_like(dv_ref)

    def body(start, first, rows, span):
        keys_at = pl.ds(aligned(start), span)
        rows_at = pl.ds(aligned(start + first), rows)
        q = q_ref[rows_at, :]
        do = do_ref[rows_at, :]
        k = k_ref[keys_at, :]
        v = v_ref[keys_at, :]
        dq = dk = dv = None
        for h in range(2):
            kh = k * masks[h]
            lse = lse_ref[rows_at, h * HD : h * HD + 1]
            s = dot(q, kh, NT) + bias_block(toep, h, first, rows, span)
            p = jnp.exp(s - lse)
            dp = dot(do, v * masks[h], NT)
            t = p * dp
            ds = t - p * jnp.sum(t, axis=-1, keepdims=True)
            for sub in range(rows // SUB):
                left = ROW - SUB - first - sub * SUB
                diag[h, :, left : left + span] += ds[sub * SUB : (sub + 1) * SUB]
            low = ds.astype(BF16)
            parts = (
                dot(low, kh, NN),
                dot(low, q * masks[h], TN),
                dot(p.astype(BF16), do * masks[h], TN),
            )
            if dq is None:
                dq, dk, dv = parts
            else:
                dq, dk, dv = dq + parts[0], dk + parts[1], dv + parts[2]
        dq_ref[rows_at, :] = dq.astype(BF16)
        if rows == span:
            dk_ref[keys_at, :] = dk.astype(BF16)
            dv_ref[keys_at, :] = dv.astype(BF16)
        elif first == 0:
            dk_acc[...] = dk
            dv_acc[...] = dv
        else:
            dk_ref[...] = (dk_acc[...] + dk).astype(BF16)
            dv_ref[...] = (dv_acc[...] + dv).astype(BF16)

    for_items(length, count, body)

    @pl.when(row == pl.num_programs(1) - 1)
    def _():
        for h in range(2):
            dbias_ref[0, h : h + 1, :] = fold_diagonals(diag[h])


def attend_back_call(lengths, counts, packed, grad_mixed, lse, table, group):
    tokens = packed.shape[0]
    rows = tokens // ROW
    at = group * GROUP
    low = jax.ShapeDtypeStruct((tokens, GROUP * WIDE), BF16)
    return pl.pallas_call(
        attend_back_kernel,
        grid_spec=pltpu.PrefetchScalarGridSpec(
            num_scalar_prefetch=2,
            grid=(GROUP, rows),
            in_specs=[
                pair_blocks(at),
                pair_blocks(PAIRS + at),
                pair_blocks(2 * PAIRS + at),
                pair_blocks(at),
                pair_blocks(0),
                pl.BlockSpec((1, 2, SPAN), lambda p, r, *_: (at + p, 0, 0)),
            ],
            out_specs=[
                pair_blocks(0),
                pair_blocks(0),
                pair_blocks(0),
                pl.BlockSpec((1, 2, SPAN), lambda p, r, *_: (p, 0, 0)),
            ],
            scratch_shapes=[
                pltpu.VMEM((2, SUB, TOEP), F32),
                pltpu.VMEM((2, SUB, TOEP), F32),
                pltpu.VMEM((ROW, WIDE), F32),
                pltpu.VMEM((ROW, WIDE), F32),
            ],
        ),
        out_shape=[low, low, low, jax.ShapeDtypeStruct((GROUP, 2, SPAN), F32)],
        compiler_params=params(),
        cost_estimate=cost(6e9, 5e6, 2e6),
        name="attend_back",
    )(lengths, counts, packed, packed, packed, grad_mixed, lse, table)


def middle_kernel(x_ref, *refs):
    mixed_refs = refs[:GROUPS]
    gain_ref, weight_ref, middle_ref, second_ref = refs[GROUPS:]
    middle = x_ref[...].astype(F32)
    for g, ref in enumerate(mixed_refs):
        middle += dot(ref[...], weight_ref[:, g * PART : (g + 1) * PART], NT)
    middle_ref[...] = middle
    scale = lax.rsqrt(jnp.mean(middle * middle, axis=-1, keepdims=True) + EPS)
    second_ref[...] = (middle * scale * gain_ref[...]).astype(BF16)


def middle_call(x, mixed, gain, weight):
    tokens = x.shape[0]
    return pl.pallas_call(
        middle_kernel,
        grid=(tokens // TILE,),
        in_specs=[tiles(TILE, D)] + [tiles(TILE, PART)] * GROUPS + [whole((1, D)), out_block()],
        out_specs=[tiles(TILE, D), tiles(TILE, D)],
        out_shape=[
            jax.ShapeDtypeStruct((tokens, D), F32),
            jax.ShapeDtypeStruct((tokens, D), BF16),
        ],
        compiler_params=params(),
        cost_estimate=cost(2 * tokens * D * D, 9e6),
        name="middle",
    )(x, *mixed, gain, weight)


def feed_kernel(*refs):
    up_ref, down_ref, second_ref, grad_ref, start_ref, back_ref, hidden_ref, out_ref, up, down, dpre = refs
    half = pl.program_id(0)
    tokens = second_ref.shape[0]
    up[...] = up_ref[...].reshape(D, D)
    down[...] = down_ref[...].reshape(D, D)

    @pl.when(half == 0)
    def _():
        back_ref[...] = jnp.zeros_like(back_ref) if start_ref is None else start_ref[...]

    @pl.loop(0, tokens // TILE)
    def _(tile):
        at = pl.ds(pl.multiple_of(tile * TILE, TILE), TILE)
        u = dot(second_ref[at, :], up[...], NT)
        square = u * u
        t = jnp.tanh(0.7978845608 * u * (1.0 + 0.044715 * square))
        plus = 0.5 * (1.0 + t)
        hidden_ref[at, :] = (u * plus).astype(BF16)
        slope = plus + (0.5 * 0.7978845608) * u * (1.0 - t * t) * (1.0 + 3 * 0.044715 * square)
        dh = dot(grad_ref[at, :], down[...], NT).astype(BF16).astype(F32)
        du = (dh * slope).astype(BF16)
        dpre[at, :] = du
        back_ref[at, :] += dot(du, up[...], NN)

    out_ref[0, 0] = dot(dpre[...], second_ref[...], TN).astype(out_ref.dtype)
    out_ref[0, 1] = dot(hidden_ref[...], grad_ref[...], TN).astype(out_ref.dtype)


def first_feed_kernel(*refs):
    feed_kernel(*refs[:4], None, *refs[4:])


def feed_call(weights, second, out_grad, start, kind):
    tokens = second.shape[0]
    flat = pl.BlockSpec((tokens, D), lambda i: (0, 0), pipeline_mode=pl.Buffered(1))
    more = [] if start is None else [start]
    return pl.pallas_call(
        first_feed_kernel if start is None else feed_kernel,
        grid=(2,),
        in_specs=[
            pl.BlockSpec((16, HALF, D), lambda i: (0, 2 * i, 0)),
            pl.BlockSpec((16, HALF, D), lambda i: (0, 2 * i + 1, 0)),
        ]
        + [flat, flat]
        + [flat] * len(more),
        out_specs=[
            whole((tokens, D)),
            pl.BlockSpec((tokens, D), lambda i: (0, i)),
            pl.BlockSpec((1, 2, D, D), lambda i: (i, 0, 0, 0)),
        ],
        out_shape=[
            jax.ShapeDtypeStruct((tokens, D), F32),
            jax.ShapeDtypeStruct((tokens, 2 * D), BF16),
            jax.ShapeDtypeStruct((2, 2, D, D), kind),
        ],
        scratch_shapes=[pltpu.VMEM((D, D), BF16), pltpu.VMEM((D, D), BF16), pltpu.VMEM((tokens, D), BF16)],
        compiler_params=params(),
        cost_estimate=cost(10 * tokens * 2 * D * D, 30e6, tokens * 2 * D),
        name="feed",
    )(weights, weights, second, out_grad, *more)


def output_kernel(middle_ref, first_ref, second_ref, *refs):
    downs, out_ref = refs[:4], refs[4]
    total = middle_ref[...]
    for i, ref in enumerate(downs):
        hidden = (first_ref, second_ref)[i % 2]
        cols = slice(i // 2 * D, (i // 2 + 1) * D)
        total += dot(hidden[:, cols], ref[...].reshape(D, D), NN)
    out_ref[...] = total.astype(BF16)


def unit_block(index):
    return pl.BlockSpec((16, HALF, D), lambda i: (0, index, 0), pipeline_mode=pl.Buffered(1))


def output_call(middle, hidden_own, hidden_other, own, other):
    tokens = middle.shape[0]
    return pl.pallas_call(
        output_kernel,
        grid=(tokens // TILE,),
        in_specs=[tiles(TILE, D), tiles(TILE, 2 * D), tiles(TILE, 2 * D)]
        + [unit_block(1), unit_block(1), unit_block(3), unit_block(3)],
        out_specs=tiles(TILE, D),
        out_shape=jax.ShapeDtypeStruct((tokens, D), BF16),
        compiler_params=params(),
        cost_estimate=cost(2 * tokens * FF * D, 17e6),
        name="output",
    )(middle, hidden_own, hidden_other, own, other, own, other)


def middle_back_kernel(part_ref, middle_ref, grad_ref, *refs):
    mixed_refs = refs[:GROUPS]
    gain_ref, weight_ref, dmiddle_ref, dmixed_ref, dgain_ref, dweight_ref = refs[GROUPS:]
    step = pl.program_id(0)
    db = part_ref[...]
    middle = middle_ref[...]
    scale = lax.rsqrt(jnp.mean(middle * middle, axis=-1, keepdims=True) + EPS)
    dn = db * gain_ref[...]
    inner = jnp.mean(dn * middle, axis=-1, keepdims=True)
    dmiddle = grad_ref[...].astype(F32) + scale * dn - middle * (scale * scale * scale * inner)
    dmiddle_ref[...] = dmiddle
    low = dmiddle.astype(BF16)
    dmixed_ref[...] = dot(low, weight_ref[...], NN).astype(BF16)
    dgain = jnp.sum(db * middle * scale, axis=0, keepdims=True)
    dweight = jnp.concatenate([dot(low, ref[...], TN) for ref in mixed_refs], axis=1)

    @pl.when(step == 0)
    def _():
        dgain_ref[...] = dgain
        dweight_ref[...] = dweight

    @pl.when(step > 0)
    def _():
        dgain_ref[...] += dgain
        dweight_ref[...] += dweight


def middle_back_call(part, middle, out_grad, mixed, gain, weight):
    tokens = part.shape[0]
    return pl.pallas_call(
        middle_back_kernel,
        grid=(tokens // TILE,),
        in_specs=[tiles(TILE, D)] * 3 + [tiles(TILE, PART)] * GROUPS + [whole((1, D)), out_block()],
        out_specs=[tiles(TILE, D), tiles(TILE, D), whole((1, D)), whole((D, D))],
        out_shape=[
            jax.ShapeDtypeStruct((tokens, D), F32),
            jax.ShapeDtypeStruct((tokens, D), BF16),
            jax.ShapeDtypeStruct((1, D), F32),
            jax.ShapeDtypeStruct((D, D), F32),
        ],
        compiler_params=params(),
        cost_estimate=cost(4 * tokens * D * D, 18e6),
        name="middle_back",
    )(part, middle, out_grad, *mixed, gain, weight)


def qkv_grad_kernel(me_ref, *refs):
    grads = refs[: 3 * GROUPS]
    normed_ref, dout_ref, own_ref, other_ref, total = refs[3 * GROUPS :]
    step = pl.program_id(0)
    for part in range(3):

        @pl.when(step == part)
        def _(part=part):
            for g in range(GROUPS):
                at = part * D + g * PART
                total[at : at + PART] = dot(grads[part * GROUPS + g][...], normed_ref[...], TN)

    @pl.when(step == 2)
    def _():
        total[3 * D :] = dout_ref[...]
        for core, out in enumerate((own_ref, other_ref)):

            @pl.loop(0, 32)
            def _(i):
                half, z, plane = i // 16, i // 4 % 4, i % 4
                owner = me_ref[0] ^ (z * 8 + plane * 2 + core)
                row = pl.multiple_of(owner * SHARD + half * HALF, 16)
                to = pl.multiple_of(i * HALF, 16)
                out[pl.ds(to, HALF), :] = total[pl.ds(row, HALF), :].astype(out.dtype)


def qkv_grad_call(me, dq, dk, dv, normed, grad_out):
    tokens = normed.shape[0]
    return pl.pallas_call(
        qkv_grad_kernel,
        grid_spec=pltpu.PrefetchScalarGridSpec(
            num_scalar_prefetch=1,
            grid=(3,),
            in_specs=[whole((tokens, PART))] * (3 * GROUPS) + [whole((tokens, D)), whole((D, D))],
            out_specs=[whole((2 * D, D)), whole((2 * D, D))],
            scratch_shapes=[pltpu.VMEM((4 * D, D), F32)],
        ),
        out_shape=[
            jax.ShapeDtypeStruct((2 * D, D), F32),
            jax.ShapeDtypeStruct((2 * D, D), BF16),
        ],
        compiler_params=params(),
        cost_estimate=cost(2 * tokens * D * 3 * D, 18e6),
        name="qkv_grad",
    )(me, *dq, *dk, *dv, normed, grad_out)


def input_back_kernel(*refs):
    grads = refs[: 3 * GROUPS]
    x_ref, dmiddle_ref, gain_ref, weight_ref, dx_ref, dgain_ref = refs[3 * GROUPS :]
    step = pl.program_id(0)
    da = jnp.zeros(dx_ref.shape, F32)
    for i, ref in enumerate(grads):
        da += dot(ref[...], weight_ref[i * PART : (i + 1) * PART, :], NN)
    x = x_ref[...].astype(F32)
    scale = lax.rsqrt(jnp.mean(x * x, axis=-1, keepdims=True) + EPS)
    dm = da * gain_ref[...]
    inner = jnp.mean(dm * x, axis=-1, keepdims=True)
    dx_ref[...] = dmiddle_ref[...] + scale * dm - x * (scale * scale * scale * inner)
    dgain = jnp.sum(da * x * scale, axis=0, keepdims=True)

    @pl.when(step == 0)
    def _():
        dgain_ref[...] = dgain

    @pl.when(step > 0)
    def _():
        dgain_ref[...] += dgain


def input_back_call(dq, dk, dv, x, dmiddle, gain, weight):
    tokens = x.shape[0]
    return pl.pallas_call(
        input_back_kernel,
        grid=(tokens // TILE,),
        in_specs=[tiles(TILE, PART)] * (3 * GROUPS) + [tiles(TILE, D)] * 2 + [whole((1, D)), whole((3 * D, D))],
        out_specs=[tiles(TILE, D), whole((1, D))],
        out_shape=[jax.ShapeDtypeStruct((tokens, D), F32), jax.ShapeDtypeStruct((1, D), F32)],
        compiler_params=params(),
        cost_estimate=cost(2 * tokens * D * 3 * D, 18e6),
        name="input_back",
    )(*dq, *dk, *dv, x, dmiddle, gain, weight)


def adam_update(param, grad, first, second, rate):
    first_new = BETA_ONE * first + (1.0 - BETA_ONE) * grad
    second_new = BETA_TWO * second + (1.0 - BETA_TWO) * grad * grad
    first_hat = first_new / (1.0 - BETA_ONE**STEP)
    second_hat = second_new / (1.0 - BETA_TWO**STEP)
    param_new = param - rate * (first_hat / (jnp.sqrt(second_hat) + ADAM_EPS) + DECAY * param)
    return (param_new, first_new, second_new)


AXES = ("tree", "rest")
CORE, Y, X, Z = 1, 2, 4, 8


def swap(value, bits):
    return lax.ppermute(value, "tree", [(i, i ^ bits) for i in range(32)])


def tie(values, after):
    return list(lax.optimization_barrier(tuple(values) + tuple(after))[: len(values)])


def gather_z(shard):
    return [shard] + [swap(shard, k * Z) for k in (1, 2, 3)]


def gather_halves(line):
    return [jnp.concatenate([p[:HALF] for p in line]), jnp.concatenate([p[HALF:] for p in line])]


def gather_plane(halves):
    return [swap(halves[0], X), swap(halves[1], Y)]


def gather_rest(halves, turned):
    return [swap(halves[0], Y), swap(turned[0], Y), swap(halves[1], X), swap(turned[1], X)]


def gathered(halves, turned, rest):
    return [halves[0], rest[0], turned[0], rest[1], halves[1], turned[1], rest[2], rest[3]]


def gather_core(pieces):
    return [swap(p, CORE) for p in pieces]


def low(value):
    return value.astype(BF16)


def pick(value, axis, index):
    return lax.dynamic_index_in_dim(value, index, axis, keepdims=False)


def reduce_plane(at, own, got):
    own = own.reshape(-1, 2, 4, 2, 2, HALF, D) + got.reshape(-1, 2, 4, 2, 2, HALF, D).astype(F32)
    one, two = own[:, 0], own[:, 1]
    z, x, y = at
    return [
        pick(one, 3, y),
        pick(two, 2, x),
        swap(low(pick(one, 3, 1 - y)), Y),
        swap(low(pick(two, 2, 1 - x)), X),
    ]


def reduce_rest(at, one, two, got_one, got_two):
    one = one + got_one.astype(F32)
    two = two + got_two.astype(F32)
    z, x, y = at
    return [
        pick(one, 2, x),
        pick(two, 2, y),
        swap(low(pick(one, 2, 1 - x)), X),
        swap(low(pick(two, 2, 1 - y)), Y),
    ]


def reduce_z(at, one, two, got_one, got_two):
    line = jnp.stack([one + got_one.astype(F32), two + got_two.astype(F32)])
    z, x, y = at
    return [pick(line, 2, z)] + [swap(low(pick(line, 2, z ^ k)), k * Z) for k in (1, 2, 3)]


def reduced(line):
    return line[0] + line[1].astype(F32) + line[2].astype(F32) + line[3].astype(F32)


def sum_all(value):
    value = value + swap(value, CORE)
    value = (value + swap(value, Y)) + (swap(value, X) + swap(value, X | Y))
    return (value + swap(value, Z)) + (swap(value, 2 * Z) + swap(value, 3 * Z))


def on_device(
    layer_input, out_grad, matrices, mat_first, mat_second, mat_ema, gains, gain_first, gain_second,
    rel_bias, bias_first, bias_second, bucket_len, item_count, bucket_table,
):
    rest = lax.axis_size("rest")
    shards = jnp.swapaxes(matrices, 1, 2).astype(BF16)
    if rest > 1:
        shards = lax.all_gather(shards, "rest", axis=1, tiled=True)
    shard_f = jnp.concatenate(
        [shards[1, :HALF], shards[2, :HALF], shards[1, HALF:], shards[2, HALF:]]
    )
    where = lax.axis_index("tree").astype(jnp.int32)
    me = where.reshape(1)
    here = (where // Z, where // X % 2, where // Y % 2)
    zero = (jnp.int32(0),) * 3
    gain_one = gains[0:1]
    gain_two = gains[1:2]

    flipped = jnp.concatenate([bucket_table[::-1], jnp.full((1,), -1, jnp.int32)])
    onehot = (flipped[None, :] == jnp.arange(BUCKETS, dtype=jnp.int32)[:, None]).astype(F32)
    table = jnp.dot(rel_bias.T, onehot, precision=lax.Precision.HIGHEST).reshape(PAIRS, 2, SPAN)

    line_w = gather_z(shards[0])
    own_f = lax.all_gather(shard_f, "tree", axis=0, axis_index_groups=[list(range(c, 32, 2)) for c in range(2)])
    halves_w = gather_halves(line_w)
    turned_w = gather_plane(halves_w)
    rest_w = gather_rest(halves_w, turned_w)
    own_w = gathered(halves_w, turned_w, rest_w)
    pieces_w = own_w + gather_core(own_w)
    normed, packed, attn_weight = qkv_call(me, pieces_w, layer_input, gain_one)

    mixed, lse = [], []
    for group in range(GROUPS):
        mixed_g, lse_g = attend_call(bucket_len, item_count, packed, table, group)
        mixed.append(mixed_g)
        lse.append(lse_g)
    middle, second = middle_call(layer_input, mixed, gain_two, attn_weight)
    (own_f,) = tie([own_f], [mixed[1]])
    other_f = swap(own_f, CORE)
    back, hidden_other, other_g = feed_call(other_f, second, out_grad, None, BF16)
    core_f = swap(other_g, CORE)
    (second_b,) = tie([second], [back])
    back, hidden_own, own_g = feed_call(own_f, second_b, out_grad, back, F32)
    (back,) = tie([back], [core_f])
    plane_f = reduce_plane(here, own_g, core_f)
    dmiddle, dmixed, dgain_two, grad_out = middle_back_call(
        back, middle, out_grad, mixed, gain_two, attn_weight
    )

    def attend_back(group, dmixed):
        return attend_back_call(bucket_len, item_count, packed, dmixed, lse[group], table, group)

    grads_0 = attend_back(0, dmixed)
    plane_f = plane_f[:2] + tie(plane_f[2:], [grads_0[0]])
    rest_f = reduce_rest(here, *plane_f)
    (dmixed_1,) = tie([dmixed], plane_f[2:])
    grads_1 = attend_back(1, dmixed_1)
    rest_f = rest_f[:2] + tie(rest_f[2:], [grads_1[0]])
    line_f = reduce_z(here, *rest_f)
    (dmixed_2,) = tie([dmixed], rest_f[2:])
    grads_2 = attend_back(2, dmixed_2)
    dq, dk, dv, dlines = [list(g) for g in zip(grads_0, grads_1, grads_2)]
    mine_w, other_w = qkv_grad_call(me, dq, dk, dv, normed, grad_out)
    (other_w,) = tie([other_w], line_f[1:])
    core_w = swap(other_w, CORE)
    plane_w = reduce_plane(zero, mine_w, core_w)
    (dq[0],) = tie([dq[0]], plane_w[:1])
    input_grad, dgain_one = input_back_call(dq, dk, dv, layer_input, dmiddle, gain_one, attn_weight)
    plane_w = plane_w[:2] + tie(plane_w[2:], [input_grad])
    rest_w = reduce_rest(zero, *plane_w)
    line_w = reduce_z(zero, *rest_w)
    (middle_end,) = tie([middle], rest_w[2:] + line_w[:1])
    layer_output = output_call(middle_end, hidden_own, hidden_other, own_f, other_f)
    line_w = line_w[:1] + tie(line_w[1:], [layer_output])
    sum_f, sum_w = reduced(line_f), reduced(line_w)

    bias_local = jnp.dot(onehot, jnp.concatenate(dlines).reshape(HEADS, SPAN).T, precision=lax.Precision.HIGHEST)
    small = jnp.concatenate([dgain_one.reshape(-1), dgain_two.reshape(-1), bias_local.reshape(-1)])
    small = sum_all(small.reshape(-1, 128)).reshape(-1)
    summed = jnp.concatenate([sum_w.reshape(1, SHARD, D), sum_f.reshape(2, SHARD, D)])
    if rest > 1:
        small = lax.psum(small, "rest")
        summed = lax.psum_scatter(summed, "rest", scatter_dimension=1, tiled=True)
    gain_grad = small[: 2 * D].reshape(2, D)
    bias_grad = small[2 * D :].reshape(BUCKETS, HEADS)
    mat_grad = jnp.swapaxes(summed, 1, 2)
    mat_new, mat_first_new, mat_second_new = adam_update(
        matrices, mat_grad, mat_first, mat_second, RATE
    )
    mat_ema_new = EMA_KEEP * mat_ema + (1.0 - EMA_KEEP) * mat_new
    gain_new, gain_first_new, gain_second_new = adam_update(
        gains, gain_grad, gain_first, gain_second, RATE_SMALL
    )
    bias_new, bias_first_new, bias_second_new = adam_update(
        rel_bias, bias_grad, bias_first, bias_second, RATE_SMALL
    )
    return (
        layer_output, input_grad, mat_grad, mat_new, mat_first_new, mat_second_new, mat_ema_new,
        gain_grad, gain_new, gain_first_new, gain_second_new,
        bias_grad, bias_new, bias_first_new, bias_second_new,
    )


def solution(mesh):
    fine = Mesh(mesh.devices.reshape(32, -1), AXES)
    rows = P(AXES, None)
    columns = P(None, None, AXES)
    return jax.shard_map(
        on_device,
        mesh=fine,
        in_specs=(rows, rows) + (columns,) * 4 + (P(),) * 6 + (P(AXES), P(AXES), P()),
        out_specs=(rows, rows) + (columns,) * 5 + (P(),) * 8,
        check_vma=False,
    )
```

```python
import functools

import jax
import jax.numpy as jnp
from jax import lax
from jax.experimental import pallas as pl
from jax.experimental.pallas import tpu as pltpu
from jax.sharding import Mesh, PartitionSpec as P

D = 768
FF = 3072
HEADS = 12
HD = 64
BUCKETS = 32
ROW = 512
STEP = 10
PAIRS = HEADS // 2
WIDE = 2 * HD
SUB = 128
QB = 256
SPAN = 1024
TOEP = 896

EPS = 1e-06
RATE = 0.05
RATE_SMALL = 0.5
BETA_ONE = 0.9
BETA_TWO = 0.999
ADAM_EPS = 1e-08
DECAY = 0.1
EMA_KEEP = 0.75

F32 = jnp.float32
BF16 = jnp.bfloat16
VMEM_LIMIT = 56 * 1024 * 1024
TILE = 256
SHARD = 96
HALF = 48
PIECES = 8
AHEAD = 3
FIRST = 4

NN = (((1,), (0,)), ((), ()))
NT = (((1,), (1,)), ((), ()))
TN = (((0,), (0,)), ((), ()))


def dot(left, right, dims):
    return lax.dot_general(left, right, dims, preferred_element_type=F32)


def params(**more):
    return pltpu.CompilerParams(vmem_limit_bytes=VMEM_LIMIT, **more)


def cost(flops, moved, special=0):
    return pl.CostEstimate(flops=int(flops), bytes_accessed=int(moved), transcendentals=int(special))


def whole(shape):
    return pl.BlockSpec(shape, lambda *_: (0,) * len(shape))


def tiles(rows, columns):
    return pl.BlockSpec((rows, columns), lambda i, *_: (i, 0))


def piece_block():
    return pl.BlockSpec((4 * HALF, D), lambda i: (0, 0), pipeline_mode=pl.Buffered(1))


def fill_toeplitz(table_ref, toep):
    for h in range(2):
        line = jnp.broadcast_to(table_ref[0, h : h + 1, :], (SUB, SPAN))
        rolled = pltpu.roll(line, SPAN - (SUB - 1), 1, stride=1, stride_axis=0)
        toep[h] = rolled[:, :TOEP]


def head_masks():
    lane = lax.broadcasted_iota(jnp.int32, (1, WIDE), 1)
    return [(lane < HD).astype(BF16), (lane >= HD).astype(BF16)]


def bias_block(toep, h, first, rows, span):
    parts = []
    for t in range(rows // SUB):
        left = ROW - SUB - first - t * SUB
        parts.append(toep[h, :, left : left + span])
    return parts[0] if len(parts) == 1 else jnp.concatenate(parts, axis=0)


def blocks_of(span):
    rows = min(span, QB)
    return [(start, first, rows) for start in range(0, ROW, span) for first in range(0, span, rows)]


def live_rows(live, first, rows):
    return first + lax.broadcasted_iota(jnp.int32, (rows, 1), 0) < live


def attend(pairs, offset, rows, len_ref, count_ref, packed, table_ref, toep, mixed_ref, lse_ref):
    masks = head_masks()
    lane = lax.broadcasted_iota(jnp.int32, (1, WIDE), 1)

    @pl.loop(0, pairs)
    def _(pair):
        fill_toeplitz(table_ref.at[pl.ds(pair + offset, 1)], toep)

        @pl.loop(0, rows)
        def _(row):
            length = len_ref[row]
            live = length * count_ref[row]
            at = pl.ds(pl.multiple_of(row * ROW, ROW), ROW)
            cols = columns_of(pair, (0, packed.shape[1] // 3 // WIDE, packed.shape[1] // 3 * 2 // WIDE))
            to = columns_of(pair, (offset,))[0]

            def body(span):
                q_all, k_all, v_all = (packed[at, c] for c in cols)
                stats_all = lse_ref[at, :]
                spots = blocks_of(span)
                keys = [k_all * m for m in masks]
                vals = [v_all * m for m in masks]
                both = [(spot, h) for spot in spots for h in range(2)]
                scores = [
                    dot(q_all[start + first : start + first + rows], keys[h][start : start + span], NT)
                    + bias_block(toep, h, first, rows, span)
                    for (start, first, rows), h in both
                ]
                tops = [jnp.max(s, axis=-1, keepdims=True) for s in scores]
                exps = [jnp.exp(s - top) for s, top in zip(scores, tops)]
                totals = [jnp.sum(e, axis=-1, keepdims=True) for e in exps]
                probs = [(e * (1.0 / total)).astype(BF16) for e, total in zip(exps, totals)]
                outs_h = [
                    dot(p, vals[h][start : start + span], NN) for p, ((start, first, rows), h) in zip(probs, both)
                ]
                mixed_parts, stats_parts = [], []
                for i, (start, first, rows) in enumerate(spots):
                    mixed = outs_h[2 * i] + outs_h[2 * i + 1]
                    stats = stats_all[start + first : start + first + rows]
                    for h in range(2):
                        head = (pair + offset) * 2 + h
                        stats = jnp.where(lane == head, tops[2 * i + h] + jnp.log(totals[2 * i + h]), stats)
                    if span < ROW:
                        mixed = jnp.where(live_rows(live, start + first, rows), mixed, 0.0)
                    mixed_parts.append(mixed.astype(BF16))
                    stats_parts.append(stats)
                mixed_ref[at, to] = jnp.concatenate(mixed_parts, axis=0)
                lse_ref[at, :] = jnp.concatenate(stats_parts, axis=0)

            for span in (ROW, ROW // 2, ROW // 4):
                pl.when(length == span)(functools.partial(body, span))


def first_forward_kernel(me_ref, len_ref, count_ref, *refs):
    pieces = refs[:PIECES]
    (
        x_ref, gain_ref, table_ref, normed_out, packed_out, weight_out, lse_ref, mixed_ref,
        weight, normed, packed, toep, in_sem, out_sem,
    ) = refs[PIECES:]
    copies = []
    for i, ref in enumerate(pieces):
        core, half, far = i // 4, i // 2 % 2, i % 2
        for j in range(8):
            near, z = j // 4, j % 4
            plane = near * 2 + far if half == 0 else far * 2 + near
            owner = me_ref[0] ^ (z * 8 + plane * 2 + core)
            row = pl.multiple_of(owner * SHARD + half * HALF, 16)
            copies.append(
                pltpu.make_async_copy(ref.at[pl.ds(j * HALF, HALF)], weight.at[pl.ds(row, HALF)], in_sem)
            )
    for copy in copies:
        copy.start()

    tokens = x_ref.shape[0]

    @pl.loop(0, tokens // TILE)
    def _(tile):
        at = pl.ds(pl.multiple_of(tile * TILE, TILE), TILE)
        x = x_ref[at, :].astype(F32)
        scale = lax.rsqrt(jnp.mean(x * x, axis=-1, keepdims=True) + EPS)
        normed[at, :] = (x * scale * gain_ref[0:1, :]).astype(BF16)

    for copy in copies:
        copy.wait()
    outs = [
        pltpu.make_async_copy(weight, weight_out, out_sem.at[0]),
        pltpu.make_async_copy(normed, normed_out, out_sem.at[1]),
        pltpu.make_async_copy(packed, packed_out, out_sem.at[2]),
    ]
    outs[0].start()
    outs[1].start()

    @pl.loop(0, tokens // TILE)
    def _(tile):
        at = pl.ds(pl.multiple_of(tile * TILE, TILE), TILE)
        for part in range(3):
            cols = slice(part * D, (part + 1) * D)
            packed[at, cols] = dot(normed[at, :], weight[cols, :], NT).astype(BF16)

    outs[2].start()
    lse_ref[...] = jnp.zeros_like(lse_ref)
    attend(AHEAD, 0, tokens // ROW, len_ref, count_ref, packed, table_ref, toep, mixed_ref, lse_ref)
    for copy in outs:
        copy.wait()


def first_forward_call(me, lengths, counts, pieces, x, gains, table):
    tokens = x.shape[0]
    anywhere = pl.BlockSpec(memory_space=pl.ANY)
    inside = pl.BlockSpec(memory_space=pltpu.VMEM)
    return pl.pallas_call(
        first_forward_kernel,
        grid_spec=pltpu.PrefetchScalarGridSpec(
            num_scalar_prefetch=3,
            grid=(),
            in_specs=[anywhere] * PIECES + [inside] * 3,
            out_specs=[anywhere] * 3 + [inside] * 2,
            scratch_shapes=[
                pltpu.VMEM((4 * D, D), BF16),
                pltpu.VMEM((tokens, D), BF16),
                pltpu.VMEM((tokens, 3 * D), BF16),
                pltpu.VMEM((2, SUB, TOEP), F32),
                pltpu.SemaphoreType.DMA,
                pltpu.SemaphoreType.DMA((3,)),
            ],
        ),
        out_shape=[
            jax.ShapeDtypeStruct((tokens, D), BF16),
            jax.ShapeDtypeStruct((tokens, 3 * D), BF16),
            jax.ShapeDtypeStruct((4 * D, D), BF16),
            jax.ShapeDtypeStruct((tokens, WIDE), F32),
            jax.ShapeDtypeStruct((tokens, AHEAD * WIDE), BF16),
        ],
        compiler_params=params(),
        cost_estimate=cost(12e9, 30e6, 4e6),
        name="first_forward",
    )(me, lengths, counts, *pieces, x, gains, table)


def last_forward_kernel(
    len_ref, count_ref, x_ref, gain_ref, table_ref, first_ref, stats_ref, weight_in, packed_in,
    lse_ref, mixed_ref, middle_out, second_out,
    weight, packed, middle_s, second_s, toep, in_sems, out_sems,
):
    tokens = x_ref.shape[0]
    start = AHEAD * WIDE
    width = D - start
    copies = [pltpu.make_async_copy(weight_in.at[pl.ds(3 * D, D)], weight, in_sems.at[0])]
    for part in range(3):
        copies.append(
            pltpu.make_async_copy(
                packed_in.at[:, pl.ds(part * D + start, width)], packed.at[:, pl.ds(part * width, width)], in_sems.at[1 + part]
            )
        )
    for copy in copies:
        copy.start()
    lse_ref[...] = stats_ref[...]
    mixed_ref[:, :start] = first_ref[...]
    for copy in copies[1:]:
        copy.wait()
    attend(PAIRS - AHEAD, AHEAD, tokens // ROW, len_ref, count_ref, packed, table_ref, toep, mixed_ref, lse_ref)
    copies[0].wait()
    outs = []
    for tile in range(tokens // TILE):
        at = pl.ds(tile * TILE, TILE)
        middle = x_ref[at, :].astype(F32) + dot(mixed_ref[at, :], weight[...], NT)
        middle_s[at, :] = middle
        scale = lax.rsqrt(jnp.mean(middle * middle, axis=-1, keepdims=True) + EPS)
        second_s[at, :] = (middle * scale * gain_ref[1:2, :]).astype(BF16)
        for i, (src, dst) in enumerate(((middle_s, middle_out), (second_s, second_out))):
            copy = pltpu.make_async_copy(src.at[at], dst.at[at], out_sems.at[2 * tile + i])
            copy.start()
            outs.append(copy)
    for copy in outs:
        copy.wait()


def last_forward_call(lengths, counts, x, gains, table, first, stats, weight, packed):
    tokens = x.shape[0]
    anywhere = pl.BlockSpec(memory_space=pl.ANY)
    inside = pl.BlockSpec(memory_space=pltpu.VMEM)
    flat = jax.ShapeDtypeStruct((tokens, D), BF16)
    return pl.pallas_call(
        last_forward_kernel,
        grid_spec=pltpu.PrefetchScalarGridSpec(
            num_scalar_prefetch=2,
            grid=(),
            in_specs=[inside] * 5 + [anywhere] * 2,
            out_specs=[inside] * 2 + [anywhere] * 2,
            scratch_shapes=[
                pltpu.VMEM((D, D), BF16),
                pltpu.VMEM((tokens, 3 * (PAIRS - AHEAD) * WIDE), BF16),
                pltpu.VMEM((tokens, D), F32),
                pltpu.VMEM((tokens, D), BF16),
                pltpu.VMEM((2, SUB, TOEP), F32),
                pltpu.SemaphoreType.DMA((4,)),
                pltpu.SemaphoreType.DMA((2 * tokens // TILE,)),
            ],
        ),
        out_shape=[
            jax.ShapeDtypeStruct((tokens, WIDE), F32),
            flat,
            jax.ShapeDtypeStruct((tokens, D), F32),
            flat,
        ],
        compiler_params=params(),
        cost_estimate=cost(8e9, 20e6, 4e6),
        name="last_forward",
    )(lengths, counts, x, gains, table, first, stats, weight, packed)


def fold_diagonals(grid):
    height = SUB
    total = jnp.concatenate([grid, jnp.zeros((SUB, SPAN - TOEP), F32)], axis=1)
    while height > 8:
        height //= 2
        total = pltpu.roll(total[:height], height, 1) + total[height:]
    line = total[7:8]
    for r in range(7):
        line = line + pltpu.roll(total, 7 - r, 1)[r : r + 1]
    return line


def attend_back(
    pairs, offset, me_rows, len_ref, count_ref, cols_of, packed, dmixed, lse_ref, table_ref, toep, diag, out_ref, dbias_ref
):
    masks = head_masks()
    lane = lax.broadcasted_iota(jnp.int32, (1, WIDE), 1)

    @pl.loop(0, pairs)
    def _(pair):
        fill_toeplitz(table_ref.at[pl.ds(pair + offset, 1)], toep)
        diag[...] = jnp.zeros_like(diag)

        @pl.loop(0, me_rows)
        def _(row):
            length = len_ref[row]
            live = length * count_ref[row]
            at = pl.ds(pl.multiple_of(row * ROW, ROW), ROW)
            cols = cols_of(pair)

            def body(span):
                q_all, k_all, v_all = (packed[at, c] for c in cols[:3])
                do_all = dmixed[at, cols[3]]
                if span < ROW:
                    do_all = jnp.where(live_rows(live, 0, ROW), do_all.astype(F32), 0.0).astype(BF16)
                stats = lse_ref[at, :]
                spots = blocks_of(span)
                queries, keys, vals, dos = ([a * m for m in masks] for a in (q_all, k_all, v_all, do_all))
                lses = [
                    jnp.sum(jnp.where(lane == (pair + offset) * 2 + h, stats, 0.0), axis=-1, keepdims=True) for h in range(2)
                ]
                both = [(spot, h) for spot in spots for h in range(2)]

                def rows_of(value, spot):
                    return value[spot[0] + spot[1] : spot[0] + spot[1] + spot[2]]

                def keys_of(value, spot):
                    return value[spot[0] : spot[0] + span]

                scores = [
                    dot(rows_of(q_all, spot), keys_of(keys[h], spot), NT) + bias_block(toep, h, spot[1], spot[2], span)
                    for spot, h in both
                ]
                dps = [dot(rows_of(do_all, spot), keys_of(vals[h], spot), NT) for spot, h in both]
                probs = [jnp.exp(s - rows_of(lses[h], spot)) for s, (spot, h) in zip(scores, both)]
                parts = [p * dp for p, dp in zip(probs, dps)]
                sums = [jnp.sum(t, axis=-1, keepdims=True) for t in parts]
                dss = [t - p * total for t, p, total in zip(parts, probs, sums)]
                for ds, (spot, h) in zip(dss, both):
                    for sub in range(spot[2] // SUB):
                        left = ROW - SUB - spot[1] - sub * SUB
                        diag[h, :, left : left + span] += ds[sub * SUB : (sub + 1) * SUB]
                lows = [ds.astype(BF16) for ds in dss]
                plows = [p.astype(BF16) for p in probs]
                dqs = [dot(low, keys_of(keys[h], spot), NN) for low, (spot, h) in zip(lows, both)]
                dks = [dot(low, rows_of(queries[h], spot), TN) for low, (spot, h) in zip(lows, both)]
                dvs = [dot(low, rows_of(dos[h], spot), TN) for low, (spot, h) in zip(plows, both)]
                dq = jnp.concatenate([dqs[2 * i] + dqs[2 * i + 1] for i in range(len(spots))], axis=0)
                each = len(both) * span // ROW
                dk, dv = (
                    jnp.concatenate([sum(d[i + 1 : i + each], d[i]) for i in range(0, len(both), each)], axis=0)
                    for d in (dks, dvs)
                )
                for part, value in enumerate((dq, dk, dv)):
                    to = pl.ds(pl.multiple_of(pair * WIDE + part * pairs * WIDE, WIDE), WIDE)
                    out_ref[at, to] = value.astype(BF16)

            for span in (ROW, ROW // 2, ROW // 4):
                pl.when(length == span)(functools.partial(body, span))

        for h in range(2):
            dbias_ref[pl.ds(pair, 1), h : h + 1, :] = fold_diagonals(diag[h]).reshape(1, 1, SPAN)


def columns_of(pair, widths):
    return [pl.ds(pl.multiple_of((pair + w) * WIDE, WIDE), WIDE) for w in widths]


def first_back_kernel(
    len_ref, count_ref, mixed_ref, gain_ref, lse_ref, table_ref,
    part_in, got_in, middle_in, grad_in, weight_in, packed_in,
    dgain_ref, out_ref, dbias_ref, dmiddle_out, dmixed_out, dweight_out,
    part_s, got_s, middle_s, grad_s, dmixed, dweight, weight, packed, lows, toep, diag, in_sems, sems, out_sems,
):
    tokens = mixed_ref.shape[0]
    count = tokens // TILE
    width = FIRST * WIDE
    first = pltpu.make_async_copy(weight_in.at[pl.ds(3 * D, D)], weight, sems.at[0])
    first.start()
    ins = []
    for tile in range(count):
        at = pl.ds(tile * TILE, TILE)
        for i, (src, dst) in enumerate(((part_in, part_s), (got_in, got_s), (middle_in, middle_s), (grad_in, grad_s))):
            copy = pltpu.make_async_copy(src.at[at], dst.at[at], in_sems.at[4 * tile + i])
            copy.start()
            ins.append(copy)
    later = []
    for part in range(3):
        copy = pltpu.make_async_copy(
            packed_in.at[:, pl.ds(part * D, width)], packed.at[:, pl.ds(part * width, width)], sems.at[1 + part]
        )
        copy.start()
        later.append(copy)
    first.wait()
    outs = []
    dgain = jnp.zeros((1, D), F32)
    for tile in range(count):
        at = pl.ds(tile * TILE, TILE)
        for copy in ins[4 * tile : 4 * tile + 4]:
            copy.wait()
        db = part_s[at, :] + got_s[at, :]
        middle = middle_s[at, :]
        scale = lax.rsqrt(jnp.mean(middle * middle, axis=-1, keepdims=True) + EPS)
        dn = db * gain_ref[1:2, :]
        inner = jnp.mean(dn * middle, axis=-1, keepdims=True)
        dmiddle = grad_s[at, :].astype(F32) + scale * dn - middle * (scale * scale * scale * inner)
        part_s[at, :] = dmiddle
        copy = pltpu.make_async_copy(part_s.at[at], dmiddle_out.at[at], out_sems.at[tile])
        copy.start()
        outs.append(copy)
        low = dmiddle.astype(BF16)
        lows[at, :] = low
        dmixed[at, :] = dot(low, weight[...], NN).astype(BF16)
        dgain += jnp.sum(db * middle * scale, axis=0, keepdims=True)
    dgain_ref[...] = dgain
    copy = pltpu.make_async_copy(dmixed, dmixed_out, out_sems.at[count])
    copy.start()
    outs.append(copy)
    dweight[...] = dot(lows[...], mixed_ref[...], TN)
    copy = pltpu.make_async_copy(dweight, dweight_out, out_sems.at[count + 1])
    copy.start()
    outs.append(copy)
    for copy in later:
        copy.wait()

    def cols_of(pair):
        return columns_of(pair, (0, FIRST, 2 * FIRST, 0))

    attend_back(
        FIRST, 0, tokens // ROW, len_ref, count_ref, cols_of, packed, dmixed, lse_ref, table_ref, toep, diag, out_ref, dbias_ref
    )
    for copy in outs:
        copy.wait()


def first_back_call(lengths, counts, part, got, middle, out_grad, mixed, gains, lse, table, weight, packed):
    tokens = part.shape[0]
    anywhere = pl.BlockSpec(memory_space=pl.ANY)
    inside = pl.BlockSpec(memory_space=pltpu.VMEM)
    width = 3 * FIRST * WIDE
    count = tokens // TILE
    return pl.pallas_call(
        first_back_kernel,
        grid_spec=pltpu.PrefetchScalarGridSpec(
            num_scalar_prefetch=2,
            grid=(),
            in_specs=[inside] * 4 + [anywhere] * 6,
            out_specs=[inside] * 3 + [anywhere] * 3,
            scratch_shapes=[pltpu.VMEM((tokens, D), F32)] * 3
            + [
                pltpu.VMEM((tokens, D), BF16),
                pltpu.VMEM((tokens, D), BF16),
                pltpu.VMEM((D, D), F32),
                pltpu.VMEM((D, D), BF16),
                pltpu.VMEM((tokens, width), BF16),
                pltpu.VMEM((tokens, D), BF16),
                pltpu.VMEM((2, SUB, TOEP), F32),
                pltpu.VMEM((2, SUB, TOEP), F32),
                pltpu.SemaphoreType.DMA((4 * count,)),
                pltpu.SemaphoreType.DMA((4,)),
                pltpu.SemaphoreType.DMA((count + 2,)),
            ],
        ),
        out_shape=[
            jax.ShapeDtypeStruct((1, D), F32),
            jax.ShapeDtypeStruct((tokens, width), BF16),
            jax.ShapeDtypeStruct((FIRST, 2, SPAN), F32),
            jax.ShapeDtypeStruct((tokens, D), F32),
            jax.ShapeDtypeStruct((tokens, D), BF16),
            jax.ShapeDtypeStruct((D, D), F32),
        ],
        compiler_params=params(),
        cost_estimate=cost(15e9, 30e6, 7e6),
        name="first_back",
    )(lengths, counts, mixed, gains, lse, table, part, got, middle, out_grad, weight, packed)


def last_back_kernel(
    me_ref, len_ref, count_ref, lse_ref, table_ref, normed_in, first_in, dout_in, packed_in, dmixed_in,
    out_ref, dbias_ref, own_out, other_out,
    packed, dmixed, normed, first, own, other, total, toep, diag, sems, out_sems,
):
    tokens = normed.shape[0]
    pairs = PAIRS - FIRST
    width = pairs * WIDE
    start = FIRST * WIDE
    copies = [pltpu.make_async_copy(dmixed_in.at[:, pl.ds(start, width)], dmixed, sems.at[0])]
    for part in range(3):
        copies.append(
            pltpu.make_async_copy(
                packed_in.at[:, pl.ds(part * D + start, width)], packed.at[:, pl.ds(part * width, width)], sems.at[1 + part]
            )
        )
    later = [
        pltpu.make_async_copy(normed_in, normed, sems.at[4]),
        pltpu.make_async_copy(first_in, first, sems.at[5]),
        pltpu.make_async_copy(dout_in, total.at[pl.ds(3 * D, D)], sems.at[6]),
    ]
    for copy in copies + later:
        copy.start()
    for copy in copies:
        copy.wait()

    def cols_of(pair):
        return columns_of(pair, (0, pairs, 2 * pairs, 0))

    attend_back(
        pairs, FIRST, tokens // ROW, len_ref, count_ref, cols_of, packed, dmixed, lse_ref, table_ref, toep, diag, out_ref, dbias_ref
    )
    for copy in later:
        copy.wait()
    for part in range(3):
        at = part * D
        total[at : at + start] = dot(first[:, part * start : (part + 1) * start], normed[...], TN)
        total[at + start : at + D] = dot(out_ref[:, part * width : (part + 1) * width], normed[...], TN)
    for core, kept, out in ((1, other, other_out), (0, own, own_out)):

        @pl.loop(0, 32)
        def _(i):
            half, plane, z = i // 16, i // 4 % 4, i % 4
            owner = me_ref[0] ^ (z * 8 + plane * 2 + core)
            row = pl.multiple_of(owner * SHARD + half * HALF, 16)
            to = pl.multiple_of(i * HALF, 16)
            kept[pl.ds(to, HALF), :] = total[pl.ds(row, HALF), :].astype(kept.dtype)

        pltpu.make_async_copy(kept, out, out_sems.at[core]).start()
    for core, kept, out in ((1, other, other_out), (0, own, own_out)):
        pltpu.make_async_copy(kept, out, out_sems.at[core]).wait()


def last_back_call(me, lengths, counts, lse, table, normed, first, grad_out, packed, dmixed):
    tokens = normed.shape[0]
    anywhere = pl.BlockSpec(memory_space=pl.ANY)
    inside = pl.BlockSpec(memory_space=pltpu.VMEM)
    width = (PAIRS - FIRST) * WIDE
    return pl.pallas_call(
        last_back_kernel,
        grid_spec=pltpu.PrefetchScalarGridSpec(
            num_scalar_prefetch=3,
            grid=(),
            in_specs=[inside] * 2 + [anywhere] * 5,
            out_specs=[inside] * 2 + [anywhere] * 2,
            scratch_shapes=[
                pltpu.VMEM((tokens, 3 * width), BF16),
                pltpu.VMEM((tokens, width), BF16),
                pltpu.VMEM((tokens, D), BF16),
                pltpu.VMEM((tokens, 3 * FIRST * WIDE), BF16),
                pltpu.VMEM((2 * D, D), F32),
                pltpu.VMEM((2 * D, D), BF16),
                pltpu.VMEM((4 * D, D), F32),
                pltpu.VMEM((2, SUB, TOEP), F32),
                pltpu.VMEM((2, SUB, TOEP), F32),
                pltpu.SemaphoreType.DMA((7,)),
                pltpu.SemaphoreType.DMA((2,)),
            ],
        ),
        out_shape=[
            jax.ShapeDtypeStruct((tokens, 3 * width), BF16),
            jax.ShapeDtypeStruct((PAIRS - FIRST, 2, SPAN), F32),
            jax.ShapeDtypeStruct((2 * D, D), F32),
            jax.ShapeDtypeStruct((2 * D, D), BF16),
        ],
        compiler_params=params(),
        cost_estimate=cost(10e9, 30e6, 4e6),
        name="last_back",
    )(me, lengths, counts, lse, table, normed, first, grad_out, packed, dmixed)


def feed_tile(second, grad, up, down):
    u = dot(second, up, NT)
    square = u * u
    t = jnp.tanh(0.7978845608 * u * (1.0 + 0.044715 * square))
    plus = 0.5 * (1.0 + t)
    slope = plus + (0.5 * 0.7978845608) * u * (1.0 - t * t) * (1.0 + 3 * 0.044715 * square)
    dh = dot(grad, down, NT).astype(BF16).astype(F32)
    return (u * plus).astype(BF16), (dh * slope).astype(BF16)


def weights_of(refs):
    return [jnp.concatenate([ref[...] for ref in refs[i : i + 4]], axis=0) for i in (0, 4)]


def feed_kernel(parts, *refs):
    up, down = weights_of(refs[:8])
    second_ref, grad_ref, *refs, back_ref, hidden_ref, dpre_ref = refs[8:]
    hidden, du = feed_tile(second_ref[...], grad_ref[...], up, down)
    hidden_ref[...] = hidden
    dpre_ref[...] = du
    back = dot(du, up, NN)
    back_ref[...] = back + refs[0][...] if parts else back


def feed_call(weights, second, out_grad, start=None):
    tokens = second.shape[0]
    flat = tiles(TILE, D)
    low_flat = jax.ShapeDtypeStruct((tokens, D), BF16)
    more = [] if start is None else [start]
    return pl.pallas_call(
        functools.partial(feed_kernel, len(more)),
        grid=(tokens // TILE,),
        in_specs=[piece_block()] * 8 + [flat, flat] + [flat] * len(more),
        out_specs=[flat, flat, flat],
        out_shape=[jax.ShapeDtypeStruct((tokens, D), F32), low_flat, low_flat],
        compiler_params=params(),
        cost_estimate=cost(6 * tokens * D * D, 15e6, tokens * D),
        name="feed",
    )(*weights, second, out_grad, *more)


def feed_sum_kernel(parts, *refs):
    weights = refs[:8]
    second_ref, grad_ref, second_other, grad_other, hidden_other, dpre_other, *refs = refs[8:]
    back_ref, hidden_ref, out_ref, dpre = refs[-4:]
    step = pl.program_id(0)
    count = second_ref.shape[0] // TILE

    @pl.when(step < count)
    def _():
        at = pl.ds(pl.multiple_of(step * TILE, TILE), TILE)
        up, down = weights_of(weights)
        hidden, du = feed_tile(second_ref[at, :], grad_ref[at, :], up, down)
        hidden_ref[at, :] = hidden
        dpre[at, :] = du
        back = dot(du, up, NN)
        back_ref[...] = back + refs[0][...] if parts else back

    @pl.when(step == count)
    def _():
        out_ref[0] = dot(dpre[...], second_ref[...], TN) + dot(dpre_other[...], second_other[...], TN)

    @pl.when(step == count + 1)
    def _():
        out_ref[0] = dot(hidden_ref[...], grad_ref[...], TN) + dot(hidden_other[...], grad_other[...], TN)


def feed_sum_call(weights, second, out_grad, second_other, grad_other, hidden_other, dpre_other, start=None):
    tokens = second.shape[0]
    count = tokens // TILE
    flat = pl.BlockSpec((tokens, D), lambda i: (0, 0), pipeline_mode=pl.Buffered(1))
    tile = pl.BlockSpec((TILE, D), lambda i: (jnp.minimum(i, count - 1), 0))
    more = [] if start is None else [start]
    return pl.pallas_call(
        functools.partial(feed_sum_kernel, len(more)),
        grid=(count + 2,),
        in_specs=[piece_block()] * 8 + [flat] * 6 + [tile] * len(more),
        out_specs=[tile, whole((tokens, D)), pl.BlockSpec((1, D, D), lambda i: (jnp.maximum(i - count, 0), 0, 0))],
        out_shape=[
            jax.ShapeDtypeStruct((tokens, D), F32),
            jax.ShapeDtypeStruct((tokens, D), BF16),
            jax.ShapeDtypeStruct((2, D, D), F32),
        ],
        scratch_shapes=[pltpu.VMEM((tokens, D), BF16)],
        compiler_params=params(),
        cost_estimate=cost(14 * tokens * D * D, 30e6, tokens * D),
        name="feed_sum",
    )(*weights, second, out_grad, second_other, grad_other, hidden_other, dpre_other, *more)


def output_part(refs):
    total = None
    for half, hidden in enumerate(refs[:2]):
        down = jnp.concatenate([ref[...] for ref in refs[2 + 4 * half : 6 + 4 * half]], axis=0)
        part = dot(hidden[...], down, NN)
        total = part if total is None else total + part
    return total


def output_other_kernel(*refs):
    refs[-1][...] = output_part(refs)


def output_kernel(*refs):
    middle_ref, got_ref, out_ref = refs[10:]
    out_ref[...] = (middle_ref[...] + (output_part(refs) + got_ref[...])).astype(BF16)


def output_call(hiddens, weights, more=()):
    tokens = hiddens[0].shape[0]
    return pl.pallas_call(
        output_kernel if more else output_other_kernel,
        grid=(tokens // TILE,),
        in_specs=[tiles(TILE, D)] * 2 + [piece_block()] * 8 + [tiles(TILE, D)] * len(more),
        out_specs=tiles(TILE, D),
        out_shape=jax.ShapeDtypeStruct((tokens, D), BF16 if more else F32),
        compiler_params=params(),
        cost_estimate=cost(4 * tokens * D * D, 12e6),
        name="output",
    )(*hiddens, *weights, *more)


def input_back_kernel(first_ref, last_ref, x_ref, dmiddle_ref, gain_ref, weight_ref, dx_ref, dgain_ref):
    step = pl.program_id(0)
    da = jnp.zeros(dx_ref.shape, F32)
    cut = FIRST * WIDE
    for part in range(3):
        da += dot(first_ref[:, part * cut : (part + 1) * cut], weight_ref[part * D : part * D + cut, :], NN)
        rest = D - cut
        da += dot(last_ref[:, part * rest : (part + 1) * rest], weight_ref[part * D + cut : (part + 1) * D, :], NN)
    x = x_ref[...].astype(F32)
    scale = lax.rsqrt(jnp.mean(x * x, axis=-1, keepdims=True) + EPS)
    dm = da * gain_ref[0:1, :]
    inner = jnp.mean(dm * x, axis=-1, keepdims=True)
    dx_ref[...] = dmiddle_ref[...] + scale * dm - x * (scale * scale * scale * inner)
    dgain = jnp.sum(da * x * scale, axis=0, keepdims=True)

    @pl.when(step == 0)
    def _():
        dgain_ref[...] = dgain

    @pl.when(step > 0)
    def _():
        dgain_ref[...] += dgain


def input_back_call(first, last, x, dmiddle, gains, weight):
    tokens = x.shape[0]
    return pl.pallas_call(
        input_back_kernel,
        grid=(tokens // TILE,),
        in_specs=[
            tiles(TILE, first.shape[1]),
            tiles(TILE, last.shape[1]),
            tiles(TILE, D),
            tiles(TILE, D),
            whole((2, D)),
            whole((3 * D, D)),
        ],
        out_specs=[tiles(TILE, D), whole((1, D))],
        out_shape=[jax.ShapeDtypeStruct((tokens, D), F32), jax.ShapeDtypeStruct((1, D), F32)],
        compiler_params=params(),
        cost_estimate=cost(2 * tokens * D * 3 * D, 18e6),
        name="input_back",
    )(first, last, x, dmiddle, gains, weight)


def adam_update(param, grad, first, second, rate):
    first_new = BETA_ONE * first + (1.0 - BETA_ONE) * grad
    second_new = BETA_TWO * second + (1.0 - BETA_TWO) * grad * grad
    first_hat = first_new / (1.0 - BETA_ONE**STEP)
    second_hat = second_new / (1.0 - BETA_TWO**STEP)
    param_new = param - rate * (first_hat / (jnp.sqrt(second_hat) + ADAM_EPS) + DECAY * param)
    return (param_new, first_new, second_new)


AXES = ("tree", "rest")
CORE, Y, X, Z = 1, 2, 4, 8


def swap(value, bits):
    return lax.ppermute(value, "tree", [(i, i ^ bits) for i in range(32)])


def tie(values, after):
    return list(lax.optimization_barrier(tuple(values) + tuple(after))[: len(values)])


def gather_z(shard):
    return [shard] + [swap(shard, k * Z) for k in (1, 2, 3)]


def gather_halves(line, first=0):
    return [jnp.concatenate([p[i : i + HALF] for p in line]) for i in (first, first + HALF)]


def gather_plane(halves):
    return [swap(halves[0], X), swap(halves[1], Y)]


def gather_rest(halves, turned):
    return [swap(halves[0], Y), swap(turned[0], Y), swap(halves[1], X), swap(turned[1], X)]


def gathered(halves, turned, rest):
    return [halves[0], rest[0], turned[0], rest[1], halves[1], turned[1], rest[2], rest[3]]


def gather_core(pieces):
    return [swap(p, CORE) for p in pieces]


def low(value):
    return value.astype(BF16)


def added(value, got):
    return value if got is None else value + got.astype(F32)


def reduce_plane(own, got=None):
    shape = (2, 2, 2, 4, HALF, D)
    own = own.reshape(shape)
    got = None if got is None else got.reshape(shape)

    def part(*at):
        return added(own[at], None if got is None else got[at])

    every = slice(None)
    return [part(0, every, 0), part(1, 0)], [low(part(0, every, 1)), low(part(1, 1))]


def swap_plane(sends):
    return [swap(sends[0], Y), swap(sends[1], X)]


def reduce_rest(keep, got):
    parts = [[added(k[i], g[i]) for k, g in zip(keep, got)] for i in range(2)]
    return parts[0], [low(part) for part in parts[1]]


def swap_rest(sends):
    return [swap(sends[0], X), swap(sends[1], Y)]


def line_kernel(one_ref, two_ref, got_one, got_two, *outs):
    for k, out in enumerate(outs):
        out[:HALF] = (one_ref[k] + got_one[k].astype(F32)).astype(out.dtype)
        out[HALF:] = (two_ref[k] + got_two[k].astype(F32)).astype(out.dtype)


def reduce_line(keep, got):
    shape = (SHARD, D)
    outs = pl.pallas_call(
        line_kernel,
        out_shape=[jax.ShapeDtypeStruct(shape, F32)] + [jax.ShapeDtypeStruct(shape, BF16)] * 3,
        compiler_params=params(),
        cost_estimate=cost(1e6, 6e6),
        name="line",
    )(*keep, *got)
    return outs[0], list(outs[1:])


def swap_line(sends):
    return [swap(send, k * Z) for k, send in zip((1, 2, 3), sends)]


def reduced(keep, got):
    return keep + got[0].astype(F32) + got[1].astype(F32) + got[2].astype(F32)


def on_device(
    layer_input, out_grad, matrices, mat_first, mat_second, mat_ema, gains, gain_first, gain_second,
    rel_bias, bias_first, bias_second, bucket_len, item_count, bucket_table,
):
    rest = lax.axis_size("rest")
    shards = jnp.swapaxes(matrices, 1, 2).astype(BF16)
    if rest > 1:
        shards = lax.all_gather(shards, "rest", axis=1, tiled=True)
    shard_f = jnp.concatenate(
        [shards[1, :HALF], shards[2, :HALF], shards[1, HALF:], shards[2, HALF:]]
    )
    where = lax.axis_index("tree").astype(jnp.int32)
    me = where.reshape(1)
    flipped = jnp.concatenate([bucket_table[::-1], jnp.full((1,), -1, jnp.int32)])
    onehot = (flipped[None, :] == jnp.arange(BUCKETS, dtype=jnp.int32)[:, None]).astype(F32)
    table = jnp.dot(rel_bias.T, onehot, precision=lax.Precision.HIGHEST).reshape(PAIRS, 2, SPAN)

    line_w = gather_z(shards[0])
    halves_w = gather_halves(line_w)
    turned_w = gather_plane(halves_w)
    (shard_f,) = tie([shard_f], halves_w)
    line_f = gather_z(shard_f)
    near_w = [jnp.concatenate([half, turned]) for half, turned in zip(halves_w, turned_w)]
    far_w = [swap(near_w[0], Y), swap(near_w[1], X)]
    own_w = [near_w[0], far_w[0], near_w[1], far_w[1]]
    (own_w[0], own_w[2]) = tie(near_w, far_w)
    other_w = gather_core(own_w)
    halves_a = tie(gather_halves(line_f, 0), far_w)
    halves_b = tie(gather_halves(line_f, 2 * HALF), far_w)
    turned_a = gather_plane(halves_a)
    turned_b = gather_plane(halves_b)
    (late_input,) = tie([layer_input], halves_a + halves_b)
    normed, packed, attn_weight, stats, mixed_first = first_forward_call(
        me, bucket_len, item_count, own_w + other_w, late_input, gains, table
    )
    (grad_send,) = tie([out_grad], [normed])
    grad_other = swap(grad_send, CORE)
    turned_a = tie(turned_a, [normed])
    turned_b = tie(turned_b, [normed])
    rest_a = gather_rest(halves_a, turned_a)
    (mixed_first,) = tie([mixed_first], turned_a + turned_b)
    lse, mixed, middle, second = last_forward_call(
        bucket_len, item_count, layer_input, gains, table, mixed_first, stats, attn_weight, packed
    )

    rest_a = tie(rest_a, [lse])
    own_a = gathered(halves_a, turned_a, rest_a)
    halves_b = tie(halves_b, rest_a)
    rest_b = gather_rest(halves_b, turned_b)
    (second,) = tie([second], rest_a)
    second_other = swap(second, CORE)
    back_other, hidden_oa, dpre_oa = feed_call(own_a, second_other, grad_other)
    (second_a,) = tie([second], [dpre_oa])
    back, hidden_a, grad_a = feed_sum_call(own_a, second_a, out_grad, second_other, grad_other, hidden_oa, dpre_oa)
    rest_b = tie(rest_b, [grad_a])
    own_b = gathered(halves_b, turned_b, rest_b)
    keep_a, send_a = reduce_plane(grad_a)
    (second_other_b,) = tie([second_other], send_a + rest_b)
    got_a = swap_plane(send_a)
    back_other, hidden_ob, dpre_ob = feed_call(own_b, second_other_b, grad_other, back_other)
    back_got = swap(back_other, CORE)
    (second_b,) = tie([second], [dpre_ob])
    back, hidden_b, grad_b = feed_sum_call(
        own_b, second_b, out_grad, second_other_b, grad_other, hidden_ob, dpre_ob, back
    )

    got_a = tie(got_a, [grad_b])
    keep_a, send_a = reduce_rest(keep_a, got_a)
    got_a = swap_rest(send_a)
    keep_b, send_b = reduce_plane(grad_b)
    got_b = swap_plane(send_b)
    (back,) = tie([back], send_a + send_b + [back_got])
    dgain_two, first_d, lines_a, dmiddle, dmixed, grad_out = first_back_call(
        bucket_len, item_count, back, back_got, middle, out_grad, mixed, gains, lse, table, attn_weight, packed
    )
    got_a = tie(got_a, [dmixed])
    got_b = tie(got_b, [dmixed])
    keep_a, send_a = reduce_line(keep_a, got_a)
    got_a = swap_line(send_a)
    keep_b, send_b = reduce_rest(keep_b, got_b)
    got_b = swap_rest(send_b)
    (dmixed,) = tie([dmixed], send_a + send_b)
    last_d, lines_b, mine_w, other_w = last_back_call(
        me, bucket_len, item_count, lse, table, normed, first_d, grad_out, packed, dmixed
    )

    got_b = tie(got_b, [last_d])
    (other_w,) = tie([other_w], got_a + got_b)
    core_w = swap(other_w, CORE)
    keep_b, send_b = reduce_line(keep_b, got_b)
    got_b = swap_line(send_b)
    (core_w,) = tie([core_w], send_b)
    keep_w, send_w = reduce_plane(mine_w, core_w)
    got_w = swap_plane(send_w)
    (last_e,) = tie([last_d], send_w)
    input_grad, dgain_one = input_back_call(first_d, last_e, layer_input, dmiddle, gains, attn_weight)
    got_w = tie(got_w, [input_grad])
    keep_w, send_w = reduce_rest(keep_w, got_w)
    got_w = swap_rest(send_w)

    lines_a, lines_b, dgain_one = tie([lines_a, lines_b, dgain_one], send_w)
    bias_local = jnp.dot(
        onehot, jnp.concatenate([lines_a, lines_b]).reshape(HEADS, SPAN).T, precision=lax.Precision.HIGHEST
    )
    small = jnp.concatenate([dgain_one.reshape(-1), dgain_two.reshape(-1), bias_local.reshape(-1)]).reshape(-1, 128)
    small_got = swap(small, CORE)
    (hidden_late,) = tie([hidden_oa], send_w + [small] + got_b)
    downs = own_a[4:] + own_b[4:]
    output_other = output_call([hidden_late, hidden_ob], downs)
    got_w = tie(got_w, [output_other])
    small = small + tie([small_got], [output_other])[0]
    keep_w, send_w = reduce_line(keep_w, got_w)
    got_w = swap_line(send_w)
    small_y, small_x, small_xy = (swap(small, bits) for bits in (Y, X, X | Y))
    (output_other,) = tie([output_other], send_w)
    output_got = swap(output_other, CORE)
    (hidden_last,) = tie([hidden_a], [output_other, small])
    layer_output = output_call([hidden_last, hidden_b], downs, (middle, output_got))
    small_y, small_x, small_xy, *got_w = tie([small_y, small_x, small_xy] + got_w, [layer_output])
    small = (small + small_y) + (small_x + small_xy)
    small = (small + swap(small, Z)) + (swap(small, 2 * Z) + swap(small, 3 * Z))
    small = small.reshape(-1)
    sum_a, sum_b, sum_w = reduced(keep_a, got_a), reduced(keep_b, got_b), reduced(keep_w, got_w)
    sum_f = jnp.stack([sum_a, sum_b]).reshape(2, 2, HALF, D).swapaxes(0, 1)

    summed = jnp.concatenate([sum_w.reshape(1, SHARD, D), sum_f.reshape(2, SHARD, D)])
    if rest > 1:
        small = lax.psum(small, "rest")
        summed = lax.psum_scatter(summed, "rest", scatter_dimension=1, tiled=True)
    gain_grad = small[: 2 * D].reshape(2, D)
    bias_grad = small[2 * D :].reshape(BUCKETS, HEADS)
    mat_grad = jnp.swapaxes(summed, 1, 2)
    mat_new, mat_first_new, mat_second_new = adam_update(
        matrices, mat_grad, mat_first, mat_second, RATE
    )
    mat_ema_new = EMA_KEEP * mat_ema + (1.0 - EMA_KEEP) * mat_new
    gain_new, gain_first_new, gain_second_new = adam_update(
        gains, gain_grad, gain_first, gain_second, RATE_SMALL
    )
    bias_new, bias_first_new, bias_second_new = adam_update(
        rel_bias, bias_grad, bias_first, bias_second, RATE_SMALL
    )
    return (
        layer_output, input_grad, mat_grad, mat_new, mat_first_new, mat_second_new, mat_ema_new,
        gain_grad, gain_new, gain_first_new, gain_second_new,
        bias_grad, bias_new, bias_first_new, bias_second_new,
    )


def solution(mesh):
    fine = Mesh(mesh.devices.reshape(32, -1), AXES)
    rows = P(AXES, None)
    columns = P(None, None, AXES)
    return jax.shard_map(
        on_device,
        mesh=fine,
        in_specs=(rows, rows) + (columns,) * 4 + (P(),) * 6 + (P(AXES), P(AXES), P()),
        out_specs=(rows, rows) + (columns,) * 5 + (P(),) * 8,
        check_vma=False,
    )
```

```python
import functools

import jax
import jax.numpy as jnp
from jax import lax
from jax.experimental import pallas as pl
from jax.experimental.pallas import tpu as pltpu
from jax.sharding import Mesh, PartitionSpec as P

D = 768
FF = 3072
HEADS = 12
HD = 64
BUCKETS = 32
ROW = 512
STEP = 10
PAIRS = HEADS // 2
WIDE = 2 * HD
SUB = 128
QB = 256
SPAN = 1024
TOEP = 896

EPS = 1e-06
RATE = 0.05
RATE_SMALL = 0.5
BETA_ONE = 0.9
BETA_TWO = 0.999
ADAM_EPS = 1e-08
DECAY = 0.1
EMA_KEEP = 0.75

F32 = jnp.float32
BF16 = jnp.bfloat16
TILE = 256
SHARD = 96
HALF = 48
PIECES = 8
AHEAD = 3
FIRST = 4

NN = (((1,), (0,)), ((), ()))
NT = (((1,), (1,)), ((), ()))
TN = (((0,), (0,)), ((), ()))


def dot(left, right, dims):
    return lax.dot_general(left, right, dims, preferred_element_type=F32)


def params(mebibytes=56):
    return pltpu.CompilerParams(vmem_limit_bytes=mebibytes * 1024 * 1024)


def cost(flops, moved, special=0):
    return pl.CostEstimate(flops=int(flops), bytes_accessed=int(moved), transcendentals=int(special))


def whole(shape):
    return pl.BlockSpec(shape, lambda *_: (0,) * len(shape))


def tiles(rows, columns):
    return pl.BlockSpec((rows, columns), lambda i, *_: (i, 0))


def piece_block():
    return pl.BlockSpec((8 * HALF, D), lambda i: (0, 0), pipeline_mode=pl.Buffered(1))


def toeplitz_kernel(table_ref, out_ref):
    for h in range(2):
        line = jnp.broadcast_to(table_ref[0, h : h + 1, :], (SUB, SPAN))
        rolled = pltpu.roll(line, SPAN - (SUB - 1), 1, stride=1, stride_axis=0)
        out_ref[0, h] = rolled[:, :TOEP]


def toeplitz_call(table):
    return pl.pallas_call(
        toeplitz_kernel,
        grid=(PAIRS,),
        in_specs=[pl.BlockSpec((1, 2, SPAN), lambda p: (p, 0, 0))],
        out_specs=pl.BlockSpec((1, 2, SUB, TOEP), lambda p: (p, 0, 0, 0)),
        out_shape=jax.ShapeDtypeStruct((PAIRS, 2, SUB, TOEP), F32),
        compiler_params=params(16),
        cost_estimate=cost(1e6, 6e6),
        name="toeplitz",
    )(table)


def head_masks():
    lane = lax.broadcasted_iota(jnp.int32, (1, WIDE), 1)
    return [(lane < HD).astype(BF16), (lane >= HD).astype(BF16)]


def bias_block(toep, pair, h, first, rows, span):
    parts = []
    for t in range(rows // SUB):
        left = ROW - SUB - first - t * SUB
        parts.append(toep[pair, h, :, left : left + span])
    return parts[0] if len(parts) == 1 else jnp.concatenate(parts, axis=0)


def blocks_of(span):
    rows = min(span, QB)
    return [(start, first, rows) for start in range(0, ROW, span) for first in range(0, span, rows)]


def live_rows(live, first, rows):
    return first + lax.broadcasted_iota(jnp.int32, (rows, 1), 0) < live


def attend(pairs, offset, rows, len_ref, count_ref, packed, toep, mixed_ref, lse_ref):
    masks = head_masks()
    lane = lax.broadcasted_iota(jnp.int32, (1, WIDE), 1)

    @pl.loop(0, pairs)
    def _(pair):
        @pl.loop(0, rows)
        def _(row):
            length = len_ref[row]
            live = length * count_ref[row]
            at = pl.ds(pl.multiple_of(row * ROW, ROW), ROW)
            cols = columns_of(pair, (0, packed.shape[1] // 3 // WIDE, packed.shape[1] // 3 * 2 // WIDE))
            to = columns_of(pair, (offset,))[0]

            def body(span):
                q_all, k_all, v_all = (packed[at, c] for c in cols)
                stats_all = lse_ref[at, :]
                spots = blocks_of(span)
                keys = [k_all * m for m in masks]
                vals = [v_all * m for m in masks]
                both = [(spot, h) for spot in spots for h in range(2)]
                scores = [
                    dot(q_all[start + first : start + first + rows], keys[h][start : start + span], NT)
                    + bias_block(toep, pair, h, first, rows, span)
                    for (start, first, rows), h in both
                ]
                tops = [jnp.max(s, axis=-1, keepdims=True) for s in scores]
                exps = [jnp.exp(s - top) for s, top in zip(scores, tops)]
                totals = [jnp.sum(e, axis=-1, keepdims=True) for e in exps]
                outs_h = [
                    dot(e.astype(BF16), vals[h][start : start + span], NN) * (1.0 / total)
                    for e, total, ((start, first, rows), h) in zip(exps, totals, both)
                ]
                mixed_parts, stats_parts = [], []
                for i, (start, first, rows) in enumerate(spots):
                    mixed = outs_h[2 * i] + outs_h[2 * i + 1]
                    stats = stats_all[start + first : start + first + rows]
                    for h in range(2):
                        head = (pair + offset) * 2 + h
                        stats = jnp.where(lane == head, tops[2 * i + h] + jnp.log(totals[2 * i + h]), stats)
                    if span < ROW:
                        mixed = jnp.where(live_rows(live, start + first, rows), mixed, 0.0)
                    mixed_parts.append(mixed.astype(BF16))
                    stats_parts.append(stats)
                mixed_ref[at, to] = jnp.concatenate(mixed_parts, axis=0)
                lse_ref[at, :] = jnp.concatenate(stats_parts, axis=0)

            for span in (ROW, ROW // 2, ROW // 4):
                pl.when(length == span)(functools.partial(body, span))


def first_forward_kernel(me_ref, len_ref, count_ref, *refs):
    pieces = refs[:PIECES]
    (
        toep_in, x_ref, gain_ref, normed_out, packed_out, weight_out, lse_ref, mixed_ref,
        weight, normed, packed, toep, in_sem, out_sem, toep_sem,
    ) = refs[PIECES:]
    bias_copy = pltpu.make_async_copy(toep_in.at[pl.ds(0, AHEAD)], toep, toep_sem)
    copies = []
    for i, ref in enumerate(pieces):
        core, half, far = i // 4, i // 2 % 2, i % 2
        for j in range(8):
            near, z = j // 4, j % 4
            plane = near * 2 + far if half == 0 else far * 2 + near
            owner = me_ref[0] ^ (z * 8 + plane * 2 + core)
            row = pl.multiple_of(owner * SHARD + half * HALF, 16)
            copies.append(
                pltpu.make_async_copy(ref.at[pl.ds(j * HALF, HALF)], weight.at[pl.ds(row, HALF)], in_sem)
            )
    for copy in copies:
        copy.start()
    bias_copy.start()
    tokens = x_ref.shape[0]

    @pl.loop(0, tokens // TILE)
    def _(tile):
        at = pl.ds(pl.multiple_of(tile * TILE, TILE), TILE)
        x = x_ref[at, :].astype(F32)
        scale = lax.rsqrt(jnp.mean(x * x, axis=-1, keepdims=True) + EPS)
        normed[at, :] = (x * scale * gain_ref[0:1, :]).astype(BF16)

    for copy in copies:
        copy.wait()
    outs = [
        pltpu.make_async_copy(weight, weight_out, out_sem.at[0]),
        pltpu.make_async_copy(normed, normed_out, out_sem.at[1]),
        pltpu.make_async_copy(packed, packed_out, out_sem.at[2]),
    ]
    outs[0].start()
    outs[1].start()

    @pl.loop(0, tokens // TILE)
    def _(tile):
        at = pl.ds(pl.multiple_of(tile * TILE, TILE), TILE)
        for part in range(3):
            cols = slice(part * D, (part + 1) * D)
            packed[at, cols] = dot(normed[at, :], weight[cols, :], NT).astype(BF16)

    outs[2].start()
    lse_ref[...] = jnp.zeros_like(lse_ref)
    bias_copy.wait()
    attend(AHEAD, 0, tokens // ROW, len_ref, count_ref, packed, toep, mixed_ref, lse_ref)
    for copy in outs:
        copy.wait()


def first_forward_call(me, lengths, counts, pieces, toep, x, gains):
    tokens = x.shape[0]
    anywhere = pl.BlockSpec(memory_space=pl.ANY)
    inside = pl.BlockSpec(memory_space=pltpu.VMEM)
    return pl.pallas_call(
        first_forward_kernel,
        grid_spec=pltpu.PrefetchScalarGridSpec(
            num_scalar_prefetch=3,
            grid=(),
            in_specs=[anywhere] * (PIECES + 1) + [inside] * 2,
            out_specs=[anywhere] * 3 + [inside] * 2,
            scratch_shapes=[
                pltpu.VMEM((4 * D, D), BF16),
                pltpu.VMEM((tokens, D), BF16),
                pltpu.VMEM((tokens, 3 * D), BF16),
                pltpu.VMEM((AHEAD, 2, SUB, TOEP), F32),
                pltpu.SemaphoreType.DMA,
                pltpu.SemaphoreType.DMA((3,)),
                pltpu.SemaphoreType.DMA,
            ],
        ),
        out_shape=[
            jax.ShapeDtypeStruct((tokens, D), BF16),
            jax.ShapeDtypeStruct((tokens, 3 * D), BF16),
            jax.ShapeDtypeStruct((4 * D, D), BF16),
            jax.ShapeDtypeStruct((tokens, WIDE), F32),
            jax.ShapeDtypeStruct((tokens, AHEAD * WIDE), BF16),
        ],
        compiler_params=params(56),
        cost_estimate=cost(12e9, 30e6, 4e6),
        name="first_forward",
    )(me, lengths, counts, *pieces, toep, x, gains)


def last_forward_kernel(
    len_ref, count_ref, x_ref, gain_ref, first_ref, stats_ref, toep_in, weight_in, packed_in,
    lse_ref, mixed_ref, middle_out, second_out,
    weight, packed, middle_s, second_s, toep, in_sems, out_sems,
):
    tokens = x_ref.shape[0]
    start = AHEAD * WIDE
    width = D - start
    copies = [
        pltpu.make_async_copy(weight_in.at[pl.ds(3 * D, D)], weight, in_sems.at[0]),
        pltpu.make_async_copy(toep_in.at[pl.ds(AHEAD, PAIRS - AHEAD)], toep, in_sems.at[4]),
    ]
    for part in range(3):
        copies.append(
            pltpu.make_async_copy(
                packed_in.at[:, pl.ds(part * D + start, width)], packed.at[:, pl.ds(part * width, width)], in_sems.at[1 + part]
            )
        )
    for copy in copies:
        copy.start()
    lse_ref[...] = stats_ref[...]
    mixed_ref[:, :start] = first_ref[...]
    for copy in copies[1:]:
        copy.wait()
    attend(PAIRS - AHEAD, AHEAD, tokens // ROW, len_ref, count_ref, packed, toep, mixed_ref, lse_ref)
    copies[0].wait()
    outs = []
    for tile in range(tokens // TILE):
        at = pl.ds(tile * TILE, TILE)
        middle = x_ref[at, :].astype(F32) + dot(mixed_ref[at, :], weight[...], NT)
        middle_s[at, :] = middle
        scale = lax.rsqrt(jnp.mean(middle * middle, axis=-1, keepdims=True) + EPS)
        second_s[at, :] = (middle * scale * gain_ref[1:2, :]).astype(BF16)
        for i, (src, dst) in enumerate(((middle_s, middle_out), (second_s, second_out))):
            copy = pltpu.make_async_copy(src.at[at], dst.at[at], out_sems.at[2 * tile + i])
            copy.start()
            outs.append(copy)
    for copy in outs:
        copy.wait()


def last_forward_call(lengths, counts, x, gains, first, stats, toep, weight, packed):
    tokens = x.shape[0]
    anywhere = pl.BlockSpec(memory_space=pl.ANY)
    inside = pl.BlockSpec(memory_space=pltpu.VMEM)
    flat = jax.ShapeDtypeStruct((tokens, D), BF16)
    return pl.pallas_call(
        last_forward_kernel,
        grid_spec=pltpu.PrefetchScalarGridSpec(
            num_scalar_prefetch=2,
            grid=(),
            in_specs=[inside] * 4 + [anywhere] * 3,
            out_specs=[inside] * 2 + [anywhere] * 2,
            scratch_shapes=[
                pltpu.VMEM((D, D), BF16),
                pltpu.VMEM((tokens, 3 * (PAIRS - AHEAD) * WIDE), BF16),
                pltpu.VMEM((tokens, D), F32),
                pltpu.VMEM((tokens, D), BF16),
                pltpu.VMEM((PAIRS - AHEAD, 2, SUB, TOEP), F32),
                pltpu.SemaphoreType.DMA((5,)),
                pltpu.SemaphoreType.DMA((2 * tokens // TILE,)),
            ],
        ),
        out_shape=[
            jax.ShapeDtypeStruct((tokens, WIDE), F32),
            flat,
            jax.ShapeDtypeStruct((tokens, D), F32),
            flat,
        ],
        compiler_params=params(56),
        cost_estimate=cost(8e9, 20e6, 4e6),
        name="last_forward",
    )(lengths, counts, x, gains, first, stats, toep, weight, packed)


def fold_kernel(first_ref, last_ref, out_ref):
    def fold(ref):
        total = jnp.concatenate([ref[0], jnp.zeros((2, SUB, SPAN - TOEP), F32)], axis=2)
        height = SUB
        while height > 8:
            height //= 2
            total = pltpu.roll(total[:, :height], height, 2) + total[:, height:]
        line = total[:, 7]
        for r in range(7):
            line = line + pltpu.roll(total, 7 - r, 2)[:, r]
        out_ref[0] = line

    pl.when(pl.program_id(0) < FIRST)(functools.partial(fold, first_ref))
    pl.when(pl.program_id(0) >= FIRST)(functools.partial(fold, last_ref))


def fold_call(first, last):
    def block(start, count):
        return pl.BlockSpec((1, 2, SUB, TOEP), lambda p: (jnp.clip(p - start, 0, count - 1), 0, 0, 0))

    return pl.pallas_call(
        fold_kernel,
        grid=(PAIRS,),
        in_specs=[block(0, FIRST), block(FIRST, PAIRS - FIRST)],
        out_specs=pl.BlockSpec((1, 2, SPAN), lambda p: (p, 0, 0)),
        out_shape=jax.ShapeDtypeStruct((PAIRS, 2, SPAN), F32),
        compiler_params=params(62),
        cost_estimate=cost(1e6, 6e6),
        name="fold",
    )(first, last)


def attend_back(
    pairs, offset, me_rows, len_ref, count_ref, cols_of, packed, dmixed, lse_ref, delta_ref, toep, diag, out_ref,
    diag_out, diag_sems,
):
    masks = head_masks()
    lane = lax.broadcasted_iota(jnp.int32, (1, WIDE), 1)

    @pl.loop(0, pairs)
    def _(pair):
        diag[pair] = jnp.zeros((2, SUB, TOEP), F32)

        @pl.loop(0, me_rows)
        def _(row):
            length = len_ref[row]
            live = length * count_ref[row]
            at = pl.ds(pl.multiple_of(row * ROW, ROW), ROW)
            cols = cols_of(pair)

            def body(span):
                q_all, k_all, v_all = (packed[at, c] for c in cols[:3])
                do_all = dmixed[at, cols[3]]
                if span < ROW:
                    do_all = jnp.where(live_rows(live, 0, ROW), do_all.astype(F32), 0.0).astype(BF16)
                stats = lse_ref[at, :]
                spots = blocks_of(span)
                queries, keys, vals, dos = ([a * m for m in masks] for a in (q_all, k_all, v_all, do_all))
                lses, sums = (
                    [jnp.sum(jnp.where(lane == (pair + offset) * 2 + h, a, 0.0), axis=-1, keepdims=True) for h in range(2)]
                    for a in (stats, delta_ref[at, :])
                )
                both = [(spot, h) for spot in spots for h in range(2)]

                def rows_of(value, spot):
                    return value[spot[0] + spot[1] : spot[0] + spot[1] + spot[2]]

                def keys_of(value, spot):
                    return value[spot[0] : spot[0] + span]

                scores = [
                    dot(rows_of(q_all, spot), keys_of(keys[h], spot), NT) + bias_block(toep, pair, h, spot[1], spot[2], span)
                    for spot, h in both
                ]
                dps = [dot(rows_of(do_all, spot), keys_of(vals[h], spot), NT) for spot, h in both]
                probs = [jnp.exp(s - rows_of(lses[h], spot)) for s, (spot, h) in zip(scores, both)]
                dss = [p * (dp - rows_of(sums[h], spot)) for p, dp, (spot, h) in zip(probs, dps, both)]
                for ds, (spot, h) in zip(dss, both):
                    for sub in range(spot[2] // SUB):
                        left = ROW - SUB - spot[1] - sub * SUB
                        diag[pair, h, :, left : left + span] += ds[sub * SUB : (sub + 1) * SUB]
                lows = [ds.astype(BF16) for ds in dss]
                plows = [p.astype(BF16) for p in probs]
                dqs = [dot(low, keys_of(keys[h], spot), NN) for low, (spot, h) in zip(lows, both)]
                dks = [dot(low, rows_of(queries[h], spot), TN) for low, (spot, h) in zip(lows, both)]
                dvs = [dot(low, rows_of(dos[h], spot), TN) for low, (spot, h) in zip(plows, both)]
                dq = jnp.concatenate([dqs[2 * i] + dqs[2 * i + 1] for i in range(len(spots))], axis=0)
                each = len(both) * span // ROW
                dk, dv = (
                    jnp.concatenate([sum(d[i + 1 : i + each], d[i]) for i in range(0, len(both), each)], axis=0)
                    for d in (dks, dvs)
                )
                for part, value in enumerate((dq, dk, dv)):
                    to = pl.ds(pl.multiple_of(pair * WIDE + part * pairs * WIDE, WIDE), WIDE)
                    out_ref[at, to] = value.astype(BF16)

            for span in (ROW, ROW // 2, ROW // 4):
                pl.when(length == span)(functools.partial(body, span))

        pltpu.make_async_copy(diag.at[pair], diag_out.at[pair], diag_sems.at[pair]).start()

    for pair in range(pairs):
        pltpu.make_async_copy(diag.at[pair], diag_out.at[pair], diag_sems.at[pair]).wait()


def columns_of(pair, widths):
    return [pl.ds(pl.multiple_of((pair + w) * WIDE, WIDE), WIDE) for w in widths]


def first_back_kernel(
    len_ref, count_ref, mixed_ref, gain_ref, lse_ref, part_in, got_in, middle_in, grad_in, toep_in, weight_in, packed_in,
    dgain_ref, out_ref, delta_ref, diag_out, dmiddle_out, dmixed_out, dweight_out,
    part_s, got_s, middle_s, grad_s, dmixed, dweight, weight, packed, lows, toep, diag, in_sems, sems, out_sems, diag_sems,
):
    tokens = mixed_ref.shape[0]
    count = tokens // TILE
    width = FIRST * WIDE
    first = pltpu.make_async_copy(weight_in.at[pl.ds(3 * D, D)], weight, sems.at[0])
    first.start()
    ins = []
    for tile in range(count):
        at = pl.ds(tile * TILE, TILE)
        for i, (src, dst) in enumerate(((part_in, part_s), (got_in, got_s), (middle_in, middle_s), (grad_in, grad_s))):
            copy = pltpu.make_async_copy(src.at[at], dst.at[at], in_sems.at[4 * tile + i])
            copy.start()
            ins.append(copy)
    later = [pltpu.make_async_copy(toep_in.at[pl.ds(0, FIRST)], toep, sems.at[4])]
    later[0].start()
    for part in range(3):
        copy = pltpu.make_async_copy(
            packed_in.at[:, pl.ds(part * D, width)], packed.at[:, pl.ds(part * width, width)], sems.at[1 + part]
        )
        copy.start()
        later.append(copy)
    first.wait()
    outs = []
    of_feature = lax.broadcasted_iota(jnp.int32, (D, WIDE), 0) // HD
    heads = (of_feature == lax.broadcasted_iota(jnp.int32, (D, WIDE), 1)).astype(BF16)
    dgain = jnp.zeros((1, D), F32)
    for tile in range(count):
        at = pl.ds(tile * TILE, TILE)
        for copy in ins[4 * tile : 4 * tile + 4]:
            copy.wait()
        db = part_s[at, :] + got_s[at, :]
        middle = middle_s[at, :]
        scale = lax.rsqrt(jnp.mean(middle * middle, axis=-1, keepdims=True) + EPS)
        dn = db * gain_ref[1:2, :]
        inner = jnp.mean(dn * middle, axis=-1, keepdims=True)
        dmiddle = grad_s[at, :].astype(F32) + scale * dn - middle * (scale * scale * scale * inner)
        part_s[at, :] = dmiddle
        copy = pltpu.make_async_copy(part_s.at[at], dmiddle_out.at[at], out_sems.at[tile])
        copy.start()
        outs.append(copy)
        low = dmiddle.astype(BF16)
        lows[at, :] = low
        do = dot(low, weight[...], NN).astype(BF16)
        dmixed[at, :] = do
        dgain += jnp.sum(db * middle * scale, axis=0, keepdims=True)
        product = do.astype(F32) * mixed_ref[at, :].astype(F32)
        high = product.astype(BF16)
        delta = dot(high, heads, NN) + dot((product - high.astype(F32)).astype(BF16), heads, NN)
        delta_ref[at, :] = delta
    dgain_ref[...] = dgain
    copy = pltpu.make_async_copy(dmixed, dmixed_out, out_sems.at[count])
    copy.start()
    outs.append(copy)
    dweight[...] = dot(lows[...], mixed_ref[...], TN)
    copy = pltpu.make_async_copy(dweight, dweight_out, out_sems.at[count + 1])
    copy.start()
    outs.append(copy)
    for copy in later:
        copy.wait()

    def cols_of(pair):
        return columns_of(pair, (0, FIRST, 2 * FIRST, 0))

    attend_back(
        FIRST, 0, tokens // ROW, len_ref, count_ref, cols_of, packed, dmixed, lse_ref, delta_ref, toep, diag,
        out_ref, diag_out, diag_sems,
    )
    for copy in outs:
        copy.wait()


def first_back_call(lengths, counts, part, got, middle, out_grad, mixed, gains, lse, toep, weight, packed):
    tokens = part.shape[0]
    anywhere = pl.BlockSpec(memory_space=pl.ANY)
    inside = pl.BlockSpec(memory_space=pltpu.VMEM)
    width = 3 * FIRST * WIDE
    count = tokens // TILE
    return pl.pallas_call(
        first_back_kernel,
        grid_spec=pltpu.PrefetchScalarGridSpec(
            num_scalar_prefetch=2,
            grid=(),
            in_specs=[inside] * 3 + [anywhere] * 7,
            out_specs=[inside] * 3 + [anywhere] * 4,
            scratch_shapes=[pltpu.VMEM((tokens, D), F32)] * 3
            + [
                pltpu.VMEM((tokens, D), BF16),
                pltpu.VMEM((tokens, D), BF16),
                pltpu.VMEM((D, D), F32),
                pltpu.VMEM((D, D), BF16),
                pltpu.VMEM((tokens, width), BF16),
                pltpu.VMEM((tokens, D), BF16),
                pltpu.VMEM((FIRST, 2, SUB, TOEP), F32),
                pltpu.VMEM((FIRST, 2, SUB, TOEP), F32),
                pltpu.SemaphoreType.DMA((4 * count,)),
                pltpu.SemaphoreType.DMA((5,)),
                pltpu.SemaphoreType.DMA((count + 2,)),
                pltpu.SemaphoreType.DMA((FIRST,)),
            ],
        ),
        out_shape=[
            jax.ShapeDtypeStruct((1, D), F32),
            jax.ShapeDtypeStruct((tokens, width), BF16),
            jax.ShapeDtypeStruct((tokens, WIDE), F32),
            jax.ShapeDtypeStruct((FIRST, 2, SUB, TOEP), F32),
            jax.ShapeDtypeStruct((tokens, D), F32),
            jax.ShapeDtypeStruct((tokens, D), BF16),
            jax.ShapeDtypeStruct((D, D), F32),
        ],
        compiler_params=params(62),
        cost_estimate=cost(15e9, 30e6, 7e6),
        name="first_back",
    )(lengths, counts, mixed, gains, lse, part, got, middle, out_grad, toep, weight, packed)


def last_back_kernel(
    me_ref, len_ref, count_ref, lse_ref, delta_ref, gain_ref, toep_in, normed_in, first_in, dout_in, packed_in, dmixed_in, weight_in,
    out_ref, dgain_ref, diag_out, own_out, other_out,
    packed, dmixed, normed, first, weight, total, low_total, toep, diag, sems, out_sems, diag_sems,
):
    tokens = normed.shape[0]
    pairs = PAIRS - FIRST
    width = pairs * WIDE
    start = FIRST * WIDE
    copies = [
        pltpu.make_async_copy(dmixed_in.at[:, pl.ds(start, width)], dmixed, sems.at[0]),
        pltpu.make_async_copy(toep_in.at[pl.ds(FIRST, pairs)], toep, sems.at[7]),
    ]
    for part in range(3):
        copies.append(
            pltpu.make_async_copy(
                packed_in.at[:, pl.ds(part * D + start, width)], packed.at[:, pl.ds(part * width, width)], sems.at[1 + part]
            )
        )
    later = [
        pltpu.make_async_copy(normed_in, normed, sems.at[4]),
        pltpu.make_async_copy(first_in, first, sems.at[5]),
        pltpu.make_async_copy(dout_in, total.at[pl.ds(3 * D, D)], sems.at[6]),
        pltpu.make_async_copy(weight_in.at[pl.ds(0, 3 * D)], weight, sems.at[8]),
    ]
    for copy in copies + later:
        copy.start()
    for copy in copies:
        copy.wait()

    def cols_of(pair):
        return columns_of(pair, (0, pairs, 2 * pairs, 0))

    attend_back(
        pairs, FIRST, tokens // ROW, len_ref, count_ref, cols_of, packed, dmixed, lse_ref, delta_ref, toep, diag,
        out_ref, diag_out, diag_sems,
    )
    for copy in later:
        copy.wait()
    low_total[3 * D :] = total[3 * D :].astype(BF16)
    for part in range(3):
        for at, rows, grads in ((part * D, start, first), (part * D + start, width, out_ref)):
            grad = dot(grads[:, part * rows : (part + 1) * rows], normed[...], TN)
            total[at : at + rows] = grad
            low_total[at : at + rows] = grad.astype(BF16)
    outs = []
    for core, kept, out in ((1, low_total, other_out), (0, total, own_out)):
        for i in range(32):
            half, plane, z = i // 16, i // 4 % 4, i % 4
            owner = me_ref[0] ^ (z * 8 + plane * 2 + core)
            row = pl.multiple_of(owner * SHARD + half * HALF, 16)
            copy = pltpu.make_async_copy(kept.at[pl.ds(row, HALF)], out.at[pl.ds(i * HALF, HALF)], out_sems.at[core])
            copy.start()
            outs.append(copy)
    dgain = jnp.zeros((8, D), F32)
    for at in range(0, 3 * D, D // 2):
        product = weight[at : at + D // 2].astype(F32) * total[at : at + D // 2]
        dgain += jnp.sum(product.reshape(D // 16, 8, D), axis=0)
    dgain_ref[...] = jnp.sum(dgain, axis=0, keepdims=True) / gain_ref[0:1, :]
    for copy in outs:
        copy.wait()


def last_back_call(me, lengths, counts, lse, delta, gains, toep, normed, first, grad_out, packed, dmixed, weight):
    tokens = normed.shape[0]
    anywhere = pl.BlockSpec(memory_space=pl.ANY)
    inside = pl.BlockSpec(memory_space=pltpu.VMEM)
    pairs = PAIRS - FIRST
    width = pairs * WIDE
    return pl.pallas_call(
        last_back_kernel,
        grid_spec=pltpu.PrefetchScalarGridSpec(
            num_scalar_prefetch=3,
            grid=(),
            in_specs=[inside] * 3 + [anywhere] * 7,
            out_specs=[inside] * 2 + [anywhere] * 3,
            scratch_shapes=[
                pltpu.VMEM((tokens, 3 * width), BF16),
                pltpu.VMEM((tokens, width), BF16),
                pltpu.VMEM((tokens, D), BF16),
                pltpu.VMEM((tokens, 3 * FIRST * WIDE), BF16),
                pltpu.VMEM((3 * D, D), BF16),
                pltpu.VMEM((4 * D, D), F32),
                pltpu.VMEM((4 * D, D), BF16),
                pltpu.VMEM((pairs, 2, SUB, TOEP), F32),
                pltpu.VMEM((pairs, 2, SUB, TOEP), F32),
                pltpu.SemaphoreType.DMA((9,)),
                pltpu.SemaphoreType.DMA((2,)),
                pltpu.SemaphoreType.DMA((pairs,)),
            ],
        ),
        out_shape=[
            jax.ShapeDtypeStruct((tokens, 3 * width), BF16),
            jax.ShapeDtypeStruct((1, D), F32),
            jax.ShapeDtypeStruct((pairs, 2, SUB, TOEP), F32),
            jax.ShapeDtypeStruct((2 * D, D), F32),
            jax.ShapeDtypeStruct((2 * D, D), BF16),
        ],
        compiler_params=params(62),
        cost_estimate=cost(10e9, 30e6, 4e6),
        name="last_back",
    )(me, lengths, counts, lse, delta, gains, toep, normed, first, grad_out, packed, dmixed, weight)


def feed_tile(second, grad, up, down):
    u = dot(second, up, NT)
    square = u * u
    t = jnp.tanh(0.7978845608 * u * (1.0 + 0.044715 * square))
    plus = 0.5 * (1.0 + t)
    slope = plus + (0.5 * 0.7978845608) * u * (1.0 - t * t) * (1.0 + 3 * 0.044715 * square)
    dh = dot(grad, down, NT).astype(BF16).astype(F32)
    return (u * plus).astype(BF16), (dh * slope).astype(BF16)


def planes_of(near, far, half):
    rows = 4 * HALF
    near, far = ([value[i : i + rows] for i in (0, rows)] for value in (near, far))
    order = (near[0], far[0], near[1], far[1]) if half == 0 else (near[0], near[1], far[0], far[1])
    return jnp.concatenate(order, axis=0)


def weights_of(refs):
    return [planes_of(refs[2 * half][...], refs[2 * half + 1][...], half) for half in range(2)]


def feed_kernel(parts, *refs):
    up, down = weights_of(refs[:4])
    second_ref, grad_ref, *refs, back_ref, hidden_ref, dpre_ref = refs[4:]
    hidden, du = feed_tile(second_ref[...], grad_ref[...], up, down)
    hidden_ref[...] = hidden
    dpre_ref[...] = du
    back = dot(du, up, NN)
    back_ref[...] = back + refs[0][...] if parts else back


def feed_call(weights, second, out_grad, start=None):
    tokens = second.shape[0]
    flat = tiles(TILE, D)
    low_flat = jax.ShapeDtypeStruct((tokens, D), BF16)
    more = [] if start is None else [start]
    return pl.pallas_call(
        functools.partial(feed_kernel, len(more)),
        grid=(tokens // TILE,),
        in_specs=[piece_block()] * 4 + [flat, flat] + [flat] * len(more),
        out_specs=[flat, flat, flat],
        out_shape=[jax.ShapeDtypeStruct((tokens, D), F32), low_flat, low_flat],
        compiler_params=params(20),
        cost_estimate=cost(6 * tokens * D * D, 15e6, tokens * D),
        name="feed",
    )(*weights, second, out_grad, *more)


def feed_sum_kernel(parts, *refs):
    weights = refs[:4]
    ins = refs[4:10]
    refs = refs[10:]
    start_ref = refs[0] if parts else None
    back_ref, hidden_ref, out_ref, up_send, down_send = refs[parts : parts + 5]
    second, grad, second_other, grad_other, hidden_other, dpre_other, hidden, dpre, tile_sems, sems = refs[parts + 5 :]
    step = pl.program_id(0)
    count = second.shape[0] // TILE

    def tile_copies(tile):
        at = pl.ds(pl.multiple_of(tile * TILE, TILE), TILE)
        return [
            pltpu.make_async_copy(src.at[at], dst.at[at], tile_sems.at[2 * tile + i])
            for i, (src, dst) in enumerate(((ins[0], second), (ins[1], grad)))
        ]

    others = [
        pltpu.make_async_copy(src, dst, sems.at[i])
        for i, (src, dst) in enumerate(zip(ins[2:], (second_other, grad_other, hidden_other, dpre_other)))
    ]

    @pl.when(step == 0)
    def _():
        for tile in range(count):
            for copy in tile_copies(tile):
                copy.start()
        for copy in others:
            copy.start()

    @pl.when(step < count)
    def _():
        at = pl.ds(pl.multiple_of(step * TILE, TILE), TILE)
        for copy in tile_copies(step):
            copy.wait()
        up, down = weights_of(weights)
        low_hidden, du = feed_tile(second[at, :], grad[at, :], up, down)
        hidden_ref[...] = low_hidden
        hidden[at, :] = low_hidden
        dpre[at, :] = du
        back = dot(du, up, NN)
        back_ref[...] = back if start_ref is None else back + start_ref[...]

    @pl.when(step == count)
    def _():
        for copy in others:
            copy.wait()
        total = dot(dpre[...], second[...], TN) + dot(dpre_other[...], second_other[...], TN)
        out_ref[0] = total
        for x in range(2):
            up_send[x * 4 * HALF : (x + 1) * 4 * HALF] = total[(2 * x + 1) * 4 * HALF : (2 * x + 2) * 4 * HALF].astype(BF16)

    @pl.when(step == count + 1)
    def _():
        total = dot(hidden[...], grad[...], TN) + dot(hidden_other[...], grad_other[...], TN)
        out_ref[0] = total
        down_send[...] = total[8 * HALF :].astype(BF16)


def feed_sum_call(weights, second, out_grad, second_other, grad_other, hidden_other, dpre_other, start=None):
    tokens = second.shape[0]
    count = tokens // TILE
    anywhere = pl.BlockSpec(memory_space=pl.ANY)
    tile = pl.BlockSpec((TILE, D), lambda i: (jnp.minimum(i, count - 1), 0))
    more = [] if start is None else [start]
    return pl.pallas_call(
        functools.partial(feed_sum_kernel, len(more)),
        grid=(count + 2,),
        in_specs=[piece_block()] * 4 + [anywhere] * 6 + [tile] * len(more),
        out_specs=[
            tile,
            tile,
            pl.BlockSpec((1, D, D), lambda i: (jnp.maximum(i - count, 0), 0, 0)),
            whole((8 * HALF, D)),
            whole((8 * HALF, D)),
        ],
        out_shape=[
            jax.ShapeDtypeStruct((tokens, D), F32),
            jax.ShapeDtypeStruct((tokens, D), BF16),
            jax.ShapeDtypeStruct((2, D, D), F32),
            jax.ShapeDtypeStruct((8 * HALF, D), BF16),
            jax.ShapeDtypeStruct((8 * HALF, D), BF16),
        ],
        scratch_shapes=[pltpu.VMEM((tokens, D), BF16)] * 8
        + [pltpu.SemaphoreType.DMA((2 * count,)), pltpu.SemaphoreType.DMA((4,))],
        compiler_params=params(56 if more else 36),
        cost_estimate=cost(14 * tokens * D * D, 30e6, tokens * D),
        name="feed_sum",
    )(*weights, second, out_grad, second_other, grad_other, hidden_other, dpre_other, *more)


def output_kernel(*refs):
    total = None
    for i in range(2):
        part = dot(refs[i][...], planes_of(refs[2 + 2 * i][...], refs[3 + 2 * i][...], 1), NN)
        total = part if total is None else total + part
    for ref in refs[6:-1]:
        total += ref[...]
    refs[-1][...] = total.astype(refs[-1].dtype)


def output_call(hiddens, downs, more=(), kind=F32):
    tokens = hiddens[0].shape[0]
    return pl.pallas_call(
        output_kernel,
        grid=(tokens // TILE,),
        in_specs=[tiles(TILE, D)] * 2 + [piece_block()] * 4 + [tiles(TILE, D)] * len(more),
        out_specs=tiles(TILE, D),
        out_shape=jax.ShapeDtypeStruct((tokens, D), kind),
        compiler_params=params(62),
        cost_estimate=cost(4 * tokens * D * D, 12e6),
        name="output",
    )(*hiddens, *downs, *more)


def input_back_kernel(first_ref, last_ref, x_ref, dmiddle_ref, gain_ref, weight_ref, dx_ref):
    da = jnp.zeros(dx_ref.shape, F32)
    cut = FIRST * WIDE
    for part in range(3):
        da += dot(first_ref[:, part * cut : (part + 1) * cut], weight_ref[part * D : part * D + cut, :], NN)
        rest = D - cut
        da += dot(last_ref[:, part * rest : (part + 1) * rest], weight_ref[part * D + cut : (part + 1) * D, :], NN)
    x = x_ref[...].astype(F32)
    scale = lax.rsqrt(jnp.mean(x * x, axis=-1, keepdims=True) + EPS)
    dm = da * gain_ref[0:1, :]
    inner = jnp.mean(dm * x, axis=-1, keepdims=True)
    dx_ref[...] = dmiddle_ref[...] + scale * dm - x * (scale * scale * scale * inner)


def input_back_call(first, last, x, dmiddle, gains, weight):
    tokens = x.shape[0]
    return pl.pallas_call(
        input_back_kernel,
        grid=(tokens // TILE,),
        in_specs=[
            tiles(TILE, first.shape[1]),
            tiles(TILE, last.shape[1]),
            tiles(TILE, D),
            tiles(TILE, D),
            whole((2, D)),
            whole((3 * D, D)),
        ],
        out_specs=tiles(TILE, D),
        out_shape=jax.ShapeDtypeStruct((tokens, D), F32),
        compiler_params=params(62),
        cost_estimate=cost(2 * tokens * D * 3 * D, 18e6),
        name="input_back",
    )(first, last, x, dmiddle, gains, weight)


def adam_update(param, grad, first, second, rate):
    first_new = BETA_ONE * first + (1.0 - BETA_ONE) * grad
    second_new = BETA_TWO * second + (1.0 - BETA_TWO) * grad * grad
    first_hat = first_new / (1.0 - BETA_ONE**STEP)
    second_hat = second_new / (1.0 - BETA_TWO**STEP)
    param_new = param - rate * (first_hat / (jnp.sqrt(second_hat) + ADAM_EPS) + DECAY * param)
    return (param_new, first_new, second_new)


AXES = ("tree", "rest")
CORE, Y, X, Z = 1, 2, 4, 8


def swap(value, bits):
    return lax.ppermute(value, "tree", [(i, i ^ bits) for i in range(32)])


def tie(values, after):
    return list(lax.optimization_barrier(tuple(values) + tuple(after))[: len(values)])


def gather_z(shard):
    return [shard] + [swap(shard, k * Z) for k in (1, 2, 3)]


def gather_halves(line, first=0):
    return [jnp.concatenate([p[i : i + HALF] for p in line]) for i in (first, first + HALF)]


def gather_plane(halves):
    return [swap(halves[0], X), swap(halves[1], Y)]


def gather_near(halves, turned):
    return [jnp.concatenate([half, got]) for half, got in zip(halves, turned)]


def gather_far(near):
    return [swap(near[0], Y), swap(near[1], X)]


def gathered(near, far):
    return [near[0], far[0], near[1], far[1]]


def gather_core(pieces):
    return [swap(p, CORE) for p in pieces]


def swap_plane(sends):
    return [swap(sends[0], Y), swap(sends[1], X)]


def swap_rest(sends):
    return [swap(sends[0], X), swap(sends[1], Y)]


def feed_rest_kernel(*refs):
    grads, gots, outs = refs[:8], refs[8:12], refs[12:]
    rows = 4 * HALF
    for chunk in range(2):
        for half in range(2):
            got = gots[2 * chunk + half]
            for far in range(2):
                value = grads[4 * chunk + 2 * half + far][0] + got[far * rows : (far + 1) * rows].astype(F32)
                out = outs[2 * far + half]
                out[chunk] = value.astype(out.dtype)


def feed_rest_call(grads, gots):
    rows = 4 * HALF
    blocks = [(0, 0), (0, 2), (1, 0), (1, 1)]
    shape = (2, rows, D)
    outs = pl.pallas_call(
        feed_rest_kernel,
        grid=(1,),
        in_specs=[pl.BlockSpec((1, rows, D), lambda i, b=b: (b[0], b[1], 0)) for _ in range(2) for b in blocks]
        + [whole((2 * rows, D))] * 4,
        out_specs=[whole(shape)] * 4,
        out_shape=[jax.ShapeDtypeStruct(shape, kind) for kind in (F32, F32, BF16, BF16)],
        compiler_params=params(62),
        cost_estimate=cost(1e6, 10e6),
        name="feed_rest",
    )(*[grads[0]] * 4, *[grads[1]] * 4, *gots)
    return outs[:2], outs[2:]


def plane_kernel(*refs):
    for half, out in enumerate(refs[8:]):
        for i in range(2):
            value = refs[4 * half + i][...] + refs[4 * half + 2 + i][...].astype(F32)
            out[i * 4 * HALF : (i + 1) * 4 * HALF] = value.astype(BF16)


def plane_call(own, got):
    rows = 4 * HALF

    def blocks(*places):
        return [pl.BlockSpec((rows, D), lambda i, p=p: (p, 0)) for p in places]

    return pl.pallas_call(
        plane_kernel,
        grid=(1,),
        in_specs=blocks(1, 3, 1, 3, 6, 7, 6, 7),
        out_specs=[whole((2 * rows, D))] * 2,
        out_shape=[jax.ShapeDtypeStruct((2 * rows, D), BF16)] * 2,
        compiler_params=params(62),
        cost_estimate=cost(1e6, 5e6),
        name="plane",
    )(own, own, got, got, own, own, got, got)


def rest_kernel(*refs):
    owns, cores, gots, outs = refs[:4], refs[4:8], refs[8:10], refs[10:]
    rows = 4 * HALF
    for half in range(2):
        for far in range(2):
            i = 2 * half + far
            value = owns[i][...] + cores[i][...].astype(F32) + gots[half][far * rows : (far + 1) * rows].astype(F32)
            out = outs[2 * far + half]
            out[...] = value.astype(out.dtype)


def rest_call(own, core, gots):
    rows = 4 * HALF
    blocks = [pl.BlockSpec((rows, D), lambda i, p=p: (p, 0)) for p in (0, 2, 4, 5)]
    outs = pl.pallas_call(
        rest_kernel,
        grid=(1,),
        in_specs=blocks * 2 + [whole((2 * rows, D))] * 2,
        out_specs=[whole((rows, D))] * 4,
        out_shape=[jax.ShapeDtypeStruct((rows, D), kind) for kind in (F32, F32, BF16, BF16)],
        compiler_params=params(62),
        cost_estimate=cost(1e6, 7e6),
        name="rest",
    )(*[own] * 4, *[core] * 4, *gots)
    return outs[:2], outs[2:]


def line_kernel(one_ref, two_ref, got_one, got_two, *outs):
    for k, out in enumerate(outs):
        at = slice(k * HALF, (k + 1) * HALF)
        for chunk in range(one_ref.shape[0]):
            for half, (ref, got) in enumerate(((one_ref, got_one), (two_ref, got_two))):
                out[chunk, half] = (ref[chunk, at] + got[chunk, at].astype(F32)).astype(out.dtype)


def reduce_line(keep, got):
    chunks = keep[0].size // (4 * HALF * D)
    keep, got = ([a.reshape(chunks, 4 * HALF, D) for a in values] for values in (keep, got))
    shape = (chunks, 2, HALF, D)
    outs = pl.pallas_call(
        line_kernel,
        out_shape=[jax.ShapeDtypeStruct(shape, F32)] + [jax.ShapeDtypeStruct(shape, BF16)] * 3,
        compiler_params=params(62),
        cost_estimate=cost(1e6, 6e6),
        name="line",
    )(*keep, *got)
    return outs[0], list(outs[1:])


def swap_line(sends):
    return [swap(send, k * Z) for k, send in zip((1, 2, 3), sends)]


def reduced(keep, got):
    return keep + got[0].astype(F32) + got[1].astype(F32) + got[2].astype(F32)


def on_device(
    layer_input, out_grad, matrices, mat_first, mat_second, mat_ema, gains, gain_first, gain_second,
    rel_bias, bias_first, bias_second, bucket_len, item_count, bucket_table,
):
    rest = lax.axis_size("rest")
    shards = jnp.swapaxes(matrices, 1, 2).astype(BF16)
    if rest > 1:
        shards = lax.all_gather(shards, "rest", axis=1, tiled=True)
    shard_a, shard_b = (jnp.concatenate([shards[1, i : i + HALF], shards[2, i : i + HALF]]) for i in (0, HALF))
    where = lax.axis_index("tree").astype(jnp.int32)
    me = where.reshape(1)
    flipped = jnp.concatenate([bucket_table[::-1], jnp.full((1,), -1, jnp.int32)])
    onehot = (flipped[None, :] == jnp.arange(BUCKETS, dtype=jnp.int32)[:, None]).astype(F32)
    table = jnp.dot(rel_bias.T, onehot, precision=lax.Precision.HIGHEST).reshape(PAIRS, 2, SPAN)

    toep = toeplitz_call(table)

    grad_other = swap(out_grad, CORE)
    line_w = gather_z(shards[0])
    line_w = line_w[:1] + tie(line_w[1:], [toep, grad_other])
    halves_w = gather_halves(line_w)
    turned_w = gather_plane(halves_w)
    (shard_a,) = tie([shard_a], halves_w)
    line_a = gather_z(shard_a)
    near_w = gather_near(halves_w, turned_w)
    far_w = gather_far(near_w)
    near_c = gather_core(tie(near_w, line_a[1:]))
    far_c = gather_core(far_w)
    halves_a = tie(gather_halves(line_a), near_c + far_w)
    turned_a = gather_plane(halves_a)
    (shard_b,) = tie([shard_b], near_c + far_w)
    line_b = gather_z(shard_b)
    own_w, other_w = gathered(near_w, far_w), gathered(near_c, far_c)
    (late_input,) = tie([layer_input], halves_a)
    normed, packed, attn_weight, stats, mixed_first = first_forward_call(
        me, bucket_len, item_count, own_w + other_w, toep, late_input, gains
    )
    turned_a, line_b = tie(turned_a, [normed]), line_b[:1] + tie(line_b[1:], [normed])
    near_a = gather_near(halves_a, turned_a)
    far_a = gather_far(near_a)
    halves_b = gather_halves(line_b)
    (mixed_first,) = tie([mixed_first], near_a + halves_b)
    turned_b = gather_plane(halves_b)
    lse, mixed, middle, second = last_forward_call(
        bucket_len, item_count, layer_input, gains, mixed_first, stats, toep, attn_weight, packed
    )

    own_a = gathered(near_a, tie(far_a, [lse]))
    (second,) = tie([second], far_a)
    second_other = swap(second, CORE)
    back_other, hidden_oa, dpre_oa = feed_call(own_a, second_other, grad_other)
    turned_b = tie(turned_b, [dpre_oa])
    near_b = gather_near(halves_b, turned_b)
    far_b = gather_far(near_b)
    (second_a,) = tie([second], [dpre_oa] + near_b)
    back, hidden_a, grad_a, *send_a = feed_sum_call(
        own_a, second_a, out_grad, second_other, grad_other, hidden_oa, dpre_oa
    )
    far_b = tie(far_b, [back])
    own_b = gathered(near_b, far_b)
    (second_other_b,) = tie([second_other], list(send_a) + far_b)
    got_a = swap_plane(send_a)
    back_other, hidden_ob, dpre_ob = feed_call(own_b, second_other_b, grad_other, back_other)
    back_got = swap(back_other, CORE)
    (second_b,) = tie([second], [dpre_ob])
    back, hidden_b, grad_b, *send_b = feed_sum_call(
        own_b, second_b, out_grad, second_other_b, grad_other, hidden_ob, dpre_ob, back
    )

    got_b = swap_plane(send_b)
    (back,) = tie([back], send_b + got_a + [back_got])
    dgain_two, first_d, delta, diag_a, dmiddle, dmixed, grad_out = first_back_call(
        bucket_len, item_count, back, back_got, middle, out_grad, mixed, gains, lse, toep, attn_weight, packed
    )
    got_b = tie(got_b, [dmixed])
    keep_f, send_f = feed_rest_call([grad_a, grad_b], got_a + got_b)
    (dmixed,) = tie([dmixed], send_f)
    got_f = swap_rest(send_f)
    last_d, dgain_one, diag_b, mine_w, other_w = last_back_call(
        me, bucket_len, item_count, lse, delta, gains, toep, normed, first_d, grad_out, packed, dmixed, attn_weight
    )

    got_f = tie(got_f, [last_d])
    (other_w,) = tie([other_w], got_f)
    core_w = swap(other_w, CORE)
    keep_f, send_f = reduce_line(keep_f, got_f)
    (core_w,) = tie([core_w], send_f)
    send_w = plane_call(mine_w, core_w)
    got_w = swap_plane(send_w)
    send_f = tie(send_f, send_w)
    got_f = swap_line(send_f)
    (diag_a,) = tie([diag_a], send_f)
    lines = fold_call(diag_a, diag_b)
    bias_local = jnp.dot(onehot, lines.reshape(HEADS, SPAN).T, precision=lax.Precision.HIGHEST)
    small = jnp.concatenate([dgain_one.reshape(-1), dgain_two.reshape(-1), bias_local.reshape(-1)]).reshape(-1, 128)
    downs = own_a[2:] + own_b[2:]
    (hidden_late,) = tie([hidden_oa], [small])
    output_other = output_call([hidden_late, hidden_ob], downs)
    got_w = tie(got_w, [output_other])
    keep_w, send_w = rest_call(mine_w, core_w, got_w)
    got_w = swap_rest(send_w)
    (last_e,) = tie([last_d], send_w)
    input_grad = input_back_call(first_d, last_e, layer_input, dmiddle, gains, attn_weight)
    (small, *got_f) = tie([small] + got_f, [input_grad])
    got_w = tie(got_w, [input_grad])
    small_got = swap(small, CORE)
    (got_w[0],) = tie(got_w[:1], [small])
    keep_w, send_w = reduce_line(keep_w, got_w)
    (small_got,) = tie([small_got], send_w)
    small = small + small_got
    small_got = swap(small, X)
    got_w = swap_line(send_w)
    (output_other,) = tie([output_other], send_w)
    output_got = swap(output_other, CORE)
    (hidden_last,) = tie([hidden_a], [small] + list(send_w))
    layer_output = output_call([hidden_last, hidden_b], downs, (middle, output_got), BF16)
    (small_got, *got_w) = tie([small_got] + got_w, [layer_output])
    small = small + small_got
    small = small + swap(small, Y)
    small = small + swap(small, Z)
    small = (small + swap(small, 2 * Z)).reshape(-1)
    sum_f, sum_w = reduced(keep_f, got_f), reduced(keep_w, got_w)
    sum_f = sum_f.swapaxes(0, 1)

    summed = jnp.concatenate([sum_w.reshape(1, SHARD, D), sum_f.reshape(2, SHARD, D)])
    if rest > 1:
        small = lax.psum(small, "rest")
        summed = lax.psum_scatter(summed, "rest", scatter_dimension=1, tiled=True)
    gain_grad = small[: 2 * D].reshape(2, D)
    bias_grad = small[2 * D :].reshape(BUCKETS, HEADS)
    mat_grad = jnp.swapaxes(summed, 1, 2)
    mat_new, mat_first_new, mat_second_new = adam_update(
        matrices, mat_grad, mat_first, mat_second, RATE
    )
    mat_ema_new = EMA_KEEP * mat_ema + (1.0 - EMA_KEEP) * mat_new
    gain_new, gain_first_new, gain_second_new = adam_update(
        gains, gain_grad, gain_first, gain_second, RATE_SMALL
    )
    bias_new, bias_first_new, bias_second_new = adam_update(
        rel_bias, bias_grad, bias_first, bias_second, RATE_SMALL
    )
    return (
        layer_output, input_grad, mat_grad, mat_new, mat_first_new, mat_second_new, mat_ema_new,
        gain_grad, gain_new, gain_first_new, gain_second_new,
        bias_grad, bias_new, bias_first_new, bias_second_new,
    )


def solution(mesh):
    fine = Mesh(mesh.devices.reshape(32, -1), AXES)
    rows = P(AXES, None)
    columns = P(None, None, AXES)
    return jax.shard_map(
        on_device,
        mesh=fine,
        in_specs=(rows, rows) + (columns,) * 4 + (P(),) * 6 + (P(AXES), P(AXES), P()),
        out_specs=(rows, rows) + (columns,) * 5 + (P(),) * 8,
        check_vma=False,
    )
```

```python
import functools

import jax
import jax.numpy as jnp
from jax import lax
from jax.experimental import pallas as pl
from jax.experimental.pallas import tpu as pltpu
from jax.sharding import Mesh, PartitionSpec as P

D = 768
FF = 3072
HEADS = 12
HD = 64
BUCKETS = 32
ROW = 512
STEP = 10
PAIRS = HEADS // 2
WIDE = 2 * HD
SUB = 128
QB = 256
SPAN = 1024
TOEP = 896

EPS = 1e-06
RATE = 0.05
RATE_SMALL = 0.5
BETA_ONE = 0.9
BETA_TWO = 0.999
ADAM_EPS = 1e-08
DECAY = 0.1
EMA_KEEP = 0.75

F32 = jnp.float32
BF16 = jnp.bfloat16
TILE = 256
SHARD = 96
HALF = 48
PIECES = 8
AHEAD = 3
FIRST = 4

NN = (((1,), (0,)), ((), ()))
NT = (((1,), (1,)), ((), ()))
TN = (((0,), (0,)), ((), ()))


def dot(left, right, dims):
    return lax.dot_general(left, right, dims, preferred_element_type=F32)


def params(mebibytes=56):
    return pltpu.CompilerParams(vmem_limit_bytes=mebibytes * 1024 * 1024)


def cost(flops, moved, special=0):
    return pl.CostEstimate(flops=int(flops), bytes_accessed=int(moved), transcendentals=int(special))


def whole(shape):
    return pl.BlockSpec(shape, lambda *_: (0,) * len(shape))


def tiles(rows, columns):
    return pl.BlockSpec((rows, columns), lambda i, *_: (i, 0))


def piece_block():
    return pl.BlockSpec((8 * HALF, D), lambda i: (0, 0), pipeline_mode=pl.Buffered(1))


def toeplitz_kernel(table_ref, out_ref):
    for h in range(2):
        line = jnp.broadcast_to(table_ref[0, h : h + 1, :], (SUB, SPAN))
        rolled = pltpu.roll(line, SPAN - (SUB - 1), 1, stride=1, stride_axis=0)
        out_ref[0, h] = rolled[:, :TOEP]


def toeplitz_call(table):
    return pl.pallas_call(
        toeplitz_kernel,
        grid=(PAIRS,),
        in_specs=[pl.BlockSpec((1, 2, SPAN), lambda p: (p, 0, 0))],
        out_specs=pl.BlockSpec((1, 2, SUB, TOEP), lambda p: (p, 0, 0, 0)),
        out_shape=jax.ShapeDtypeStruct((PAIRS, 2, SUB, TOEP), F32),
        compiler_params=params(16),
        cost_estimate=cost(1e6, 6e6),
        name="toeplitz",
    )(table)


def head_masks():
    lane = lax.broadcasted_iota(jnp.int32, (1, WIDE), 1)
    return [(lane < HD).astype(BF16), (lane >= HD).astype(BF16)]


def bias_block(toep, pair, h, first, rows, span):
    parts = []
    for t in range(rows // SUB):
        left = ROW - SUB - first - t * SUB
        parts.append(toep[pair, h, :, left : left + span])
    return parts[0] if len(parts) == 1 else jnp.concatenate(parts, axis=0)


def blocks_of(span):
    rows = min(span, QB)
    return [(start, first, rows) for start in range(0, ROW, span) for first in range(0, span, rows)]


def live_rows(live, first, rows):
    return first + lax.broadcasted_iota(jnp.int32, (rows, 1), 0) < live


def attend(pairs, offset, rows, len_ref, count_ref, packed, toep, mixed_ref, lse_ref):
    masks = head_masks()
    lane = lax.broadcasted_iota(jnp.int32, (1, WIDE), 1)

    @pl.loop(0, pairs)
    def _(pair):
        @pl.loop(0, rows)
        def _(row):
            length = len_ref[row]
            live = length * count_ref[row]
            at = pl.ds(pl.multiple_of(row * ROW, ROW), ROW)
            cols = columns_of(pair, (0, packed.shape[1] // 3 // WIDE, packed.shape[1] // 3 * 2 // WIDE))
            to = columns_of(pair, (offset,))[0]

            def body(span):
                q_all, k_all, v_all = (packed[at, c] for c in cols)
                stats_all = lse_ref[at, :]
                spots = blocks_of(span)
                keys = [k_all * m for m in masks]
                vals = [v_all * m for m in masks]
                both = [(spot, h) for spot in spots for h in range(2)]
                scores = [
                    dot(q_all[start + first : start + first + rows], keys[h][start : start + span], NT)
                    + bias_block(toep, pair, h, first, rows, span)
                    for (start, first, rows), h in both
                ]
                tops = [jnp.max(s, axis=-1, keepdims=True) for s in scores]
                exps = [jnp.exp(s - top) for s, top in zip(scores, tops)]
                totals = [jnp.sum(e, axis=-1, keepdims=True) for e in exps]
                outs_h = [
                    dot(e.astype(BF16), vals[h][start : start + span], NN) * (1.0 / total)
                    for e, total, ((start, first, rows), h) in zip(exps, totals, both)
                ]
                mixed_parts, stats_parts = [], []
                for i, (start, first, rows) in enumerate(spots):
                    mixed = outs_h[2 * i] + outs_h[2 * i + 1]
                    stats = stats_all[start + first : start + first + rows]
                    for h in range(2):
                        head = (pair + offset) * 2 + h
                        stats = jnp.where(lane == head, tops[2 * i + h] + jnp.log(totals[2 * i + h]), stats)
                    if span < ROW:
                        mixed = jnp.where(live_rows(live, start + first, rows), mixed, 0.0)
                    mixed_parts.append(mixed.astype(BF16))
                    stats_parts.append(stats)
                mixed_ref[at, to] = jnp.concatenate(mixed_parts, axis=0)
                lse_ref[at, :] = jnp.concatenate(stats_parts, axis=0)

            for span in (ROW, ROW // 2, ROW // 4):
                pl.when(length == span)(functools.partial(body, span))


def first_forward_kernel(me_ref, len_ref, count_ref, *refs):
    pieces = refs[:PIECES]
    (
        toep_in, x_ref, gain_ref, normed_out, packed_out, weight_out, lse_ref, mixed_ref,
        weight, normed, packed, toep, in_sem, out_sem, toep_sem,
    ) = refs[PIECES:]
    bias_copy = pltpu.make_async_copy(toep_in.at[pl.ds(0, AHEAD)], toep, toep_sem)
    copies = []
    for i, ref in enumerate(pieces):
        core, half, far = i // 4, i // 2 % 2, i % 2
        for j in range(8):
            near, z = j // 4, j % 4
            plane = near * 2 + far if half == 0 else far * 2 + near
            owner = me_ref[0] ^ (z * 8 + plane * 2 + core)
            row = pl.multiple_of(owner * SHARD + half * HALF, 16)
            copies.append(
                pltpu.make_async_copy(ref.at[pl.ds(j * HALF, HALF)], weight.at[pl.ds(row, HALF)], in_sem)
            )
    for copy in copies:
        copy.start()
    bias_copy.start()
    tokens = x_ref.shape[0]

    @pl.loop(0, tokens // TILE)
    def _(tile):
        at = pl.ds(pl.multiple_of(tile * TILE, TILE), TILE)
        x = x_ref[at, :].astype(F32)
        scale = lax.rsqrt(jnp.mean(x * x, axis=-1, keepdims=True) + EPS)
        normed[at, :] = (x * scale * gain_ref[0:1, :]).astype(BF16)

    for copy in copies:
        copy.wait()
    outs = [
        pltpu.make_async_copy(weight, weight_out, out_sem.at[0]),
        pltpu.make_async_copy(normed, normed_out, out_sem.at[1]),
        pltpu.make_async_copy(packed, packed_out, out_sem.at[2]),
    ]
    outs[0].start()
    outs[1].start()

    @pl.loop(0, tokens // TILE)
    def _(tile):
        at = pl.ds(pl.multiple_of(tile * TILE, TILE), TILE)
        for part in range(3):
            cols = slice(part * D, (part + 1) * D)
            packed[at, cols] = dot(normed[at, :], weight[cols, :], NT).astype(BF16)

    outs[2].start()
    lse_ref[...] = jnp.zeros_like(lse_ref)
    bias_copy.wait()
    attend(AHEAD, 0, tokens // ROW, len_ref, count_ref, packed, toep, mixed_ref, lse_ref)
    for copy in outs:
        copy.wait()


def first_forward_call(me, lengths, counts, pieces, toep, x, gains):
    tokens = x.shape[0]
    anywhere = pl.BlockSpec(memory_space=pl.ANY)
    inside = pl.BlockSpec(memory_space=pltpu.VMEM)
    return pl.pallas_call(
        first_forward_kernel,
        grid_spec=pltpu.PrefetchScalarGridSpec(
            num_scalar_prefetch=3,
            grid=(),
            in_specs=[anywhere] * (PIECES + 1) + [inside] * 2,
            out_specs=[anywhere] * 3 + [inside] * 2,
            scratch_shapes=[
                pltpu.VMEM((4 * D, D), BF16),
                pltpu.VMEM((tokens, D), BF16),
                pltpu.VMEM((tokens, 3 * D), BF16),
                pltpu.VMEM((AHEAD, 2, SUB, TOEP), F32),
                pltpu.SemaphoreType.DMA,
                pltpu.SemaphoreType.DMA((3,)),
                pltpu.SemaphoreType.DMA,
            ],
        ),
        out_shape=[
            jax.ShapeDtypeStruct((tokens, D), BF16),
            jax.ShapeDtypeStruct((tokens, 3 * D), BF16),
            jax.ShapeDtypeStruct((4 * D, D), BF16),
            jax.ShapeDtypeStruct((tokens, WIDE), F32),
            jax.ShapeDtypeStruct((tokens, AHEAD * WIDE), BF16),
        ],
        compiler_params=params(56),
        cost_estimate=cost(12e9, 30e6, 4e6),
        name="first_forward",
    )(me, lengths, counts, *pieces, toep, x, gains)


def last_forward_kernel(
    len_ref, count_ref, x_ref, gain_ref, first_ref, stats_ref, toep_in, weight_in, packed_in,
    lse_ref, mixed_ref, middle_out, second_out,
    weight, packed, middle_s, second_s, toep, in_sems, out_sems,
):
    tokens = x_ref.shape[0]
    start = AHEAD * WIDE
    width = D - start
    copies = [
        pltpu.make_async_copy(weight_in.at[pl.ds(3 * D, D)], weight, in_sems.at[0]),
        pltpu.make_async_copy(toep_in.at[pl.ds(AHEAD, PAIRS - AHEAD)], toep, in_sems.at[4]),
    ]
    for part in range(3):
        copies.append(
            pltpu.make_async_copy(
                packed_in.at[:, pl.ds(part * D + start, width)], packed.at[:, pl.ds(part * width, width)], in_sems.at[1 + part]
            )
        )
    for copy in copies:
        copy.start()
    lse_ref[...] = stats_ref[...]
    mixed_ref[:, :start] = first_ref[...]
    for copy in copies[1:]:
        copy.wait()
    attend(PAIRS - AHEAD, AHEAD, tokens // ROW, len_ref, count_ref, packed, toep, mixed_ref, lse_ref)
    copies[0].wait()
    outs = []
    for tile in range(tokens // TILE):
        at = pl.ds(tile * TILE, TILE)
        middle = x_ref[at, :].astype(F32) + dot(mixed_ref[at, :], weight[...], NT)
        middle_s[at, :] = middle
        scale = lax.rsqrt(jnp.mean(middle * middle, axis=-1, keepdims=True) + EPS)
        second_s[at, :] = (middle * scale * gain_ref[1:2, :]).astype(BF16)
        for i, (src, dst) in enumerate(((middle_s, middle_out), (second_s, second_out))):
            copy = pltpu.make_async_copy(src.at[at], dst.at[at], out_sems.at[2 * tile + i])
            copy.start()
            outs.append(copy)
    for copy in outs:
        copy.wait()


def last_forward_call(lengths, counts, x, gains, first, stats, toep, weight, packed):
    tokens = x.shape[0]
    anywhere = pl.BlockSpec(memory_space=pl.ANY)
    inside = pl.BlockSpec(memory_space=pltpu.VMEM)
    flat = jax.ShapeDtypeStruct((tokens, D), BF16)
    return pl.pallas_call(
        last_forward_kernel,
        grid_spec=pltpu.PrefetchScalarGridSpec(
            num_scalar_prefetch=2,
            grid=(),
            in_specs=[inside] * 4 + [anywhere] * 3,
            out_specs=[inside] * 2 + [anywhere] * 2,
            scratch_shapes=[
                pltpu.VMEM((D, D), BF16),
                pltpu.VMEM((tokens, 3 * (PAIRS - AHEAD) * WIDE), BF16),
                pltpu.VMEM((tokens, D), F32),
                pltpu.VMEM((tokens, D), BF16),
                pltpu.VMEM((PAIRS - AHEAD, 2, SUB, TOEP), F32),
                pltpu.SemaphoreType.DMA((5,)),
                pltpu.SemaphoreType.DMA((2 * tokens // TILE,)),
            ],
        ),
        out_shape=[
            jax.ShapeDtypeStruct((tokens, WIDE), F32),
            flat,
            jax.ShapeDtypeStruct((tokens, D), F32),
            flat,
        ],
        compiler_params=params(56),
        cost_estimate=cost(8e9, 20e6, 4e6),
        name="last_forward",
    )(lengths, counts, x, gains, first, stats, toep, weight, packed)


def fold_kernel(first_ref, last_ref, out_ref):
    def fold(ref):
        total = jnp.concatenate([ref[0], jnp.zeros((2, SUB, SPAN - TOEP), F32)], axis=2)
        height = SUB
        while height > 8:
            height //= 2
            total = pltpu.roll(total[:, :height], height, 2) + total[:, height:]
        line = total[:, 7]
        for r in range(7):
            line = line + pltpu.roll(total, 7 - r, 2)[:, r]
        out_ref[0] = line

    pl.when(pl.program_id(0) < FIRST)(functools.partial(fold, first_ref))
    pl.when(pl.program_id(0) >= FIRST)(functools.partial(fold, last_ref))


def fold_call(first, last):
    def block(start, count):
        return pl.BlockSpec((1, 2, SUB, TOEP), lambda p: (jnp.clip(p - start, 0, count - 1), 0, 0, 0))

    return pl.pallas_call(
        fold_kernel,
        grid=(PAIRS,),
        in_specs=[block(0, FIRST), block(FIRST, PAIRS - FIRST)],
        out_specs=pl.BlockSpec((1, 2, SPAN), lambda p: (p, 0, 0)),
        out_shape=jax.ShapeDtypeStruct((PAIRS, 2, SPAN), F32),
        compiler_params=params(62),
        cost_estimate=cost(1e6, 6e6),
        name="fold",
    )(first, last)


def attend_back(
    pairs, offset, me_rows, len_ref, count_ref, cols_of, packed, dmixed, lse_ref, delta_ref, toep, diag, out_ref,
    diag_out, diag_sems,
):
    masks = head_masks()
    lane = lax.broadcasted_iota(jnp.int32, (1, WIDE), 1)

    @pl.loop(0, pairs)
    def _(pair):
        diag[pair] = jnp.zeros((2, SUB, TOEP), F32)

        @pl.loop(0, me_rows)
        def _(row):
            length = len_ref[row]
            live = length * count_ref[row]
            at = pl.ds(pl.multiple_of(row * ROW, ROW), ROW)
            cols = cols_of(pair)

            def body(span):
                q_all, k_all, v_all = (packed[at, c] for c in cols[:3])
                do_all = dmixed[at, cols[3]]
                if span < ROW:
                    do_all = jnp.where(live_rows(live, 0, ROW), do_all.astype(F32), 0.0).astype(BF16)
                stats = lse_ref[at, :]
                spots = blocks_of(span)
                queries, keys, vals, dos = ([a * m for m in masks] for a in (q_all, k_all, v_all, do_all))
                lses, sums = (
                    [jnp.sum(jnp.where(lane == (pair + offset) * 2 + h, a, 0.0), axis=-1, keepdims=True) for h in range(2)]
                    for a in (stats, delta_ref[at, :])
                )
                both = [(spot, h) for spot in spots for h in range(2)]

                def rows_of(value, spot):
                    return value[spot[0] + spot[1] : spot[0] + spot[1] + spot[2]]

                def keys_of(value, spot):
                    return value[spot[0] : spot[0] + span]

                scores = [
                    dot(rows_of(q_all, spot), keys_of(keys[h], spot), NT) + bias_block(toep, pair, h, spot[1], spot[2], span)
                    for spot, h in both
                ]
                dps = [dot(rows_of(do_all, spot), keys_of(vals[h], spot), NT) for spot, h in both]
                probs = [jnp.exp(s - rows_of(lses[h], spot)) for s, (spot, h) in zip(scores, both)]
                dss = [p * (dp - rows_of(sums[h], spot)) for p, dp, (spot, h) in zip(probs, dps, both)]
                for ds, (spot, h) in zip(dss, both):
                    for sub in range(spot[2] // SUB):
                        left = ROW - SUB - spot[1] - sub * SUB
                        diag[pair, h, :, left : left + span] += ds[sub * SUB : (sub + 1) * SUB]
                lows = [ds.astype(BF16) for ds in dss]
                plows = [p.astype(BF16) for p in probs]
                dqs = [dot(low, keys_of(keys[h], spot), NN) for low, (spot, h) in zip(lows, both)]
                dks = [dot(low, rows_of(queries[h], spot), TN) for low, (spot, h) in zip(lows, both)]
                dvs = [dot(low, rows_of(dos[h], spot), TN) for low, (spot, h) in zip(plows, both)]
                dq = jnp.concatenate([dqs[2 * i] + dqs[2 * i + 1] for i in range(len(spots))], axis=0)
                each = len(both) * span // ROW
                dk, dv = (
                    jnp.concatenate([sum(d[i + 1 : i + each], d[i]) for i in range(0, len(both), each)], axis=0)
                    for d in (dks, dvs)
                )
                for part, value in enumerate((dq, dk, dv)):
                    to = pl.ds(pl.multiple_of(pair * WIDE + part * pairs * WIDE, WIDE), WIDE)
                    out_ref[at, to] = value.astype(BF16)

            for span in (ROW, ROW // 2, ROW // 4):
                pl.when(length == span)(functools.partial(body, span))

        pltpu.make_async_copy(diag.at[pair], diag_out.at[pair], diag_sems.at[pair]).start()

    for pair in range(pairs):
        pltpu.make_async_copy(diag.at[pair], diag_out.at[pair], diag_sems.at[pair]).wait()


def columns_of(pair, widths):
    return [pl.ds(pl.multiple_of((pair + w) * WIDE, WIDE), WIDE) for w in widths]


def first_back_kernel(
    len_ref, count_ref, gain_ref, mixed_in, lse_in, part_in, got_in, middle_in, grad_in, toep_in, weight_in, packed_in,
    dgain_ref, out_ref, delta_ref, diag_out, dmiddle_out, dmixed_out, dweight_out,
    part_s, got_s, middle_s, grad_s, mixed_ref, lse_ref, dmixed, dweight, weight, packed, lows, toep, diag,
    in_sems, sems, out_sems, diag_sems,
):
    tokens = mixed_ref.shape[0]
    count = tokens // TILE
    width = FIRST * WIDE
    first = pltpu.make_async_copy(weight_in.at[pl.ds(3 * D, D)], weight, sems.at[0])
    first.start()
    ins = []
    for tile in range(count):
        at = pl.ds(tile * TILE, TILE)
        tiled = ((part_in, part_s), (got_in, got_s), (middle_in, middle_s), (grad_in, grad_s), (mixed_in, mixed_ref))
        for i, (src, dst) in enumerate(tiled):
            copy = pltpu.make_async_copy(src.at[at], dst.at[at], in_sems.at[5 * tile + i])
            copy.start()
            ins.append(copy)
    later = [
        pltpu.make_async_copy(toep_in.at[pl.ds(0, FIRST)], toep, sems.at[4]),
        pltpu.make_async_copy(lse_in, lse_ref, sems.at[5]),
    ]
    for copy in later:
        copy.start()
    for part in range(3):
        copy = pltpu.make_async_copy(
            packed_in.at[:, pl.ds(part * D, width)], packed.at[:, pl.ds(part * width, width)], sems.at[1 + part]
        )
        copy.start()
        later.append(copy)
    first.wait()
    outs = []
    of_feature = lax.broadcasted_iota(jnp.int32, (D, WIDE), 0) // HD
    heads = (of_feature == lax.broadcasted_iota(jnp.int32, (D, WIDE), 1)).astype(BF16)
    dgain = jnp.zeros((1, D), F32)
    for tile in range(count):
        at = pl.ds(tile * TILE, TILE)
        for copy in ins[5 * tile : 5 * tile + 5]:
            copy.wait()
        db = part_s[at, :] + got_s[at, :]
        middle = middle_s[at, :]
        scale = lax.rsqrt(jnp.mean(middle * middle, axis=-1, keepdims=True) + EPS)
        dn = db * gain_ref[1:2, :]
        inner = jnp.mean(dn * middle, axis=-1, keepdims=True)
        dmiddle = grad_s[at, :].astype(F32) + scale * dn - middle * (scale * scale * scale * inner)
        part_s[at, :] = dmiddle
        copy = pltpu.make_async_copy(part_s.at[at], dmiddle_out.at[at], out_sems.at[tile])
        copy.start()
        outs.append(copy)
        low = dmiddle.astype(BF16)
        lows[at, :] = low
        do = dot(low, weight[...], NN).astype(BF16)
        dmixed[at, :] = do
        dgain += jnp.sum(db * middle * scale, axis=0, keepdims=True)
        product = do.astype(F32) * mixed_ref[at, :].astype(F32)
        high = product.astype(BF16)
        delta = dot(high, heads, NN) + dot((product - high.astype(F32)).astype(BF16), heads, NN)
        delta_ref[at, :] = delta
    dgain_ref[...] = dgain
    copy = pltpu.make_async_copy(dmixed, dmixed_out, out_sems.at[count])
    copy.start()
    outs.append(copy)
    dweight[...] = dot(lows[...], mixed_ref[...], TN)
    copy = pltpu.make_async_copy(dweight, dweight_out, out_sems.at[count + 1])
    copy.start()
    outs.append(copy)
    for copy in later:
        copy.wait()

    def cols_of(pair):
        return columns_of(pair, (0, FIRST, 2 * FIRST, 0))

    attend_back(
        FIRST, 0, tokens // ROW, len_ref, count_ref, cols_of, packed, dmixed, lse_ref, delta_ref, toep, diag,
        out_ref, diag_out, diag_sems,
    )
    for copy in outs:
        copy.wait()


def first_back_call(lengths, counts, part, got, middle, out_grad, mixed, gains, lse, toep, weight, packed):
    tokens = part.shape[0]
    anywhere = pl.BlockSpec(memory_space=pl.ANY)
    inside = pl.BlockSpec(memory_space=pltpu.VMEM)
    width = 3 * FIRST * WIDE
    count = tokens // TILE
    return pl.pallas_call(
        first_back_kernel,
        grid_spec=pltpu.PrefetchScalarGridSpec(
            num_scalar_prefetch=2,
            grid=(),
            in_specs=[inside] + [anywhere] * 9,
            out_specs=[inside] * 3 + [anywhere] * 4,
            scratch_shapes=[pltpu.VMEM((tokens, D), F32)] * 3
            + [
                pltpu.VMEM((tokens, D), BF16),
                pltpu.VMEM((tokens, D), BF16),
                pltpu.VMEM((tokens, WIDE), F32),
                pltpu.VMEM((tokens, D), BF16),
                pltpu.VMEM((D, D), F32),
                pltpu.VMEM((D, D), BF16),
                pltpu.VMEM((tokens, width), BF16),
                pltpu.VMEM((tokens, D), BF16),
                pltpu.VMEM((FIRST, 2, SUB, TOEP), F32),
                pltpu.VMEM((FIRST, 2, SUB, TOEP), F32),
                pltpu.SemaphoreType.DMA((5 * count,)),
                pltpu.SemaphoreType.DMA((6,)),
                pltpu.SemaphoreType.DMA((count + 2,)),
                pltpu.SemaphoreType.DMA((FIRST,)),
            ],
        ),
        out_shape=[
            jax.ShapeDtypeStruct((1, D), F32),
            jax.ShapeDtypeStruct((tokens, width), BF16),
            jax.ShapeDtypeStruct((tokens, WIDE), F32),
            jax.ShapeDtypeStruct((FIRST, 2, SUB, TOEP), F32),
            jax.ShapeDtypeStruct((tokens, D), F32),
            jax.ShapeDtypeStruct((tokens, D), BF16),
            jax.ShapeDtypeStruct((D, D), F32),
        ],
        compiler_params=params(62),
        cost_estimate=cost(15e9, 30e6, 7e6),
        name="first_back",
    )(lengths, counts, gains, mixed, lse, part, got, middle, out_grad, toep, weight, packed)


def last_back_kernel(
    me_ref, len_ref, count_ref, lse_ref, delta_ref, gain_ref, toep_in, normed_in, first_in, dout_in, packed_in, dmixed_in, weight_in,
    out_ref, dgain_ref, diag_out, own_out, other_out,
    packed, dmixed, normed, first, weight, dout, total, toep, diag, sems, out_sems, diag_sems,
):
    tokens = normed.shape[0]
    pairs = PAIRS - FIRST
    width = pairs * WIDE
    start = FIRST * WIDE
    copies = [
        pltpu.make_async_copy(dmixed_in.at[:, pl.ds(start, width)], dmixed, sems.at[0]),
        pltpu.make_async_copy(toep_in.at[pl.ds(FIRST, pairs)], toep, sems.at[7]),
    ]
    for part in range(3):
        copies.append(
            pltpu.make_async_copy(
                packed_in.at[:, pl.ds(part * D + start, width)], packed.at[:, pl.ds(part * width, width)], sems.at[1 + part]
            )
        )
    later = [
        pltpu.make_async_copy(normed_in, normed, sems.at[4]),
        pltpu.make_async_copy(first_in, first, sems.at[5]),
        pltpu.make_async_copy(dout_in, dout, sems.at[6]),
        pltpu.make_async_copy(weight_in.at[pl.ds(0, 3 * D)], weight, sems.at[8]),
    ]
    for copy in copies + later:
        copy.start()
    for copy in copies:
        copy.wait()

    def cols_of(pair):
        return columns_of(pair, (0, pairs, 2 * pairs, 0))

    attend_back(
        pairs, FIRST, tokens // ROW, len_ref, count_ref, cols_of, packed, dmixed, lse_ref, delta_ref, toep, diag,
        out_ref, diag_out, diag_sems,
    )
    for copy in later:
        copy.wait()
    total[3 * D :] = dout[...].astype(BF16)
    for part in range(3):
        for at, rows, grads in ((part * D, start, first), (part * D + start, width, out_ref)):
            total[at : at + rows] = dot(grads[:, part * rows : (part + 1) * rows], normed[...], TN).astype(BF16)
    outs = []
    for core, out in ((1, other_out), (0, own_out)):
        for i in range(32):
            half, plane, z = i // 16, i // 4 % 4, i % 4
            owner = me_ref[0] ^ (z * 8 + plane * 2 + core)
            row = pl.multiple_of(owner * SHARD + half * HALF, 16)
            copy = pltpu.make_async_copy(total.at[pl.ds(row, HALF)], out.at[pl.ds(i * HALF, HALF)], out_sems.at[core])
            copy.start()
            outs.append(copy)
    dgain = jnp.zeros((8, D), F32)
    for at in range(0, 3 * D, D // 2):
        product = weight[at : at + D // 2].astype(F32) * total[at : at + D // 2].astype(F32)
        dgain += jnp.sum(product.reshape(D // 16, 8, D), axis=0)
    dgain_ref[...] = jnp.sum(dgain, axis=0, keepdims=True) / gain_ref[0:1, :]
    for copy in outs:
        copy.wait()


def last_back_call(me, lengths, counts, lse, delta, gains, toep, normed, first, grad_out, packed, dmixed, weight):
    tokens = normed.shape[0]
    anywhere = pl.BlockSpec(memory_space=pl.ANY)
    inside = pl.BlockSpec(memory_space=pltpu.VMEM)
    pairs = PAIRS - FIRST
    width = pairs * WIDE
    return pl.pallas_call(
        last_back_kernel,
        grid_spec=pltpu.PrefetchScalarGridSpec(
            num_scalar_prefetch=3,
            grid=(),
            in_specs=[inside] * 3 + [anywhere] * 7,
            out_specs=[inside] * 2 + [anywhere] * 3,
            scratch_shapes=[
                pltpu.VMEM((tokens, 3 * width), BF16),
                pltpu.VMEM((tokens, width), BF16),
                pltpu.VMEM((tokens, D), BF16),
                pltpu.VMEM((tokens, 3 * FIRST * WIDE), BF16),
                pltpu.VMEM((3 * D, D), BF16),
                pltpu.VMEM((D, D), F32),
                pltpu.VMEM((4 * D, D), BF16),
                pltpu.VMEM((pairs, 2, SUB, TOEP), F32),
                pltpu.VMEM((pairs, 2, SUB, TOEP), F32),
                pltpu.SemaphoreType.DMA((9,)),
                pltpu.SemaphoreType.DMA((2,)),
                pltpu.SemaphoreType.DMA((pairs,)),
            ],
        ),
        out_shape=[
            jax.ShapeDtypeStruct((tokens, 3 * width), BF16),
            jax.ShapeDtypeStruct((1, D), F32),
            jax.ShapeDtypeStruct((pairs, 2, SUB, TOEP), F32),
            jax.ShapeDtypeStruct((2 * D, D), BF16),
            jax.ShapeDtypeStruct((2 * D, D), BF16),
        ],
        compiler_params=params(62),
        cost_estimate=cost(10e9, 30e6, 4e6),
        name="last_back",
    )(me, lengths, counts, lse, delta, gains, toep, normed, first, grad_out, packed, dmixed, weight)


def feed_tile(second, grad, up, down):
    u = dot(second, up, NT)
    square = u * u
    t = jnp.tanh(0.7978845608 * u * (1.0 + 0.044715 * square))
    plus = 0.5 * (1.0 + t)
    slope = plus + (0.5 * 0.7978845608) * u * (1.0 - t * t) * (1.0 + 3 * 0.044715 * square)
    dh = dot(grad, down, NT).astype(BF16).astype(F32)
    return (u * plus).astype(BF16), (dh * slope).astype(BF16)


def planes_of(near, far, half):
    rows = 4 * HALF
    near, far = ([value[i : i + rows] for i in (0, rows)] for value in (near, far))
    order = (near[0], far[0], near[1], far[1]) if half == 0 else (near[0], near[1], far[0], far[1])
    return jnp.concatenate(order, axis=0)


def weights_of(refs):
    return [planes_of(refs[2 * half][...], refs[2 * half + 1][...], half) for half in range(2)]


def feed_kernel(parts, *refs):
    up, down = weights_of(refs[:4])
    second_ref, grad_ref, *refs, back_ref, hidden_ref, dpre_ref = refs[4:]
    hidden, du = feed_tile(second_ref[...], grad_ref[...], up, down)
    hidden_ref[...] = hidden
    dpre_ref[...] = du
    back = dot(du, up, NN)
    back_ref[...] = back + refs[0][...] if parts else back


def feed_call(weights, second, out_grad, start=None):
    tokens = second.shape[0]
    flat = tiles(TILE, D)
    low_flat = jax.ShapeDtypeStruct((tokens, D), BF16)
    more = [] if start is None else [start]
    return pl.pallas_call(
        functools.partial(feed_kernel, len(more)),
        grid=(tokens // TILE,),
        in_specs=[piece_block()] * 4 + [flat, flat] + [flat] * len(more),
        out_specs=[flat, flat, flat],
        out_shape=[jax.ShapeDtypeStruct((tokens, D), F32), low_flat, low_flat],
        compiler_params=params(20),
        cost_estimate=cost(6 * tokens * D * D, 15e6, tokens * D),
        name="feed",
    )(*weights, second, out_grad, *more)


def feed_sum_kernel(parts, *refs):
    weights = refs[:4]
    ins = refs[4:10]
    refs = refs[10:]
    start_ref = refs[0] if parts else None
    back_ref, hidden_ref, out_ref, up_send, down_send = refs[parts : parts + 5]
    second, grad, second_other, grad_other, hidden_other, dpre_other, hidden, dpre, tile_sems, sems = refs[parts + 5 :]
    step = pl.program_id(0)
    count = second.shape[0] // TILE

    def tile_copies(tile):
        at = pl.ds(pl.multiple_of(tile * TILE, TILE), TILE)
        return [
            pltpu.make_async_copy(src.at[at], dst.at[at], tile_sems.at[2 * tile + i])
            for i, (src, dst) in enumerate(((ins[0], second), (ins[1], grad)))
        ]

    others = [
        pltpu.make_async_copy(src, dst, sems.at[i])
        for i, (src, dst) in enumerate(zip(ins[2:], (second_other, grad_other, hidden_other, dpre_other)))
    ]

    @pl.when(step == 0)
    def _():
        for tile in range(count):
            for copy in tile_copies(tile):
                copy.start()
        for copy in others:
            copy.start()

    @pl.when(step < count)
    def _():
        at = pl.ds(pl.multiple_of(step * TILE, TILE), TILE)
        for copy in tile_copies(step):
            copy.wait()
        up, down = weights_of(weights)
        low_hidden, du = feed_tile(second[at, :], grad[at, :], up, down)
        hidden_ref[...] = low_hidden
        hidden[at, :] = low_hidden
        dpre[at, :] = du
        back = dot(du, up, NN)
        back_ref[...] = back if start_ref is None else back + start_ref[...]

    @pl.when(step == count)
    def _():
        for copy in others:
            copy.wait()
        total = dot(dpre[...], second[...], TN) + dot(dpre_other[...], second_other[...], TN)
        rows = 4 * HALF
        for x in range(2):
            out_ref[0, x * rows : (x + 1) * rows] = total[2 * x * rows : (2 * x + 1) * rows]
            up_send[x * rows : (x + 1) * rows] = total[(2 * x + 1) * rows : (2 * x + 2) * rows].astype(BF16)

    @pl.when(step == count + 1)
    def _():
        total = dot(hidden[...], grad[...], TN) + dot(hidden_other[...], grad_other[...], TN)
        out_ref[0] = total[: 8 * HALF]
        down_send[...] = total[8 * HALF :].astype(BF16)


def feed_sum_call(weights, second, out_grad, second_other, grad_other, hidden_other, dpre_other, start=None):
    tokens = second.shape[0]
    count = tokens // TILE
    anywhere = pl.BlockSpec(memory_space=pl.ANY)
    tile = pl.BlockSpec((TILE, D), lambda i: (jnp.minimum(i, count - 1), 0))
    more = [] if start is None else [start]
    return pl.pallas_call(
        functools.partial(feed_sum_kernel, len(more)),
        grid=(count + 2,),
        in_specs=[piece_block()] * 4 + [anywhere] * 6 + [tile] * len(more),
        out_specs=[
            tile,
            tile,
            pl.BlockSpec((1, 8 * HALF, D), lambda i: (jnp.maximum(i - count, 0), 0, 0)),
            whole((8 * HALF, D)),
            whole((8 * HALF, D)),
        ],
        out_shape=[
            jax.ShapeDtypeStruct((tokens, D), F32),
            jax.ShapeDtypeStruct((tokens, D), BF16),
            jax.ShapeDtypeStruct((2, 8 * HALF, D), F32),
            jax.ShapeDtypeStruct((8 * HALF, D), BF16),
            jax.ShapeDtypeStruct((8 * HALF, D), BF16),
        ],
        scratch_shapes=[pltpu.VMEM((tokens, D), BF16)] * 8
        + [pltpu.SemaphoreType.DMA((2 * count,)), pltpu.SemaphoreType.DMA((4,))],
        compiler_params=params(56 if more else 36),
        cost_estimate=cost(14 * tokens * D * D, 30e6, tokens * D),
        name="feed_sum",
    )(*weights, second, out_grad, second_other, grad_other, hidden_other, dpre_other, *more)


def output_kernel(*refs):
    total = None
    for i in range(2):
        part = dot(refs[i][...], planes_of(refs[2 + 2 * i][...], refs[3 + 2 * i][...], 1), NN)
        total = part if total is None else total + part
    for ref in refs[6:-1]:
        total += ref[...]
    refs[-1][...] = total.astype(refs[-1].dtype)


def output_call(hiddens, downs, more=(), kind=F32):
    tokens = hiddens[0].shape[0]
    return pl.pallas_call(
        output_kernel,
        grid=(tokens // TILE,),
        in_specs=[tiles(TILE, D)] * 2 + [piece_block()] * 4 + [tiles(TILE, D)] * len(more),
        out_specs=tiles(TILE, D),
        out_shape=jax.ShapeDtypeStruct((tokens, D), kind),
        compiler_params=params(62),
        cost_estimate=cost(4 * tokens * D * D, 12e6),
        name="output",
    )(*hiddens, *downs, *more)


def input_back_kernel(first_ref, last_ref, x_ref, dmiddle_ref, gain_ref, weight_ref, dx_ref):
    da = jnp.zeros(dx_ref.shape, F32)
    cut = FIRST * WIDE
    for part in range(3):
        da += dot(first_ref[:, part * cut : (part + 1) * cut], weight_ref[part * D : part * D + cut, :], NN)
        rest = D - cut
        da += dot(last_ref[:, part * rest : (part + 1) * rest], weight_ref[part * D + cut : (part + 1) * D, :], NN)
    x = x_ref[...].astype(F32)
    scale = lax.rsqrt(jnp.mean(x * x, axis=-1, keepdims=True) + EPS)
    dm = da * gain_ref[0:1, :]
    inner = jnp.mean(dm * x, axis=-1, keepdims=True)
    dx_ref[...] = dmiddle_ref[...] + scale * dm - x * (scale * scale * scale * inner)


def input_back_call(first, last, x, dmiddle, gains, weight):
    tokens = x.shape[0]
    return pl.pallas_call(
        input_back_kernel,
        grid=(tokens // TILE,),
        in_specs=[
            tiles(TILE, first.shape[1]),
            tiles(TILE, last.shape[1]),
            tiles(TILE, D),
            tiles(TILE, D),
            whole((2, D)),
            whole((3 * D, D)),
        ],
        out_specs=tiles(TILE, D),
        out_shape=jax.ShapeDtypeStruct((tokens, D), F32),
        compiler_params=params(62),
        cost_estimate=cost(2 * tokens * D * 3 * D, 18e6),
        name="input_back",
    )(first, last, x, dmiddle, gains, weight)


def adam_update(param, grad, first, second, rate):
    first_new = BETA_ONE * first + (1.0 - BETA_ONE) * grad
    second_new = BETA_TWO * second + (1.0 - BETA_TWO) * grad * grad
    first_hat = first_new / (1.0 - BETA_ONE**STEP)
    second_hat = second_new / (1.0 - BETA_TWO**STEP)
    param_new = param - rate * (first_hat / (jnp.sqrt(second_hat) + ADAM_EPS) + DECAY * param)
    return (param_new, first_new, second_new)


AXES = ("tree", "rest")
CORE, Y, X, Z = 1, 2, 4, 8


def swap(value, bits):
    return lax.ppermute(value, "tree", [(i, i ^ bits) for i in range(32)])


def tie(values, after):
    return list(lax.optimization_barrier(tuple(values) + tuple(after))[: len(values)])


def gather_z(shard):
    return [shard] + [swap(shard, k * Z) for k in (1, 2, 3)]


def gather_halves(line, first=0):
    return [jnp.concatenate([p[i : i + HALF] for p in line]) for i in (first, first + HALF)]


def gather_plane(halves):
    return [swap(halves[0], X), swap(halves[1], Y)]


def gather_near(halves, turned):
    return [jnp.concatenate([half, got]) for half, got in zip(halves, turned)]


def gather_far(near):
    return [swap(near[0], Y), swap(near[1], X)]


def gathered(near, far):
    return [near[0], far[0], near[1], far[1]]


def gather_core(pieces):
    return [swap(p, CORE) for p in pieces]


def low(value):
    return value.astype(BF16)


def swap_plane(sends):
    return [swap(sends[0], Y), swap(sends[1], X)]


def swap_rest(sends):
    return [swap(sends[0], X), swap(sends[1], Y)]


def feed_rest_kernel(*refs):
    grads, gots, outs = refs[:4], refs[4:8], refs[8:]
    for step in range(2):

        @pl.when(pl.program_id(0) == step)
        def _(step=step):
            for chunk in range(2):
                for half in range(2):
                    i = 2 * chunk + half
                    out = outs[2 * step + half]
                    out[chunk] = (grads[i][0] + gots[i][...].astype(F32)).astype(out.dtype)


def feed_rest_call(grads, gots):
    rows = 4 * HALF
    shape = (2, rows, D)
    outs = pl.pallas_call(
        feed_rest_kernel,
        grid=(2,),
        in_specs=[pl.BlockSpec((1, rows, D), lambda i, h=h: (h, 1 - i, 0)) for _ in range(2) for h in range(2)]
        + [pl.BlockSpec((rows, D), lambda i: (1 - i, 0))] * 4,
        out_specs=[whole(shape)] * 4,
        out_shape=[jax.ShapeDtypeStruct(shape, kind) for kind in (BF16, BF16, F32, F32)],
        compiler_params=params(62),
        cost_estimate=cost(1e6, 10e6),
        name="feed_rest",
    )(*[grads[0]] * 2, *[grads[1]] * 2, *gots)
    return outs[2:], outs[:2]


def plane_kernel(*refs):
    for half, out in enumerate(refs[8:]):
        for i in range(2):
            value = refs[4 * half + i][...].astype(F32) + refs[4 * half + 2 + i][...].astype(F32)
            out[i * 4 * HALF : (i + 1) * 4 * HALF] = value.astype(BF16)


def plane_call(own, got):
    rows = 4 * HALF

    def blocks(*places):
        return [pl.BlockSpec((rows, D), lambda i, p=p: (p, 0)) for p in places]

    return pl.pallas_call(
        plane_kernel,
        grid=(1,),
        in_specs=blocks(1, 3, 1, 3, 6, 7, 6, 7),
        out_specs=[whole((2 * rows, D))] * 2,
        out_shape=[jax.ShapeDtypeStruct((2 * rows, D), BF16)] * 2,
        compiler_params=params(62),
        cost_estimate=cost(1e6, 5e6),
        name="plane",
    )(own, own, got, got, own, own, got, got)


def rest_kernel(*refs):
    owns, cores, gots, outs = refs[:4], refs[4:8], refs[8:10], refs[10:]
    rows = 4 * HALF
    for half in range(2):
        for far in range(2):
            i = 2 * half + far
            value = owns[i][...].astype(F32) + cores[i][...].astype(F32)
            value += gots[half][far * rows : (far + 1) * rows].astype(F32)
            out = outs[2 * far + half]
            out[...] = value.astype(out.dtype)


def rest_call(own, core, gots):
    rows = 4 * HALF
    blocks = [pl.BlockSpec((rows, D), lambda i, p=p: (p, 0)) for p in (0, 2, 4, 5)]
    outs = pl.pallas_call(
        rest_kernel,
        grid=(1,),
        in_specs=blocks * 2 + [whole((2 * rows, D))] * 2,
        out_specs=[whole((rows, D))] * 4,
        out_shape=[jax.ShapeDtypeStruct((rows, D), kind) for kind in (F32, F32, BF16, BF16)],
        compiler_params=params(62),
        cost_estimate=cost(1e6, 7e6),
        name="rest",
    )(*[own] * 4, *[core] * 4, *gots)
    return outs[:2], outs[2:]


def line_kernel(one_ref, two_ref, got_one, got_two, *outs):
    for k, out in enumerate(outs):
        at = slice(k * HALF, (k + 1) * HALF)
        for chunk in range(one_ref.shape[0]):
            for half, (ref, got) in enumerate(((one_ref, got_one), (two_ref, got_two))):
                out[chunk, half] = (ref[chunk, at] + got[chunk, at].astype(F32)).astype(out.dtype)


def reduce_line(keep, got):
    chunks = keep[0].size // (4 * HALF * D)
    keep, got = ([a.reshape(chunks, 4 * HALF, D) for a in values] for values in (keep, got))
    shape = (chunks, 2, HALF, D)
    outs = pl.pallas_call(
        line_kernel,
        out_shape=[jax.ShapeDtypeStruct(shape, F32)] + [jax.ShapeDtypeStruct(shape, BF16)] * 3,
        compiler_params=params(62),
        cost_estimate=cost(1e6, 6e6),
        name="line",
    )(*keep, *got)
    return outs[0], list(outs[1:])


def feed_line_kernel(one_ref, two_ref, got_one, got_two, keep, send):
    for chunk in range(one_ref.shape[0]):
        for half, (ref, got) in enumerate(((one_ref, got_one), (two_ref, got_two))):
            value = ref[chunk] + got[chunk].astype(F32)
            keep[chunk, half] = value[: 2 * HALF]
            send[chunk, half] = value[2 * HALF :].astype(BF16)


def feed_line_call(keep, got):
    shape = (2, 2, 2 * HALF, D)
    return pl.pallas_call(
        feed_line_kernel,
        out_shape=[jax.ShapeDtypeStruct(shape, F32), jax.ShapeDtypeStruct(shape, BF16)],
        compiler_params=params(62),
        cost_estimate=cost(1e6, 6e6),
        name="feed_line",
    )(*keep, *(g.reshape(2, 4 * HALF, D) for g in got))


def swap_line(sends):
    return [swap(send, k * Z) for k, send in zip((1, 2, 3), sends)]


def reduced(keep, got):
    return keep + got[0].astype(F32) + got[1].astype(F32) + got[2].astype(F32)


def on_device(
    layer_input, out_grad, matrices, mat_first, mat_second, mat_ema, gains, gain_first, gain_second,
    rel_bias, bias_first, bias_second, bucket_len, item_count, bucket_table,
):
    rest = lax.axis_size("rest")
    shards = jnp.swapaxes(matrices, 1, 2).astype(BF16)
    if rest > 1:
        shards = lax.all_gather(shards, "rest", axis=1, tiled=True)
    shard_a, shard_b = (jnp.concatenate([shards[1, i : i + HALF], shards[2, i : i + HALF]]) for i in (0, HALF))
    where = lax.axis_index("tree").astype(jnp.int32)
    me = where.reshape(1)
    flipped = jnp.concatenate([bucket_table[::-1], jnp.full((1,), -1, jnp.int32)])
    onehot = (flipped[None, :] == jnp.arange(BUCKETS, dtype=jnp.int32)[:, None]).astype(F32)
    table = jnp.dot(rel_bias.T, onehot, precision=lax.Precision.HIGHEST).reshape(PAIRS, 2, SPAN)

    toep = toeplitz_call(table)

    grad_other = swap(out_grad, CORE)
    line_w = gather_z(shards[0])
    line_w = line_w[:1] + tie(line_w[1:], [toep, grad_other])
    halves_w = gather_halves(line_w)
    turned_w = gather_plane(halves_w)
    (shard_a,) = tie([shard_a], halves_w)
    line_a = gather_z(shard_a)
    near_w = gather_near(halves_w, turned_w)
    far_w = gather_far(near_w)
    near_c = gather_core(tie(near_w, line_a[1:]))
    far_c = gather_core(far_w)
    halves_a = tie(gather_halves(line_a), near_c + far_w)
    turned_a = gather_plane(halves_a)
    (shard_b,) = tie([shard_b], near_c + far_w)
    line_b = gather_z(shard_b)
    own_w, other_w = gathered(near_w, far_w), gathered(near_c, far_c)
    (late_input,) = tie([layer_input], halves_a)
    normed, packed, attn_weight, stats, mixed_first = first_forward_call(
        me, bucket_len, item_count, own_w + other_w, toep, late_input, gains
    )
    turned_a, line_b = tie(turned_a, [normed]), line_b[:1] + tie(line_b[1:], [normed])
    near_a = gather_near(halves_a, turned_a)
    far_a = gather_far(near_a)
    halves_b = gather_halves(line_b)
    (mixed_first,) = tie([mixed_first], near_a + halves_b)
    turned_b = gather_plane(halves_b)
    lse, mixed, middle, second = last_forward_call(
        bucket_len, item_count, layer_input, gains, mixed_first, stats, toep, attn_weight, packed
    )

    own_a = gathered(near_a, tie(far_a, [lse]))
    (second,) = tie([second], far_a)
    second_other = swap(second, CORE)
    back_other, hidden_oa, dpre_oa = feed_call(own_a, second_other, grad_other)
    turned_b = tie(turned_b, [dpre_oa])
    near_b = gather_near(halves_b, turned_b)
    far_b = gather_far(near_b)
    (second_a,) = tie([second], [dpre_oa] + near_b)
    back, hidden_a, grad_a, *send_a = feed_sum_call(
        own_a, second_a, out_grad, second_other, grad_other, hidden_oa, dpre_oa
    )
    far_b = tie(far_b, [back])
    own_b = gathered(near_b, far_b)
    (second_other_b,) = tie([second_other], list(send_a) + far_b)
    got_a = swap_plane(send_a)
    back_other, hidden_ob, dpre_ob = feed_call(own_b, second_other_b, grad_other, back_other)
    back_got = swap(back_other, CORE)
    (second_b,) = tie([second], [dpre_ob])
    back, hidden_b, grad_b, *send_b = feed_sum_call(
        own_b, second_b, out_grad, second_other_b, grad_other, hidden_ob, dpre_ob, back
    )

    got_b = swap_plane(send_b)
    (back,) = tie([back], send_b + got_a + [back_got])
    dgain_two, first_d, delta, diag_a, dmiddle, dmixed, grad_out = first_back_call(
        bucket_len, item_count, back, back_got, middle, out_grad, mixed, gains, lse, toep, attn_weight, packed
    )
    got_b = tie(got_b, [dmixed])
    keep_f, send_f = feed_rest_call([grad_a, grad_b], got_a + got_b)
    (dmixed,) = tie([dmixed], send_f)
    got_f = swap_rest(send_f)
    last_d, dgain_one, diag_b, mine_w, other_w = last_back_call(
        me, bucket_len, item_count, lse, delta, gains, toep, normed, first_d, grad_out, packed, dmixed, attn_weight
    )

    got_f = tie(got_f, [last_d])
    (other_w,) = tie([other_w], got_f)
    core_w = swap(other_w, CORE)
    keep_f, send_f = feed_line_call(keep_f, got_f)
    (core_w,) = tie([core_w], [send_f])
    send_w = plane_call(mine_w, core_w)
    got_w = swap_plane(send_w)
    (send_f,) = tie([send_f], send_w)
    got_f = swap(send_f, 2 * Z)
    (diag_a,) = tie([diag_a], [send_f])
    lines = fold_call(diag_a, diag_b)
    bias_local = jnp.dot(onehot, lines.reshape(HEADS, SPAN).T, precision=lax.Precision.HIGHEST)
    small = jnp.concatenate([dgain_one.reshape(-1), dgain_two.reshape(-1), bias_local.reshape(-1)]).reshape(-1, 128)
    small_got = swap(small, CORE)
    downs = own_a[2:] + own_b[2:]
    (hidden_late,) = tie([hidden_oa], [small])
    output_other = output_call([hidden_late, hidden_ob], downs)
    (small_got, *got_w) = tie([small_got] + got_w, [output_other])
    small = small + small_got
    small_got = swap(small, Z)
    (got_w[0],) = tie(got_w[:1], [small])
    keep_w, send_w = rest_call(mine_w, core_w, got_w)
    got_w = swap_rest(send_w)
    (last_e,) = tie([last_d], send_w)
    input_grad = input_back_call(first_d, last_e, layer_input, dmiddle, gains, attn_weight)
    (small_got, got_f, *got_w) = tie([small_got, got_f] + got_w, [input_grad])
    small = small + small_got
    small_got = swap(small, 2 * Z)
    (got_w[0],) = tie(got_w[:1], [small])
    keep_w, send_w = reduce_line(keep_w, got_w)
    got_w = swap_line(send_w)
    (got_f,) = tie([got_f], send_w)
    send_f = low(keep_f[:, :, HALF:] + got_f[:, :, HALF:].astype(F32))
    got_line = swap(send_f, Z)
    (small_got, output_other) = tie([small_got, output_other], [send_f])
    output_got = swap(output_other, CORE)
    small = small + small_got
    small_got = swap(small, X)
    (hidden_last,) = tie([hidden_a], [small])
    layer_output = output_call([hidden_last, hidden_b], downs, (middle, output_got), BF16)
    (small_got,) = tie([small_got], [layer_output])
    small = small + small_got
    small_got = swap(small, Y)
    (got_line, *got_w) = tie([got_line] + got_w, [layer_output, small])
    small = (small + small_got).reshape(-1)
    sum_f = keep_f[:, :, :HALF] + got_f[:, :, :HALF].astype(F32) + got_line.astype(F32)
    sum_w = reduced(keep_w, got_w)
    sum_f = sum_f.swapaxes(0, 1)

    summed = jnp.concatenate([sum_w.reshape(1, SHARD, D), sum_f.reshape(2, SHARD, D)])
    if rest > 1:
        small = lax.psum(small, "rest")
        summed = lax.psum_scatter(summed, "rest", scatter_dimension=1, tiled=True)
    gain_grad = small[: 2 * D].reshape(2, D)
    bias_grad = small[2 * D :].reshape(BUCKETS, HEADS)
    mat_grad = jnp.swapaxes(summed, 1, 2)
    mat_new, mat_first_new, mat_second_new = adam_update(
        matrices, mat_grad, mat_first, mat_second, RATE
    )
    mat_ema_new = EMA_KEEP * mat_ema + (1.0 - EMA_KEEP) * mat_new
    gain_new, gain_first_new, gain_second_new = adam_update(
        gains, gain_grad, gain_first, gain_second, RATE_SMALL
    )
    bias_new, bias_first_new, bias_second_new = adam_update(
        rel_bias, bias_grad, bias_first, bias_second, RATE_SMALL
    )
    return (
        layer_output, input_grad, mat_grad, mat_new, mat_first_new, mat_second_new, mat_ema_new,
        gain_grad, gain_new, gain_first_new, gain_second_new,
        bias_grad, bias_new, bias_first_new, bias_second_new,
    )


def solution(mesh):
    fine = Mesh(mesh.devices.reshape(32, -1), AXES)
    rows = P(AXES, None)
    columns = P(None, None, AXES)
    return jax.shard_map(
        on_device,
        mesh=fine,
        in_specs=(rows, rows) + (columns,) * 4 + (P(),) * 6 + (P(AXES), P(AXES), P()),
        out_specs=(rows, rows) + (columns,) * 5 + (P(),) * 8,
        check_vma=False,
    )
```

```python
import functools

import jax
import jax.numpy as jnp
from jax import lax
from jax.experimental import pallas as pl
from jax.experimental.pallas import tpu as pltpu
from jax.sharding import Mesh, PartitionSpec as P

D = 768
FF = 3072
HEADS = 12
HD = 64
BUCKETS = 32
ROW = 512
STEP = 10
PAIRS = HEADS // 2
WIDE = 2 * HD
SUB = 128
QB = 256
SPAN = 1024
TOEP = 896

EPS = 1e-06
RATE = 0.05
RATE_SMALL = 0.5
BETA_ONE = 0.9
BETA_TWO = 0.999
ADAM_EPS = 1e-08
DECAY = 0.1
EMA_KEEP = 0.75

F32 = jnp.float32
BF16 = jnp.bfloat16
TILE = 256
SHARD = 96
HALF = 48
PIECES = 8
AHEAD = 3
FIRST = 4

NN = (((1,), (0,)), ((), ()))
NT = (((1,), (1,)), ((), ()))
TN = (((0,), (0,)), ((), ()))


def dot(left, right, dims):
    return lax.dot_general(left, right, dims, preferred_element_type=F32)


def params(mebibytes=56):
    return pltpu.CompilerParams(vmem_limit_bytes=mebibytes * 1024 * 1024)


def cost(flops, moved, special=0):
    return pl.CostEstimate(flops=int(flops), bytes_accessed=int(moved), transcendentals=int(special))


def whole(shape):
    return pl.BlockSpec(shape, lambda *_: (0,) * len(shape))


def tiles(rows, columns):
    return pl.BlockSpec((rows, columns), lambda i, *_: (i, 0))


def piece_block():
    return pl.BlockSpec((8 * HALF, D), lambda i: (0, 0), pipeline_mode=pl.Buffered(1))


def toeplitz_kernel(table_ref, out_ref):
    for h in range(2):
        line = jnp.broadcast_to(table_ref[0, h : h + 1, :], (SUB, SPAN))
        rolled = pltpu.roll(line, SPAN - (SUB - 1), 1, stride=1, stride_axis=0)
        out_ref[0, h] = rolled[:, :TOEP]


def toeplitz_call(table):
    return pl.pallas_call(
        toeplitz_kernel,
        grid=(PAIRS,),
        in_specs=[pl.BlockSpec((1, 2, SPAN), lambda p: (p, 0, 0))],
        out_specs=pl.BlockSpec((1, 2, SUB, TOEP), lambda p: (p, 0, 0, 0)),
        out_shape=jax.ShapeDtypeStruct((PAIRS, 2, SUB, TOEP), F32),
        compiler_params=params(16),
        cost_estimate=cost(1e6, 6e6),
        name="toeplitz",
    )(table)


def head_masks():
    lane = lax.broadcasted_iota(jnp.int32, (1, WIDE), 1)
    return [(lane < HD).astype(BF16), (lane >= HD).astype(BF16)]


def bias_block(toep, pair, h, first, rows, span):
    parts = []
    for t in range(rows // SUB):
        left = ROW - SUB - first - t * SUB
        parts.append(toep[pair, h, :, left : left + span])
    return parts[0] if len(parts) == 1 else jnp.concatenate(parts, axis=0)


def blocks_of(span):
    rows = min(span, QB)
    return [(start, first, rows) for start in range(0, ROW, span) for first in range(0, span, rows)]


def live_rows(live, first, rows):
    return first + lax.broadcasted_iota(jnp.int32, (rows, 1), 0) < live


def attend(pairs, offset, rows, len_ref, count_ref, packed, toep, mixed_ref, lse_ref):
    masks = head_masks()
    lane = lax.broadcasted_iota(jnp.int32, (1, WIDE), 1)

    @pl.loop(0, pairs)
    def _(pair):
        @pl.loop(0, rows)
        def _(row):
            length = len_ref[row]
            live = length * count_ref[row]
            at = pl.ds(pl.multiple_of(row * ROW, ROW), ROW)
            cols = columns_of(pair, (0, packed.shape[1] // 3 // WIDE, packed.shape[1] // 3 * 2 // WIDE))
            to = columns_of(pair, (offset,))[0]

            def body(span):
                q_all, k_all, v_all = (packed[at, c] for c in cols)
                stats_all = lse_ref[at, :]
                spots = blocks_of(span)
                keys = [k_all * m for m in masks]
                vals = [v_all * m for m in masks]
                both = [(spot, h) for spot in spots for h in range(2)]
                scores = [
                    dot(q_all[start + first : start + first + rows], keys[h][start : start + span], NT)
                    + bias_block(toep, pair, h, first, rows, span)
                    for (start, first, rows), h in both
                ]
                tops = [jnp.max(s, axis=-1, keepdims=True) for s in scores]
                exps = [jnp.exp(s - top) for s, top in zip(scores, tops)]
                totals = [jnp.sum(e, axis=-1, keepdims=True) for e in exps]
                outs_h = [
                    dot(e.astype(BF16), vals[h][start : start + span], NN) * (1.0 / total)
                    for e, total, ((start, first, rows), h) in zip(exps, totals, both)
                ]
                mixed_parts, stats_parts = [], []
                for i, (start, first, rows) in enumerate(spots):
                    mixed = outs_h[2 * i] + outs_h[2 * i + 1]
                    stats = stats_all[start + first : start + first + rows]
                    for h in range(2):
                        head = (pair + offset) * 2 + h
                        stats = jnp.where(lane == head, tops[2 * i + h] + jnp.log(totals[2 * i + h]), stats)
                    if span < ROW:
                        mixed = jnp.where(live_rows(live, start + first, rows), mixed, 0.0)
                    mixed_parts.append(mixed.astype(BF16))
                    stats_parts.append(stats)
                mixed_ref[at, to] = jnp.concatenate(mixed_parts, axis=0)
                lse_ref[at, :] = jnp.concatenate(stats_parts, axis=0)

            for span in (ROW, ROW // 2, ROW // 4):
                pl.when(length == span)(functools.partial(body, span))


def first_forward_kernel(me_ref, len_ref, count_ref, *refs):
    pieces = refs[:PIECES]
    (
        toep_in, x_ref, gain_ref, normed_out, packed_out, weight_out, lse_ref, mixed_ref,
        weight, normed, packed, toep, in_sem, out_sem, toep_sem,
    ) = refs[PIECES:]
    bias_copy = pltpu.make_async_copy(toep_in.at[pl.ds(0, AHEAD)], toep, toep_sem)
    copies = []
    for i, ref in enumerate(pieces):
        core, half, far = i // 4, i // 2 % 2, i % 2
        for j in range(8):
            near, z = j // 4, j % 4
            plane = near * 2 + far if half == 0 else far * 2 + near
            owner = me_ref[0] ^ (z * 8 + plane * 2 + core)
            row = pl.multiple_of(owner * SHARD + half * HALF, 16)
            copies.append(
                pltpu.make_async_copy(ref.at[pl.ds(j * HALF, HALF)], weight.at[pl.ds(row, HALF)], in_sem)
            )
    for copy in copies:
        copy.start()
    bias_copy.start()
    tokens = x_ref.shape[0]

    @pl.loop(0, tokens // TILE)
    def _(tile):
        at = pl.ds(pl.multiple_of(tile * TILE, TILE), TILE)
        x = x_ref[at, :].astype(F32)
        scale = lax.rsqrt(jnp.mean(x * x, axis=-1, keepdims=True) + EPS)
        normed[at, :] = (x * scale * gain_ref[0:1, :]).astype(BF16)

    for copy in copies:
        copy.wait()
    outs = [
        pltpu.make_async_copy(weight, weight_out, out_sem.at[0]),
        pltpu.make_async_copy(normed, normed_out, out_sem.at[1]),
        pltpu.make_async_copy(packed, packed_out, out_sem.at[2]),
    ]
    outs[0].start()
    outs[1].start()

    @pl.loop(0, tokens // TILE)
    def _(tile):
        at = pl.ds(pl.multiple_of(tile * TILE, TILE), TILE)
        for part in range(3):
            cols = slice(part * D, (part + 1) * D)
            packed[at, cols] = dot(normed[at, :], weight[cols, :], NT).astype(BF16)

    outs[2].start()
    lse_ref[...] = jnp.zeros_like(lse_ref)
    bias_copy.wait()
    attend(AHEAD, 0, tokens // ROW, len_ref, count_ref, packed, toep, mixed_ref, lse_ref)
    for copy in outs:
        copy.wait()


def first_forward_call(me, lengths, counts, pieces, toep, x, gains):
    tokens = x.shape[0]
    anywhere = pl.BlockSpec(memory_space=pl.ANY)
    inside = pl.BlockSpec(memory_space=pltpu.VMEM)
    return pl.pallas_call(
        first_forward_kernel,
        grid_spec=pltpu.PrefetchScalarGridSpec(
            num_scalar_prefetch=3,
            grid=(),
            in_specs=[anywhere] * (PIECES + 1) + [inside] * 2,
            out_specs=[anywhere] * 3 + [inside] * 2,
            scratch_shapes=[
                pltpu.VMEM((4 * D, D), BF16),
                pltpu.VMEM((tokens, D), BF16),
                pltpu.VMEM((tokens, 3 * D), BF16),
                pltpu.VMEM((AHEAD, 2, SUB, TOEP), F32),
                pltpu.SemaphoreType.DMA,
                pltpu.SemaphoreType.DMA((3,)),
                pltpu.SemaphoreType.DMA,
            ],
        ),
        out_shape=[
            jax.ShapeDtypeStruct((tokens, D), BF16),
            jax.ShapeDtypeStruct((tokens, 3 * D), BF16),
            jax.ShapeDtypeStruct((4 * D, D), BF16),
            jax.ShapeDtypeStruct((tokens, WIDE), F32),
            jax.ShapeDtypeStruct((tokens, AHEAD * WIDE), BF16),
        ],
        compiler_params=params(56),
        cost_estimate=cost(12e9, 30e6, 4e6),
        name="first_forward",
    )(me, lengths, counts, *pieces, toep, x, gains)


def last_forward_kernel(
    len_ref, count_ref, x_ref, gain_ref, first_ref, stats_ref, toep_in, weight_in, packed_in,
    lse_ref, mixed_ref, middle_out, second_out,
    weight, packed, middle_s, second_s, toep, in_sems, out_sems,
):
    tokens = x_ref.shape[0]
    start = AHEAD * WIDE
    width = D - start
    copies = [
        pltpu.make_async_copy(weight_in.at[pl.ds(3 * D, D)], weight, in_sems.at[0]),
        pltpu.make_async_copy(toep_in.at[pl.ds(AHEAD, PAIRS - AHEAD)], toep, in_sems.at[4]),
    ]
    for part in range(3):
        copies.append(
            pltpu.make_async_copy(
                packed_in.at[:, pl.ds(part * D + start, width)], packed.at[:, pl.ds(part * width, width)], in_sems.at[1 + part]
            )
        )
    for copy in copies:
        copy.start()
    lse_ref[...] = stats_ref[...]
    mixed_ref[:, :start] = first_ref[...]
    for copy in copies[1:]:
        copy.wait()
    attend(PAIRS - AHEAD, AHEAD, tokens // ROW, len_ref, count_ref, packed, toep, mixed_ref, lse_ref)
    copies[0].wait()
    outs = []
    for tile in range(tokens // TILE):
        at = pl.ds(tile * TILE, TILE)
        middle = x_ref[at, :].astype(F32) + dot(mixed_ref[at, :], weight[...], NT)
        middle_s[at, :] = middle
        scale = lax.rsqrt(jnp.mean(middle * middle, axis=-1, keepdims=True) + EPS)
        second_s[at, :] = (middle * scale * gain_ref[1:2, :]).astype(BF16)
        for i, (src, dst) in enumerate(((middle_s, middle_out), (second_s, second_out))):
            copy = pltpu.make_async_copy(src.at[at], dst.at[at], out_sems.at[2 * tile + i])
            copy.start()
            outs.append(copy)
    for copy in outs:
        copy.wait()


def last_forward_call(lengths, counts, x, gains, first, stats, toep, weight, packed):
    tokens = x.shape[0]
    anywhere = pl.BlockSpec(memory_space=pl.ANY)
    inside = pl.BlockSpec(memory_space=pltpu.VMEM)
    flat = jax.ShapeDtypeStruct((tokens, D), BF16)
    return pl.pallas_call(
        last_forward_kernel,
        grid_spec=pltpu.PrefetchScalarGridSpec(
            num_scalar_prefetch=2,
            grid=(),
            in_specs=[inside] * 4 + [anywhere] * 3,
            out_specs=[inside] * 2 + [anywhere] * 2,
            scratch_shapes=[
                pltpu.VMEM((D, D), BF16),
                pltpu.VMEM((tokens, 3 * (PAIRS - AHEAD) * WIDE), BF16),
                pltpu.VMEM((tokens, D), F32),
                pltpu.VMEM((tokens, D), BF16),
                pltpu.VMEM((PAIRS - AHEAD, 2, SUB, TOEP), F32),
                pltpu.SemaphoreType.DMA((5,)),
                pltpu.SemaphoreType.DMA((2 * tokens // TILE,)),
            ],
        ),
        out_shape=[
            jax.ShapeDtypeStruct((tokens, WIDE), F32),
            flat,
            jax.ShapeDtypeStruct((tokens, D), F32),
            flat,
        ],
        compiler_params=params(56),
        cost_estimate=cost(8e9, 20e6, 4e6),
        name="last_forward",
    )(lengths, counts, x, gains, first, stats, toep, weight, packed)


def fold_kernel(first_ref, last_ref, out_ref):
    def fold(ref):
        total = jnp.concatenate([ref[0], jnp.zeros((2, SUB, SPAN - TOEP), F32)], axis=2)
        height = SUB
        while height > 8:
            height //= 2
            total = pltpu.roll(total[:, :height], height, 2) + total[:, height:]
        line = total[:, 7]
        for r in range(7):
            line = line + pltpu.roll(total, 7 - r, 2)[:, r]
        out_ref[0] = line

    pl.when(pl.program_id(0) < FIRST)(functools.partial(fold, first_ref))
    pl.when(pl.program_id(0) >= FIRST)(functools.partial(fold, last_ref))


def fold_call(first, last):
    def block(start, count):
        return pl.BlockSpec((1, 2, SUB, TOEP), lambda p: (jnp.clip(p - start, 0, count - 1), 0, 0, 0))

    return pl.pallas_call(
        fold_kernel,
        grid=(PAIRS,),
        in_specs=[block(0, FIRST), block(FIRST, PAIRS - FIRST)],
        out_specs=pl.BlockSpec((1, 2, SPAN), lambda p: (p, 0, 0)),
        out_shape=jax.ShapeDtypeStruct((PAIRS, 2, SPAN), F32),
        compiler_params=params(62),
        cost_estimate=cost(1e6, 6e6),
        name="fold",
    )(first, last)


def attend_back(
    pairs, offset, me_rows, len_ref, count_ref, cols_of, packed, dmixed, lse_ref, delta_ref, toep, diag, out_ref,
    diag_out, diag_sems,
):
    masks = head_masks()
    lane = lax.broadcasted_iota(jnp.int32, (1, WIDE), 1)

    @pl.loop(0, pairs)
    def _(pair):
        diag[pair] = jnp.zeros((2, SUB, TOEP), F32)

        @pl.loop(0, me_rows)
        def _(row):
            length = len_ref[row]
            live = length * count_ref[row]
            at = pl.ds(pl.multiple_of(row * ROW, ROW), ROW)
            cols = cols_of(pair)

            def body(span):
                q_all, k_all, v_all = (packed[at, c] for c in cols[:3])
                do_all = dmixed[at, cols[3]]
                if span < ROW:
                    do_all = jnp.where(live_rows(live, 0, ROW), do_all.astype(F32), 0.0).astype(BF16)
                stats = lse_ref[at, :]
                spots = blocks_of(span)
                queries, keys, vals, dos = ([a * m for m in masks] for a in (q_all, k_all, v_all, do_all))
                lses, sums = (
                    [jnp.sum(jnp.where(lane == (pair + offset) * 2 + h, a, 0.0), axis=-1, keepdims=True) for h in range(2)]
                    for a in (stats, delta_ref[at, :])
                )
                both = [(spot, h) for spot in spots for h in range(2)]

                def rows_of(value, spot):
                    return value[spot[0] + spot[1] : spot[0] + spot[1] + spot[2]]

                def keys_of(value, spot):
                    return value[spot[0] : spot[0] + span]

                scores = [
                    dot(rows_of(q_all, spot), keys_of(keys[h], spot), NT) + bias_block(toep, pair, h, spot[1], spot[2], span)
                    for spot, h in both
                ]
                dps = [dot(rows_of(do_all, spot), keys_of(vals[h], spot), NT) for spot, h in both]
                probs = [jnp.exp(s - rows_of(lses[h], spot)) for s, (spot, h) in zip(scores, both)]
                dss = [p * (dp - rows_of(sums[h], spot)) for p, dp, (spot, h) in zip(probs, dps, both)]
                for ds, (spot, h) in zip(dss, both):
                    for sub in range(spot[2] // SUB):
                        left = ROW - SUB - spot[1] - sub * SUB
                        diag[pair, h, :, left : left + span] += ds[sub * SUB : (sub + 1) * SUB]
                lows = [ds.astype(BF16) for ds in dss]
                plows = [p.astype(BF16) for p in probs]
                dqs = [dot(low, keys_of(keys[h], spot), NN) for low, (spot, h) in zip(lows, both)]
                dks = [dot(low, rows_of(queries[h], spot), TN) for low, (spot, h) in zip(lows, both)]
                dvs = [dot(low, rows_of(dos[h], spot), TN) for low, (spot, h) in zip(plows, both)]
                dq = jnp.concatenate([dqs[2 * i] + dqs[2 * i + 1] for i in range(len(spots))], axis=0)
                each = len(both) * span // ROW
                dk, dv = (
                    jnp.concatenate([sum(d[i + 1 : i + each], d[i]) for i in range(0, len(both), each)], axis=0)
                    for d in (dks, dvs)
                )
                for part, value in enumerate((dq, dk, dv)):
                    to = pl.ds(pl.multiple_of(pair * WIDE + part * pairs * WIDE, WIDE), WIDE)
                    out_ref[at, to] = value.astype(BF16)

            for span in (ROW, ROW // 2, ROW // 4):
                pl.when(length == span)(functools.partial(body, span))

        pltpu.make_async_copy(diag.at[pair], diag_out.at[pair], diag_sems.at[pair]).start()

    for pair in range(pairs):
        pltpu.make_async_copy(diag.at[pair], diag_out.at[pair], diag_sems.at[pair]).wait()


def columns_of(pair, widths):
    return [pl.ds(pl.multiple_of((pair + w) * WIDE, WIDE), WIDE) for w in widths]


def first_back_kernel(
    len_ref, count_ref, gain_ref, mixed_in, lse_in, part_in, got_in, middle_in, grad_in, toep_in, weight_in, packed_in,
    dgain_ref, out_ref, delta_ref, diag_out, dmiddle_out, dmixed_out, dweight_out,
    part_s, got_s, middle_s, grad_s, mixed_ref, lse_ref, dmixed, dweight, weight, packed, lows, toep, diag,
    in_sems, sems, out_sems, diag_sems,
):
    tokens = mixed_ref.shape[0]
    count = tokens // TILE
    width = FIRST * WIDE
    first = pltpu.make_async_copy(weight_in.at[pl.ds(3 * D, D)], weight, sems.at[0])
    first.start()
    ins = []
    for tile in range(count):
        at = pl.ds(tile * TILE, TILE)
        tiled = ((part_in, part_s), (got_in, got_s), (middle_in, middle_s), (grad_in, grad_s), (mixed_in, mixed_ref))
        for i, (src, dst) in enumerate(tiled):
            copy = pltpu.make_async_copy(src.at[at], dst.at[at], in_sems.at[5 * tile + i])
            copy.start()
            ins.append(copy)
    later = [
        pltpu.make_async_copy(toep_in.at[pl.ds(0, FIRST)], toep, sems.at[4]),
        pltpu.make_async_copy(lse_in, lse_ref, sems.at[5]),
    ]
    for copy in later:
        copy.start()
    for part in range(3):
        copy = pltpu.make_async_copy(
            packed_in.at[:, pl.ds(part * D, width)], packed.at[:, pl.ds(part * width, width)], sems.at[1 + part]
        )
        copy.start()
        later.append(copy)
    first.wait()
    outs = []
    of_feature = lax.broadcasted_iota(jnp.int32, (D, WIDE), 0) // HD
    heads = (of_feature == lax.broadcasted_iota(jnp.int32, (D, WIDE), 1)).astype(BF16)
    dgain = jnp.zeros((1, D), F32)
    for tile in range(count):
        at = pl.ds(tile * TILE, TILE)
        for copy in ins[5 * tile : 5 * tile + 5]:
            copy.wait()
        db = part_s[at, :] + got_s[at, :]
        middle = middle_s[at, :]
        scale = lax.rsqrt(jnp.mean(middle * middle, axis=-1, keepdims=True) + EPS)
        dn = db * gain_ref[1:2, :]
        inner = jnp.mean(dn * middle, axis=-1, keepdims=True)
        dmiddle = grad_s[at, :].astype(F32) + scale * dn - middle * (scale * scale * scale * inner)
        part_s[at, :] = dmiddle
        copy = pltpu.make_async_copy(part_s.at[at], dmiddle_out.at[at], out_sems.at[tile])
        copy.start()
        outs.append(copy)
        low = dmiddle.astype(BF16)
        lows[at, :] = low
        do = dot(low, weight[...], NN).astype(BF16)
        dmixed[at, :] = do
        dgain += jnp.sum(db * middle * scale, axis=0, keepdims=True)
        product = do.astype(F32) * mixed_ref[at, :].astype(F32)
        high = product.astype(BF16)
        delta = dot(high, heads, NN) + dot((product - high.astype(F32)).astype(BF16), heads, NN)
        delta_ref[at, :] = delta
    dgain_ref[...] = dgain
    copy = pltpu.make_async_copy(dmixed, dmixed_out, out_sems.at[count])
    copy.start()
    outs.append(copy)
    dweight[...] = dot(lows[...], mixed_ref[...], TN)
    copy = pltpu.make_async_copy(dweight, dweight_out, out_sems.at[count + 1])
    copy.start()
    outs.append(copy)
    for copy in later:
        copy.wait()

    def cols_of(pair):
        return columns_of(pair, (0, FIRST, 2 * FIRST, 0))

    attend_back(
        FIRST, 0, tokens // ROW, len_ref, count_ref, cols_of, packed, dmixed, lse_ref, delta_ref, toep, diag,
        out_ref, diag_out, diag_sems,
    )
    for copy in outs:
        copy.wait()


def first_back_call(lengths, counts, part, got, middle, out_grad, mixed, gains, lse, toep, weight, packed):
    tokens = part.shape[0]
    anywhere = pl.BlockSpec(memory_space=pl.ANY)
    inside = pl.BlockSpec(memory_space=pltpu.VMEM)
    width = 3 * FIRST * WIDE
    count = tokens // TILE
    return pl.pallas_call(
        first_back_kernel,
        grid_spec=pltpu.PrefetchScalarGridSpec(
            num_scalar_prefetch=2,
            grid=(),
            in_specs=[inside] + [anywhere] * 9,
            out_specs=[inside] * 3 + [anywhere] * 4,
            scratch_shapes=[pltpu.VMEM((tokens, D), F32)] * 3
            + [
                pltpu.VMEM((tokens, D), BF16),
                pltpu.VMEM((tokens, D), BF16),
                pltpu.VMEM((tokens, WIDE), F32),
                pltpu.VMEM((tokens, D), BF16),
                pltpu.VMEM((D, D), F32),
                pltpu.VMEM((D, D), BF16),
                pltpu.VMEM((tokens, width), BF16),
                pltpu.VMEM((tokens, D), BF16),
                pltpu.VMEM((FIRST, 2, SUB, TOEP), F32),
                pltpu.VMEM((FIRST, 2, SUB, TOEP), F32),
                pltpu.SemaphoreType.DMA((5 * count,)),
                pltpu.SemaphoreType.DMA((6,)),
                pltpu.SemaphoreType.DMA((count + 2,)),
                pltpu.SemaphoreType.DMA((FIRST,)),
            ],
        ),
        out_shape=[
            jax.ShapeDtypeStruct((1, D), F32),
            jax.ShapeDtypeStruct((tokens, width), BF16),
            jax.ShapeDtypeStruct((tokens, WIDE), F32),
            jax.ShapeDtypeStruct((FIRST, 2, SUB, TOEP), F32),
            jax.ShapeDtypeStruct((tokens, D), F32),
            jax.ShapeDtypeStruct((tokens, D), BF16),
            jax.ShapeDtypeStruct((D, D), F32),
        ],
        compiler_params=params(62),
        cost_estimate=cost(15e9, 30e6, 7e6),
        name="first_back",
    )(lengths, counts, gains, mixed, lse, part, got, middle, out_grad, toep, weight, packed)


def last_back_kernel(
    me_ref, len_ref, count_ref, lse_ref, delta_ref, gain_ref, toep_in, normed_in, first_in, dout_in, packed_in, dmixed_in, weight_in,
    out_ref, dgain_ref, diag_out, own_out, other_out,
    packed, dmixed, normed, first, weight, dout, total, toep, diag, sems, out_sems, diag_sems,
):
    tokens = normed.shape[0]
    pairs = PAIRS - FIRST
    width = pairs * WIDE
    start = FIRST * WIDE
    copies = [
        pltpu.make_async_copy(dmixed_in.at[:, pl.ds(start, width)], dmixed, sems.at[0]),
        pltpu.make_async_copy(toep_in.at[pl.ds(FIRST, pairs)], toep, sems.at[7]),
    ]
    for part in range(3):
        copies.append(
            pltpu.make_async_copy(
                packed_in.at[:, pl.ds(part * D + start, width)], packed.at[:, pl.ds(part * width, width)], sems.at[1 + part]
            )
        )
    later = [
        pltpu.make_async_copy(normed_in, normed, sems.at[4]),
        pltpu.make_async_copy(first_in, first, sems.at[5]),
        pltpu.make_async_copy(dout_in, dout, sems.at[6]),
        pltpu.make_async_copy(weight_in.at[pl.ds(0, 3 * D)], weight, sems.at[8]),
    ]
    for copy in copies + later:
        copy.start()
    for copy in copies:
        copy.wait()

    def cols_of(pair):
        return columns_of(pair, (0, pairs, 2 * pairs, 0))

    attend_back(
        pairs, FIRST, tokens // ROW, len_ref, count_ref, cols_of, packed, dmixed, lse_ref, delta_ref, toep, diag,
        out_ref, diag_out, diag_sems,
    )
    for copy in later:
        copy.wait()
    total[3 * D :] = dout[...].astype(BF16)
    for part in range(3):
        for at, rows, grads in ((part * D, start, first), (part * D + start, width, out_ref)):
            total[at : at + rows] = dot(grads[:, part * rows : (part + 1) * rows], normed[...], TN).astype(BF16)
    outs = []
    for core, out in ((1, other_out), (0, own_out)):
        for i in range(32):
            half, plane, z = i // 16, i // 4 % 4, i % 4
            owner = me_ref[0] ^ (z * 8 + plane * 2 + core)
            row = pl.multiple_of(owner * SHARD + half * HALF, 16)
            copy = pltpu.make_async_copy(total.at[pl.ds(row, HALF)], out.at[pl.ds(i * HALF, HALF)], out_sems.at[core])
            copy.start()
            outs.append(copy)
    dgain = jnp.zeros((8, D), F32)
    for at in range(0, 3 * D, D // 2):
        product = weight[at : at + D // 2].astype(F32) * total[at : at + D // 2].astype(F32)
        dgain += jnp.sum(product.reshape(D // 16, 8, D), axis=0)
    dgain_ref[...] = jnp.sum(dgain, axis=0, keepdims=True) / gain_ref[0:1, :]
    for copy in outs:
        copy.wait()


def last_back_call(me, lengths, counts, lse, delta, gains, toep, normed, first, grad_out, packed, dmixed, weight):
    tokens = normed.shape[0]
    anywhere = pl.BlockSpec(memory_space=pl.ANY)
    inside = pl.BlockSpec(memory_space=pltpu.VMEM)
    pairs = PAIRS - FIRST
    width = pairs * WIDE
    return pl.pallas_call(
        last_back_kernel,
        grid_spec=pltpu.PrefetchScalarGridSpec(
            num_scalar_prefetch=3,
            grid=(),
            in_specs=[inside] * 3 + [anywhere] * 7,
            out_specs=[inside] * 2 + [anywhere] * 3,
            scratch_shapes=[
                pltpu.VMEM((tokens, 3 * width), BF16),
                pltpu.VMEM((tokens, width), BF16),
                pltpu.VMEM((tokens, D), BF16),
                pltpu.VMEM((tokens, 3 * FIRST * WIDE), BF16),
                pltpu.VMEM((3 * D, D), BF16),
                pltpu.VMEM((D, D), F32),
                pltpu.VMEM((4 * D, D), BF16),
                pltpu.VMEM((pairs, 2, SUB, TOEP), F32),
                pltpu.VMEM((pairs, 2, SUB, TOEP), F32),
                pltpu.SemaphoreType.DMA((9,)),
                pltpu.SemaphoreType.DMA((2,)),
                pltpu.SemaphoreType.DMA((pairs,)),
            ],
        ),
        out_shape=[
            jax.ShapeDtypeStruct((tokens, 3 * width), BF16),
            jax.ShapeDtypeStruct((1, D), F32),
            jax.ShapeDtypeStruct((pairs, 2, SUB, TOEP), F32),
            jax.ShapeDtypeStruct((2 * D, D), BF16),
            jax.ShapeDtypeStruct((2 * D, D), BF16),
        ],
        compiler_params=params(62),
        cost_estimate=cost(10e9, 30e6, 4e6),
        name="last_back",
    )(me, lengths, counts, lse, delta, gains, toep, normed, first, grad_out, packed, dmixed, weight)


def feed_tile(second, grad, up, down):
    u = dot(second, up, NT)
    square = u * u
    t = jnp.tanh(0.7978845608 * u * (1.0 + 0.044715 * square))
    plus = 0.5 * (1.0 + t)
    slope = plus + (0.5 * 0.7978845608) * u * (1.0 - t * t) * (1.0 + 3 * 0.044715 * square)
    dh = dot(grad, down, NT).astype(BF16).astype(F32)
    return (u * plus).astype(BF16), (dh * slope).astype(BF16)


def planes_of(near, far, half):
    rows = 4 * HALF
    near, far = ([value[i : i + rows] for i in (0, rows)] for value in (near, far))
    order = (near[0], far[0], near[1], far[1]) if half == 0 else (near[0], near[1], far[0], far[1])
    return jnp.concatenate(order, axis=0)


def weights_of(refs):
    return [planes_of(refs[2 * half][...], refs[2 * half + 1][...], half) for half in range(2)]


def feed_kernel(parts, *refs):
    up, down = weights_of(refs[:4])
    second_ref, grad_ref, *refs, back_ref, hidden_ref, dpre_ref = refs[4:]
    hidden, du = feed_tile(second_ref[...], grad_ref[...], up, down)
    hidden_ref[...] = hidden
    dpre_ref[...] = du
    back = dot(du, up, NN)
    back_ref[...] = back + refs[0][...] if parts else back


def feed_call(weights, second, out_grad, start=None):
    tokens = second.shape[0]
    flat = tiles(TILE, D)
    low_flat = jax.ShapeDtypeStruct((tokens, D), BF16)
    more = [] if start is None else [start]
    return pl.pallas_call(
        functools.partial(feed_kernel, len(more)),
        grid=(tokens // TILE,),
        in_specs=[piece_block()] * 4 + [flat, flat] + [flat] * len(more),
        out_specs=[flat, flat, flat],
        out_shape=[jax.ShapeDtypeStruct((tokens, D), F32), low_flat, low_flat],
        compiler_params=params(20),
        cost_estimate=cost(6 * tokens * D * D, 15e6, tokens * D),
        name="feed",
    )(*weights, second, out_grad, *more)


def feed_sum_kernel(parts, *refs):
    weights = refs[:4]
    ins = refs[4:10]
    refs = refs[10:]
    start_ref = refs[0] if parts else None
    back_ref, hidden_ref, out_ref, up_send, down_send = refs[parts : parts + 5]
    second, grad, second_other, grad_other, hidden_other, dpre_other, hidden, dpre, tile_sems, sems = refs[parts + 5 :]
    step = pl.program_id(0)
    count = second.shape[0] // TILE

    def tile_copies(tile):
        at = pl.ds(pl.multiple_of(tile * TILE, TILE), TILE)
        return [
            pltpu.make_async_copy(src.at[at], dst.at[at], tile_sems.at[2 * tile + i])
            for i, (src, dst) in enumerate(((ins[0], second), (ins[1], grad)))
        ]

    others = [
        pltpu.make_async_copy(src, dst, sems.at[i])
        for i, (src, dst) in enumerate(zip(ins[2:], (second_other, grad_other, hidden_other, dpre_other)))
    ]

    @pl.when(step == 0)
    def _():
        for tile in range(count):
            for copy in tile_copies(tile):
                copy.start()
        for copy in others:
            copy.start()

    @pl.when(step < count)
    def _():
        at = pl.ds(pl.multiple_of(step * TILE, TILE), TILE)
        for copy in tile_copies(step):
            copy.wait()
        up, down = weights_of(weights)
        low_hidden, du = feed_tile(second[at, :], grad[at, :], up, down)
        hidden_ref[...] = low_hidden
        hidden[at, :] = low_hidden
        dpre[at, :] = du
        back = dot(du, up, NN)
        back_ref[...] = back if start_ref is None else back + start_ref[...]

    @pl.when(step == count)
    def _():
        for copy in others:
            copy.wait()
        total = dot(dpre[...], second[...], TN) + dot(dpre_other[...], second_other[...], TN)
        rows = 4 * HALF
        for x in range(2):
            out_ref[0, x * rows : (x + 1) * rows] = total[2 * x * rows : (2 * x + 1) * rows]
            up_send[x * rows : (x + 1) * rows] = total[(2 * x + 1) * rows : (2 * x + 2) * rows].astype(BF16)

    @pl.when(step == count + 1)
    def _():
        total = dot(hidden[...], grad[...], TN) + dot(hidden_other[...], grad_other[...], TN)
        out_ref[0] = total[: 8 * HALF]
        down_send[...] = total[8 * HALF :].astype(BF16)


def feed_sum_call(weights, second, out_grad, second_other, grad_other, hidden_other, dpre_other, start=None):
    tokens = second.shape[0]
    count = tokens // TILE
    anywhere = pl.BlockSpec(memory_space=pl.ANY)
    tile = pl.BlockSpec((TILE, D), lambda i: (jnp.minimum(i, count - 1), 0))
    more = [] if start is None else [start]
    return pl.pallas_call(
        functools.partial(feed_sum_kernel, len(more)),
        grid=(count + 2,),
        in_specs=[piece_block()] * 4 + [anywhere] * 6 + [tile] * len(more),
        out_specs=[
            tile,
            tile,
            pl.BlockSpec((1, 8 * HALF, D), lambda i: (jnp.maximum(i - count, 0), 0, 0)),
            whole((8 * HALF, D)),
            whole((8 * HALF, D)),
        ],
        out_shape=[
            jax.ShapeDtypeStruct((tokens, D), F32),
            jax.ShapeDtypeStruct((tokens, D), BF16),
            jax.ShapeDtypeStruct((2, 8 * HALF, D), F32),
            jax.ShapeDtypeStruct((8 * HALF, D), BF16),
            jax.ShapeDtypeStruct((8 * HALF, D), BF16),
        ],
        scratch_shapes=[pltpu.VMEM((tokens, D), BF16)] * 8
        + [pltpu.SemaphoreType.DMA((2 * count,)), pltpu.SemaphoreType.DMA((4,))],
        compiler_params=params(56 if more else 36),
        cost_estimate=cost(14 * tokens * D * D, 30e6, tokens * D),
        name="feed_sum",
    )(*weights, second, out_grad, second_other, grad_other, hidden_other, dpre_other, *more)


def output_kernel(*refs):
    total = None
    for i in range(2):
        part = dot(refs[i][...], planes_of(refs[2 + 2 * i][...], refs[3 + 2 * i][...], 1), NN)
        total = part if total is None else total + part
    for ref in refs[6:-1]:
        total += ref[...]
    refs[-1][...] = total.astype(refs[-1].dtype)


def output_call(hiddens, downs, more=(), kind=F32):
    tokens = hiddens[0].shape[0]
    return pl.pallas_call(
        output_kernel,
        grid=(tokens // TILE,),
        in_specs=[tiles(TILE, D)] * 2 + [piece_block()] * 4 + [tiles(TILE, D)] * len(more),
        out_specs=tiles(TILE, D),
        out_shape=jax.ShapeDtypeStruct((tokens, D), kind),
        compiler_params=params(62),
        cost_estimate=cost(4 * tokens * D * D, 12e6),
        name="output",
    )(*hiddens, *downs, *more)


def input_back_kernel(first_ref, last_ref, x_ref, dmiddle_ref, gain_ref, weight_ref, dx_ref):
    da = jnp.zeros(dx_ref.shape, F32)
    cut = FIRST * WIDE
    for part in range(3):
        da += dot(first_ref[:, part * cut : (part + 1) * cut], weight_ref[part * D : part * D + cut, :], NN)
        rest = D - cut
        da += dot(last_ref[:, part * rest : (part + 1) * rest], weight_ref[part * D + cut : (part + 1) * D, :], NN)
    x = x_ref[...].astype(F32)
    scale = lax.rsqrt(jnp.mean(x * x, axis=-1, keepdims=True) + EPS)
    dm = da * gain_ref[0:1, :]
    inner = jnp.mean(dm * x, axis=-1, keepdims=True)
    dx_ref[...] = dmiddle_ref[...] + scale * dm - x * (scale * scale * scale * inner)


def input_back_call(first, last, x, dmiddle, gains, weight):
    tokens = x.shape[0]
    return pl.pallas_call(
        input_back_kernel,
        grid=(tokens // TILE,),
        in_specs=[
            tiles(TILE, first.shape[1]),
            tiles(TILE, last.shape[1]),
            tiles(TILE, D),
            tiles(TILE, D),
            whole((2, D)),
            whole((3 * D, D)),
        ],
        out_specs=tiles(TILE, D),
        out_shape=jax.ShapeDtypeStruct((tokens, D), F32),
        compiler_params=params(62),
        cost_estimate=cost(2 * tokens * D * 3 * D, 18e6),
        name="input_back",
    )(first, last, x, dmiddle, gains, weight)


def adam_update(param, grad, first, second, rate):
    first_new = BETA_ONE * first + (1.0 - BETA_ONE) * grad
    second_new = BETA_TWO * second + (1.0 - BETA_TWO) * grad * grad
    first_hat = first_new / (1.0 - BETA_ONE**STEP)
    second_hat = second_new / (1.0 - BETA_TWO**STEP)
    param_new = param - rate * (first_hat / (jnp.sqrt(second_hat) + ADAM_EPS) + DECAY * param)
    return (param_new, first_new, second_new)


AXES = ("tree", "rest")
CORE, Y, X, Z = 1, 2, 4, 8


def swap(value, bits):
    return lax.ppermute(value, "tree", [(i, i ^ bits) for i in range(32)])


def tie(values, after):
    return list(lax.optimization_barrier(tuple(values) + tuple(after))[: len(values)])


def gather_z(shard):
    return [shard] + [swap(shard, k * Z) for k in (1, 2, 3)]


def gather_halves(line, first=0):
    return [jnp.concatenate([p[i : i + HALF] for p in line]) for i in (first, first + HALF)]


def gather_plane(halves):
    return [swap(halves[0], X), swap(halves[1], Y)]


def gather_near(halves, turned):
    return [jnp.concatenate([half, got]) for half, got in zip(halves, turned)]


def gather_far(near):
    return [swap(near[0], Y), swap(near[1], X)]


def gathered(near, far):
    return [near[0], far[0], near[1], far[1]]


def gather_core(pieces):
    return [swap(p, CORE) for p in pieces]


def low(value):
    return value.astype(BF16)


def swap_plane(sends):
    return [swap(sends[0], Y), swap(sends[1], X)]


def swap_rest(sends):
    return [swap(sends[0], X), swap(sends[1], Y)]


def feed_rest_kernel(*refs):
    grads, gots, outs = refs[:4], refs[4:8], refs[8:]
    for step in range(2):

        @pl.when(pl.program_id(0) == step)
        def _(step=step):
            for chunk in range(2):
                for half in range(2):
                    i = 2 * chunk + half
                    out = outs[2 * step + half]
                    out[chunk] = (grads[i][0] + gots[i][...].astype(F32)).astype(out.dtype)


def feed_rest_call(grads, gots):
    rows = 4 * HALF
    shape = (2, rows, D)
    outs = pl.pallas_call(
        feed_rest_kernel,
        grid=(2,),
        in_specs=[pl.BlockSpec((1, rows, D), lambda i, h=h: (h, 1 - i, 0)) for _ in range(2) for h in range(2)]
        + [pl.BlockSpec((rows, D), lambda i: (1 - i, 0))] * 4,
        out_specs=[whole(shape)] * 4,
        out_shape=[jax.ShapeDtypeStruct(shape, kind) for kind in (BF16, BF16, F32, F32)],
        compiler_params=params(62),
        cost_estimate=cost(1e6, 10e6),
        name="feed_rest",
    )(*[grads[0]] * 2, *[grads[1]] * 2, *gots)
    return outs[2:], outs[:2]


def plane_kernel(*refs):
    for half, out in enumerate(refs[8:]):
        for i in range(2):
            value = refs[4 * half + i][...].astype(F32) + refs[4 * half + 2 + i][...].astype(F32)
            out[i * 4 * HALF : (i + 1) * 4 * HALF] = value.astype(BF16)


def plane_call(own, got):
    rows = 4 * HALF

    def blocks(*places):
        return [pl.BlockSpec((rows, D), lambda i, p=p: (p, 0)) for p in places]

    return pl.pallas_call(
        plane_kernel,
        grid=(1,),
        in_specs=blocks(1, 3, 1, 3, 6, 7, 6, 7),
        out_specs=[whole((2 * rows, D))] * 2,
        out_shape=[jax.ShapeDtypeStruct((2 * rows, D), BF16)] * 2,
        compiler_params=params(62),
        cost_estimate=cost(1e6, 5e6),
        name="plane",
    )(own, own, got, got, own, own, got, got)


def rest_kernel(*refs):
    owns, cores, gots, outs = refs[:4], refs[4:8], refs[8:10], refs[10:]
    rows = 4 * HALF
    for half in range(2):
        for far in range(2):
            i = 2 * half + far
            value = owns[i][...].astype(F32) + cores[i][...].astype(F32)
            value += gots[half][far * rows : (far + 1) * rows].astype(F32)
            out = outs[2 * far + half]
            out[...] = value.astype(out.dtype)


def rest_call(own, core, gots):
    rows = 4 * HALF
    blocks = [pl.BlockSpec((rows, D), lambda i, p=p: (p, 0)) for p in (0, 2, 4, 5)]
    outs = pl.pallas_call(
        rest_kernel,
        grid=(1,),
        in_specs=blocks * 2 + [whole((2 * rows, D))] * 2,
        out_specs=[whole((rows, D))] * 4,
        out_shape=[jax.ShapeDtypeStruct((rows, D), kind) for kind in (F32, F32, BF16, BF16)],
        compiler_params=params(62),
        cost_estimate=cost(1e6, 7e6),
        name="rest",
    )(*[own] * 4, *[core] * 4, *gots)
    return outs[:2], outs[2:]


def line_kernel(one_ref, two_ref, got_one, got_two, *outs):
    for k, out in enumerate(outs):
        at = slice(k * HALF, (k + 1) * HALF)
        for chunk in range(one_ref.shape[0]):
            for half, (ref, got) in enumerate(((one_ref, got_one), (two_ref, got_two))):
                out[chunk, half] = (ref[chunk, at] + got[chunk, at].astype(F32)).astype(out.dtype)


def reduce_line(keep, got):
    chunks = keep[0].size // (4 * HALF * D)
    keep, got = ([a.reshape(chunks, 4 * HALF, D) for a in values] for values in (keep, got))
    shape = (chunks, 2, HALF, D)
    outs = pl.pallas_call(
        line_kernel,
        out_shape=[jax.ShapeDtypeStruct(shape, F32)] + [jax.ShapeDtypeStruct(shape, BF16)] * 3,
        compiler_params=params(62),
        cost_estimate=cost(1e6, 6e6),
        name="line",
    )(*keep, *got)
    return outs[0], list(outs[1:])


def feed_line_kernel(one_ref, two_ref, got_one, got_two, keep, send):
    for chunk in range(one_ref.shape[0]):
        for half, (ref, got) in enumerate(((one_ref, got_one), (two_ref, got_two))):
            value = ref[chunk] + got[chunk].astype(F32)
            keep[chunk, half] = value[: 2 * HALF]
            send[chunk, half] = value[2 * HALF :].astype(BF16)


def feed_line_call(keep, got):
    shape = (2, 2, 2 * HALF, D)
    return pl.pallas_call(
        feed_line_kernel,
        out_shape=[jax.ShapeDtypeStruct(shape, F32), jax.ShapeDtypeStruct(shape, BF16)],
        compiler_params=params(62),
        cost_estimate=cost(1e6, 6e6),
        name="feed_line",
    )(*keep, *(g.reshape(2, 4 * HALF, D) for g in got))


def swap_line(sends):
    return [swap(send, k * Z) for k, send in zip((1, 2, 3), sends)]


def reduced(keep, got):
    return keep + got[0].astype(F32) + got[1].astype(F32) + got[2].astype(F32)


def on_device(
    layer_input, out_grad, matrices, mat_first, mat_second, mat_ema, gains, gain_first, gain_second,
    rel_bias, bias_first, bias_second, bucket_len, item_count, bucket_table,
):
    rest = lax.axis_size("rest")
    shards = jnp.swapaxes(matrices, 1, 2).astype(BF16)
    if rest > 1:
        shards = lax.all_gather(shards, "rest", axis=1, tiled=True)
    shard_a, shard_b = (jnp.concatenate([shards[1, i : i + HALF], shards[2, i : i + HALF]]) for i in (0, HALF))
    where = lax.axis_index("tree").astype(jnp.int32)
    me = where.reshape(1)
    flipped = jnp.concatenate([bucket_table[::-1], jnp.full((1,), -1, jnp.int32)])
    onehot = (flipped[None, :] == jnp.arange(BUCKETS, dtype=jnp.int32)[:, None]).astype(F32)
    table = jnp.dot(rel_bias.T, onehot, precision=lax.Precision.HIGHEST).reshape(PAIRS, 2, SPAN)

    toep = toeplitz_call(table)

    grad_other = swap(out_grad, CORE)
    line_w = gather_z(shards[0])
    line_w = line_w[:1] + tie(line_w[1:], [toep, grad_other])
    halves_w = gather_halves(line_w)
    turned_w = gather_plane(halves_w)
    (shard_a,) = tie([shard_a], turned_w[:1])
    line_a = gather_z(shard_a)
    near_w = gather_near(halves_w, turned_w)
    far_w = gather_far(near_w)
    near_c = gather_core(tie(near_w, line_a[1:]))
    far_c = gather_core(far_w)
    halves_a = tie(gather_halves(line_a), near_c + far_w)
    turned_a = gather_plane(halves_a)
    (shard_b,) = tie([shard_b], near_c + far_w)
    line_b = gather_z(shard_b)
    own_w, other_w = gathered(near_w, far_w), gathered(near_c, far_c)
    (late_input,) = tie([layer_input], halves_a)
    normed, packed, attn_weight, stats, mixed_first = first_forward_call(
        me, bucket_len, item_count, own_w + other_w, toep, late_input, gains
    )
    turned_a, line_b = tie(turned_a, [normed]), line_b[:1] + tie(line_b[1:], [normed])
    near_a = gather_near(halves_a, turned_a)
    far_a = gather_far(near_a)
    halves_b = gather_halves(line_b)
    (mixed_first,) = tie([mixed_first], near_a + halves_b)
    turned_b = gather_plane(halves_b)
    lse, mixed, middle, second = last_forward_call(
        bucket_len, item_count, layer_input, gains, mixed_first, stats, toep, attn_weight, packed
    )

    own_a = gathered(near_a, tie(far_a, [lse]))
    (second,) = tie([second], far_a)
    second_other = swap(second, CORE)
    back_other, hidden_oa, dpre_oa = feed_call(own_a, second_other, grad_other)
    turned_b = tie(turned_b, [dpre_oa])
    near_b = gather_near(halves_b, turned_b)
    far_b = gather_far(near_b)
    (second_a,) = tie([second], [dpre_oa] + near_b)
    back, hidden_a, grad_a, *send_a = feed_sum_call(
        own_a, second_a, out_grad, second_other, grad_other, hidden_oa, dpre_oa
    )
    far_b = tie(far_b, [back])
    own_b = gathered(near_b, far_b)
    (second_other_b,) = tie([second_other], list(send_a) + far_b)
    got_a = swap_plane(send_a)
    back_other, hidden_ob, dpre_ob = feed_call(own_b, second_other_b, grad_other, back_other)
    back_got = swap(back_other, CORE)
    (second_b,) = tie([second], [dpre_ob])
    back, hidden_b, grad_b, *send_b = feed_sum_call(
        own_b, second_b, out_grad, second_other_b, grad_other, hidden_ob, dpre_ob, back
    )

    got_b = swap_plane(send_b)
    (back,) = tie([back], send_b + got_a + [back_got])
    dgain_two, first_d, delta, diag_a, dmiddle, dmixed, grad_out = first_back_call(
        bucket_len, item_count, back, back_got, middle, out_grad, mixed, gains, lse, toep, attn_weight, packed
    )
    got_b = tie(got_b, [dmixed])
    keep_f, send_f = feed_rest_call([grad_a, grad_b], got_a + got_b)
    (dmixed,) = tie([dmixed], send_f)
    got_f = swap_rest(send_f)
    last_d, dgain_one, diag_b, mine_w, other_w = last_back_call(
        me, bucket_len, item_count, lse, delta, gains, toep, normed, first_d, grad_out, packed, dmixed, attn_weight
    )

    got_f = tie(got_f, [last_d])
    (other_w,) = tie([other_w], got_f)
    core_w = swap(other_w, CORE)
    keep_f, send_f = feed_line_call(keep_f, got_f)
    (core_w,) = tie([core_w], [send_f])
    send_w = plane_call(mine_w, core_w)
    got_w = swap_plane(send_w)
    (send_f,) = tie([send_f], send_w)
    got_f = swap(send_f, 2 * Z)
    (diag_a,) = tie([diag_a], [send_f])
    lines = fold_call(diag_a, diag_b)
    bias_local = jnp.dot(onehot, lines.reshape(HEADS, SPAN).T, precision=lax.Precision.HIGHEST)
    small = jnp.concatenate([dgain_one.reshape(-1), dgain_two.reshape(-1), bias_local.reshape(-1)]).reshape(-1, 128)
    small_got = swap(small, CORE)
    downs = own_a[2:] + own_b[2:]
    (hidden_late,) = tie([hidden_oa], [small])
    output_other = output_call([hidden_late, hidden_ob], downs)
    (small_got, *got_w) = tie([small_got] + got_w, [output_other])
    small = small + small_got
    small_got = swap(small, Z)
    (got_w[0],) = tie(got_w[:1], [small])
    keep_w, send_w = rest_call(mine_w, core_w, got_w)
    got_w = swap_rest(send_w)
    (last_e,) = tie([last_d], send_w)
    input_grad = input_back_call(first_d, last_e, layer_input, dmiddle, gains, attn_weight)
    (small_got, got_f, *got_w) = tie([small_got, got_f] + got_w, [input_grad])
    small = small + small_got
    small_got = swap(small, 2 * Z)
    (got_w[0],) = tie(got_w[:1], [small])
    keep_w, send_w = reduce_line(keep_w, got_w)
    got_w = swap_line(send_w)
    (got_f,) = tie([got_f], send_w)
    send_f = low(keep_f[:, :, HALF:] + got_f[:, :, HALF:].astype(F32))
    got_line = swap(send_f, Z)
    (small_got, output_other) = tie([small_got, output_other], [send_f])
    output_got = swap(output_other, CORE)
    small = small + small_got
    small_got = swap(small, X)
    (hidden_last,) = tie([hidden_a], [small])
    layer_output = output_call([hidden_last, hidden_b], downs, (middle, output_got), BF16)
    (small_got,) = tie([small_got], [layer_output])
    small = small + small_got
    small_got = swap(small, Y)
    (got_line, *got_w) = tie([got_line] + got_w, [layer_output, small])
    small = (small + small_got).reshape(-1)
    sum_f = keep_f[:, :, :HALF] + got_f[:, :, :HALF].astype(F32) + got_line.astype(F32)
    sum_w = reduced(keep_w, got_w)
    sum_f = sum_f.swapaxes(0, 1)

    summed = jnp.concatenate([sum_w.reshape(1, SHARD, D), sum_f.reshape(2, SHARD, D)])
    if rest > 1:
        small = lax.psum(small, "rest")
        summed = lax.psum_scatter(summed, "rest", scatter_dimension=1, tiled=True)
    gain_grad = small[: 2 * D].reshape(2, D)
    bias_grad = small[2 * D :].reshape(BUCKETS, HEADS)
    mat_grad = jnp.swapaxes(summed, 1, 2)
    mat_new, mat_first_new, mat_second_new = adam_update(
        matrices, mat_grad, mat_first, mat_second, RATE
    )
    mat_ema_new = EMA_KEEP * mat_ema + (1.0 - EMA_KEEP) * mat_new
    gain_new, gain_first_new, gain_second_new = adam_update(
        gains, gain_grad, gain_first, gain_second, RATE_SMALL
    )
    bias_new, bias_first_new, bias_second_new = adam_update(
        rel_bias, bias_grad, bias_first, bias_second, RATE_SMALL
    )
    return (
        layer_output, input_grad, mat_grad, mat_new, mat_first_new, mat_second_new, mat_ema_new,
        gain_grad, gain_new, gain_first_new, gain_second_new,
        bias_grad, bias_new, bias_first_new, bias_second_new,
    )


def solution(mesh):
    fine = Mesh(mesh.devices.reshape(32, -1), AXES)
    rows = P(AXES, None)
    columns = P(None, None, AXES)
    return jax.shard_map(
        on_device,
        mesh=fine,
        in_specs=(rows, rows) + (columns,) * 4 + (P(),) * 6 + (P(AXES), P(AXES), P()),
        out_specs=(rows, rows) + (columns,) * 5 + (P(),) * 8,
        check_vma=False,
    )
```
